32 devices in a mesh: pipe: 4 (over x, core), dp: 8 (over z, y).
Axes of the slice: x: 2, y: 2, z: 4, core: 2. Of those that a mesh axis runs over, the one named last changes fastest.
Arguments:
- x_ckpt: bfloat16 [4, 2, 8, 512, 512], P('pipe', None, 'dp'), may hold values from -6 to 6
- top_cot: bfloat16 [2, 8, 512, 512], P(None, 'dp'), may hold values from -6 to 6
- skip_cot: bfloat16 [2, 8, 512, 512], P(None, 'dp'), may hold values from -6 to 6
- w_conv: bfloat16 [4, 512, 3, 1024], P('pipe', 'dp'), may hold values from -0.15625 to 0.15625
- w_mix: bfloat16 [4, 512, 1024], P('pipe', 'dp'), may hold values from -0.25 to 0.25
Outputs:
- cot_inputs: bfloat16 [4, 2, 8, 512, 512], P('pipe', None, 'dp')
- grad_conv: float32 [4, 512, 3, 1024], P('pipe', 'dp')
- grad_mix: float32 [4, 512, 1024], P('pipe', 'dp')
The draws below stay inside these ranges and needn't reach their ends.
All inputs are finite; a program needn't handle non-finite values.
Results may differ from the reference program's by a relative error of at most 0.014.
Values may be sent and summed in bfloat16 or wider, within the bound.
No kernel may reach another device: no remote copies, remote signals or barrier semaphores. Data moves between devices by JAX's collectives and lax.ppermute only.
A program may use at most 128 MiB of HBM per device.

```python
import jax
import jax.numpy as jnp
from jax import lax

C = 512
MB = 2
LEN = 512
BATCH = 8
N_PIPE = 4


def with_spikes(drawn, key, source, target, shards_of, factor):
    owner, partner = [(jnp.arange(drawn.shape[dim]) // (drawn.shape[dim] // shards_of)).reshape([-1 if axis == dim else 1 for axis in range(drawn.ndim)]) for dim in (source, target)]
    chosen = jax.random.permutation(key, shards_of)[partner]
    strong = (owner == chosen) | (owner == (partner + shards_of // 2) % shards_of)
    return jnp.where(strong, factor * drawn, drawn)


def levels(stream_key, dims, pieces, least, top_value):
    loudness, own = 1.0, jax.random.fold_in(stream_key, 6)
    for axis_at, parts in pieces:
        steps = jnp.exp(jax.random.uniform(jax.random.fold_in(own, axis_at), (parts,), jnp.float32, least / len(pieces), top_value / len(pieces)))
        loudness = loudness * jnp.repeat(steps, dims[axis_at] // parts).reshape([-1 if axis == axis_at else 1 for axis in range(len(dims))])
    return loudness


def scatter_about(stream_key, extent, deviation, bound, cuts=(), kind=jnp.bfloat16):
    drawn = jax.random.normal(stream_key, extent, jnp.float32) * deviation
    if len(cuts) > 0:
        drawn = levels(stream_key, extent, cuts, -0.22, 0.18) * drawn
    return jnp.clip(drawn, min=-bound, max=bound).astype(kind)


def noise_with(key, extent, deviation, most, split, heavy, kind=jnp.bfloat16):
    array = deviation * jax.random.normal(key, extent, jnp.float32)
    if split:
        array = array * levels(key, extent, split, -0.22, 0.18)
    return jnp.clip(with_spikes(array, jax.random.fold_in(key, 3), *heavy), -most, most).astype(kind)


def setup_inputs(seed: int = 0) -> dict:
    key_of = jax.random.split(jax.random.key(seed), 6)
    x_ckpt = noise_with(key_of[0], (N_PIPE, MB, BATCH, LEN, C), 1.0, 6.0, ((0, 4), (2, 8)), (2, 4, 8, 2.0))
    top_cot = scatter_about(key_of[1], (MB, BATCH, LEN, C), 1.0, 6.0, ((1, 8),))
    skip_cot = scatter_about(key_of[2], (MB, BATCH, LEN, C), 1.0, 6.0, ((1, 8),))
    w_conv = scatter_about(key_of[3], (N_PIPE, C, 3, 2 * C), (3 * C) ** -0.5, 0.15625, ((0, 4), (1, 8)))
    w_mix = scatter_about(key_of[4], (N_PIPE, C, 2 * C), C ** -0.5, 0.25, ((0, 4), (1, 8)))
    return dict(x_ckpt=x_ckpt, top_cot=top_cot, skip_cot=skip_cot, w_conv=w_conv, w_mix=w_mix)


def delay_seq(signal, shift_by):
    samples = signal.shape[1]
    rolled = jnp.roll(signal, shift_by, axis=1)
    positions = lax.broadcasted_iota(jnp.int32, (1, samples, 1), 1)
    return jnp.where(positions >= shift_by, rolled, jnp.zeros_like(rolled))


def advance_seq(signal, shift_by):
    samples = signal.shape[1]
    rolled = jnp.roll(signal, -shift_by, axis=1)
    positions = lax.broadcasted_iota(jnp.int32, (1, samples, 1), 1)
    return jnp.where(positions < samples - shift_by, rolled, jnp.zeros_like(rolled))


def layer_back(x_rows, grad_next, skip_grad, conv_w, mix_w, dilation):
    channels = x_rows.shape[2]
    tapped_x = jnp.stack([delay_seq(x_rows, offset * dilation) for offset in range(3)], axis=2)
    pre_act = jnp.einsum("slkc,ckn->sln", tapped_x.astype(jnp.float32), conv_w.astype(jnp.float32))
    filter_act = jnp.tanh(pre_act[..., :channels])
    gate_act = jax.nn.sigmoid(pre_act[..., channels:])
    hidden = (filter_act * gate_act).astype(jnp.bfloat16)
    cot_pair = jnp.concatenate([grad_next, skip_grad], axis=2)
    hid_grad = jnp.einsum("sln,cn->slc", cot_pair.astype(jnp.float32), mix_w.astype(jnp.float32))
    pre_grad = jnp.concatenate([hid_grad * gate_act * (1.0 - filter_act * filter_act),
                                hid_grad * filter_act * gate_act * (1.0 - gate_act)], axis=2).astype(jnp.bfloat16)
    back_taps = jnp.einsum("sln,ckn->slkc", pre_grad.astype(jnp.float32), conv_w.astype(jnp.float32))
    input_grad = grad_next.astype(jnp.float32)
    for offset in range(3):
        input_grad = input_grad + advance_seq(back_taps[:, :, offset], offset * dilation)
    return input_grad.astype(jnp.bfloat16), tapped_x, hidden, pre_grad, cot_pair


def reference(x_ckpt, top_cot, skip_cot, w_conv, w_mix):
    rows_all = MB * BATCH
    skip_rows = skip_cot.reshape(rows_all, LEN, C)
    cot_next = top_cot.reshape(rows_all, LEN, C)
    cot_list = [None] * N_PIPE
    conv_list = [None] * N_PIPE
    mix_list = [None] * N_PIPE
    for sec_index in reversed(range(N_PIPE)):
        x_rows = x_ckpt[sec_index].reshape(rows_all, LEN, C)
        input_grad, tapped_x, hidden, pre_grad, cot_pair = layer_back(
            x_rows, cot_next, skip_rows, w_conv[sec_index], w_mix[sec_index], 2 ** sec_index)
        conv_list[sec_index] = jnp.einsum("slkc,sln->ckn", tapped_x.astype(jnp.float32), pre_grad.astype(jnp.float32))
        mix_list[sec_index] = jnp.einsum("slc,sln->cn", hidden.astype(jnp.float32), cot_pair.astype(jnp.float32))
        cot_list[sec_index] = input_grad.reshape(MB, BATCH, LEN, C)
        cot_next = input_grad
    return jnp.stack(cot_list), jnp.stack(conv_list), jnp.stack(mix_list)
```

```python
import functools

import jax
import jax.numpy as jnp
from jax import lax
from jax.experimental import pallas as pl
from jax.experimental.pallas import tpu as pltpu
from jax.sharding import PartitionSpec as P

F32 = jnp.float32
BF16 = jnp.bfloat16
NT = (((1,), (1,)), ((), ()))


def ring_order(count):
    return list(range(0, count, 2)) + list(range(count - 1 - count % 2, 0, -2))


def ring_pairs(order):
    count = len(order)
    right = [(order[i], order[(i + 1) % count]) for i in range(count)]
    left = [(order[(i + 1) % count], order[i]) for i in range(count)]
    return right, left


def chain_kernel(
    dilation, flags, g_hbm, hs_hbm, a1_hbm, a2_hbm, w_hbm, _pg, _ig, _gk, pg_hbm, ig_hbm, gk_hbm,
    g, hs, a1, a2, wm, wc, pg, ig, bt, sems,
):
    samples, channels = g.shape
    padding = bt.shape[1] - samples

    @pl.when(flags[0] == 1)
    def _():
        def load(source, target, number):
            copy = pltpu.make_async_copy(source, target, sems.at[number])
            copy.start()
            return copy

        get_g = load(g_hbm, g, 0)
        get_wm = load(w_hbm.at[3, :, pl.ds(0, channels)], wm, 1)
        get_hs = load(hs_hbm, hs, 2)
        get_a1 = load(a1_hbm, a1, 3)
        get_a2 = load(a2_hbm, a2, 4)
        get_wc = [load(w_hbm.at[k], wc.at[k], 5 + k) for k in range(3)]
        get_g.wait()
        keep_g = load(g, gk_hbm, 8)
        get_wm.wait()
        hid = lax.dot_general(g[...], wm[...], NT, preferred_element_type=F32)
        get_hs.wait()
        hid = hid + hs[...]
        get_a1.wait()
        pg[:, :channels] = (hid * a1[...]).astype(BF16)
        get_a2.wait()
        pg[:, channels:] = (hid * a2[...]).astype(BF16)
        put_pg = load(pg, pg_hbm, 9)
        for k in range(3):
            get_wc[k].wait()
            bt[k, :samples, :] = lax.dot_general(pg[...], wc[k], NT, preferred_element_type=F32)
            if k:
                bt[k, samples:, :] = jnp.zeros((padding, channels), F32)
        rows = 64
        for start in range(0, samples, rows):
            total = g[start : start + rows, :].astype(F32) + bt[0, start : start + rows, :]
            total = total + bt[1, start + dilation : start + dilation + rows, :]
            total = total + bt[2, start + 2 * dilation : start + 2 * dilation + rows, :]
            ig[start : start + rows, :] = total.astype(BF16)
        put_ig = load(ig, ig_hbm, 10)
        keep_g.wait()
        put_pg.wait()
        put_ig.wait()


def chain_call(dilation, flags, g, hs, a1, a2, w_full, held, padding):
    samples, channels = g.shape
    any_spec = pl.BlockSpec(memory_space=pl.ANY)
    shapes = (
        jax.ShapeDtypeStruct((samples, 2 * channels), BF16),
        jax.ShapeDtypeStruct((samples, channels), BF16),
        jax.ShapeDtypeStruct((samples, channels), BF16),
    )
    return pl.pallas_call(
        functools.partial(chain_kernel, dilation),
        out_shape=shapes,
        in_specs=[pl.BlockSpec(memory_space=pltpu.SMEM)] + [any_spec] * 8,
        out_specs=[any_spec] * 3,
        scratch_shapes=[
            pltpu.VMEM((samples, channels), BF16),
            pltpu.VMEM((samples, channels), F32),
            pltpu.VMEM((samples, channels), F32),
            pltpu.VMEM((samples, channels), F32),
            pltpu.VMEM((channels, channels), BF16),
            pltpu.VMEM((3, channels, 2 * channels), BF16),
            pltpu.VMEM((samples, 2 * channels), BF16),
            pltpu.VMEM((samples, channels), BF16),
            pltpu.VMEM((3, samples + padding, channels), F32),
            pltpu.SemaphoreType.DMA((11,)),
        ],
        input_output_aliases={6: 0, 7: 1, 8: 2},
        compiler_params=pltpu.CompilerParams(vmem_limit_bytes=24 * 2**20),
        cost_estimate=pl.CostEstimate(flops=2 * 10**9, bytes_accessed=8 * 2**20, transcendentals=0),
    )(flags, g, hs, a1, a2, w_full, *held)


def local(x_ckpt, top_cot, skip_cot, w_conv, w_mix):
    sections = lax.axis_size("pipe")
    section = lax.axis_index("pipe")
    replicas = lax.axis_size("dp")
    replica = lax.axis_index("dp")
    micro, seqs, samples, channels = x_ckpt.shape[1:]
    rows = micro * seqs * samples
    part = w_conv.shape[1]
    dilation = jnp.left_shift(jnp.int32(1), section)

    order = ring_order(replicas)
    right, left = ring_pairs(order)
    half = replicas // 2
    owners = jnp.array(order, jnp.int32)
    place = jnp.array([order.index(i) for i in range(replicas)], jnp.int32)[replica]

    def owner(offset):
        return owners[lax.rem(place + offset + replicas, replicas)]

    shard = jnp.concatenate([w_conv[0].transpose(1, 0, 2), w_mix], axis=0)
    w_full = jnp.zeros((4, channels, 2 * channels), BF16)

    def put(full, block, offset, first=0):
        return lax.dynamic_update_slice(full, block, (first, owner(offset) * part, 0))

    w_full = put(w_full, shard, 0)
    from_left, from_right = shard, shard
    for step in range(1, half):
        from_left = lax.ppermute(from_left, "dp", right)
        from_right = lax.ppermute(from_right, "dp", left)
        w_full = put(w_full, from_left, -step)
        w_full = put(w_full, from_right, step)
    w_full = put(w_full, lax.ppermute(from_left[:2], "dp", right), -half, 0)
    w_full = put(w_full, lax.ppermute(from_right[2:], "dp", left), half, 2)

    x_rows = x_ckpt[0].reshape(micro * seqs, samples, channels)
    positions = lax.broadcasted_iota(jnp.int32, (1, samples, 1), 1)
    taps = [x_rows]
    for k in (1, 2):
        rolled = jnp.roll(x_rows, k * dilation, axis=1)
        taps.append(jnp.where(positions >= k * dilation, rolled, jnp.zeros_like(rolled)))
    taps = jnp.concatenate(taps, axis=2).reshape(rows, 3 * channels)
    skip_rows = skip_cot.reshape(rows, channels)
    top_rows = top_cot.reshape(micro, seqs * samples, channels)

    w_taps = w_full[:3].reshape(3 * channels, 2 * channels)
    pre = jnp.dot(taps, w_taps, preferred_element_type=F32)
    filt = jnp.tanh(pre[:, :channels])
    gate = jax.nn.sigmoid(pre[:, channels:])
    hidden = (filt * gate).astype(BF16)
    a1 = gate * (1.0 - filt * filt)
    a2 = filt * gate * (1.0 - gate)
    h_skip = lax.dot_general(skip_rows, w_full[3, :, channels:], NT, preferred_element_type=F32)

    block = seqs * samples
    padding = max(16, 2 * 2 ** (sections - 1))

    def cut(array, m):
        return lax.slice_in_dim(array, m * block, (m + 1) * block, axis=0)

    parts = [(cut(h_skip, m), cut(a1, m), cut(a2, m)) for m in range(micro)]
    g = [top_rows[m] for m in range(micro)]
    held = [
        (jnp.zeros((block, 2 * channels), BF16), jnp.zeros((block, channels), BF16), jnp.zeros((block, channels), BF16))
        for m in range(micro)
    ]
    for stage in range(sections - 1, -1, -1):
        flags = (section == stage).astype(jnp.int32).reshape(1)
        for m in range(micro):
            held[m] = chain_call(2**stage, flags, g[m], *parts[m], w_full, held[m], padding)
            if stage:
                g[m] = lax.ppermute(held[m][1], "pipe", [(stage, stage - 1)])

    pre_grad = jnp.concatenate([h[0] for h in held], axis=0)
    cot = jnp.stack([h[1] for h in held], axis=0)
    g_all = jnp.concatenate([h[2] for h in held], axis=0)
    pair = jnp.concatenate([g_all, skip_rows], axis=1)
    over_rows = (((0,), (0,)), ((), ()))
    conv_term = lax.dot_general(taps, pre_grad, over_rows, preferred_element_type=F32).astype(BF16)
    mix_term = lax.dot_general(hidden, pair, over_rows, preferred_element_type=F32).astype(BF16)
    terms = jnp.concatenate([conv_term, mix_term], axis=0).reshape(4, channels, 2 * channels)

    def term(offset, first=0, count=4):
        return lax.dynamic_slice(terms, (first, owner(offset) * part, 0), (count, part, 2 * channels))

    to_right = lax.ppermute(term(half, 0, 2), "dp", right)
    to_left = lax.ppermute(term(-half, 2, 2), "dp", left)
    for dist in range(half - 1, 0, -1):
        mine_r, mine_l = term(dist), term(-dist)
        if dist == half - 1:
            zero = jnp.zeros_like(to_right)
            to_right = jnp.concatenate([to_right, zero], axis=0)
            to_left = jnp.concatenate([zero, to_left], axis=0)
        sum_r = (mine_r.astype(F32) + to_right.astype(F32)).astype(BF16)
        sum_l = (mine_l.astype(F32) + to_left.astype(F32)).astype(BF16)
        to_right = lax.ppermute(sum_r, "dp", right)
        to_left = lax.ppermute(sum_l, "dp", left)
    share = term(0).astype(F32) + to_right.astype(F32) + to_left.astype(F32)
    return (
        cot.reshape(1, micro, seqs, samples, channels),
        share[:3].transpose(1, 0, 2)[None],
        share[3][None],
    )


def solution(mesh):
    placed = (
        P("pipe", None, "dp", None, None),
        P(None, "dp", None, None),
        P(None, "dp", None, None),
        P("pipe", "dp", None, None),
        P("pipe", "dp", None),
    )
    return jax.shard_map(
        local,
        mesh=mesh,
        in_specs=placed,
        out_specs=(
            P("pipe", None, "dp", None, None),
            P("pipe", "dp", None, None),
            P("pipe", "dp", None),
        ),
        check_vma=False,
    )
```

```python
import functools

import jax
import jax.numpy as jnp
from jax import lax
from jax.experimental import pallas as pl
from jax.experimental.pallas import tpu as pltpu
from jax.sharding import PartitionSpec as P

F32 = jnp.float32
BF16 = jnp.bfloat16
NT = (((1,), (1,)), ((), ()))
VMEM_BYTES = 56 * 2**20
ANY = pl.BlockSpec(memory_space=pl.ANY)
SMEM = pl.BlockSpec(memory_space=pltpu.SMEM)


def ring_pairs(count):
    order = list(range(0, count, 2)) + list(range(count - 1 - count % 2, 0, -2))
    right = [(order[i], order[(i + 1) % count]) for i in range(count)]
    return right, [(b, a) for a, b in right]


def starter(sems):
    number = iter(range(sems.shape[0]))

    def start(source, target):
        copy = pltpu.make_async_copy(source, target, sems.at[next(number)])
        copy.start()
        return copy

    return start


def forward_kernel(pieces, owners, taps_hbm, skip_hbm, *refs):
    shards, refs = refs[: len(pieces)], refs[len(pieces) :]
    a1_hbm, a2_hbm, hs_hbm, hid_hbm, w_hbm, taps, skip, w, a1, a2, hs, hid, sems = refs
    samples, channels = skip.shape
    start = starter(sems)
    get_taps = start(taps_hbm, taps)
    get_conv, get_mix = [], []
    for (slot, first), shard in zip(pieces, shards):
        count, part = shard.shape[:2]
        offset = pl.multiple_of(owners[slot] * part, part)
        for k in range(count):
            tap = first + k
            copy = start(shard.at[k], w.at[pl.ds(tap * channels + offset, part), :])
            (get_mix if tap == 3 else get_conv).append(copy)
    get_skip = start(skip_hbm, skip)
    get_taps.wait()
    for copy in get_conv:
        copy.wait()
    chunk = samples // 2
    puts = []
    for at in range(0, samples, chunk):
        rows = slice(at, at + chunk)
        pre = jnp.dot(taps[rows, :], w[: 3 * channels, :], preferred_element_type=F32)
        filt = jnp.tanh(pre[:, :channels])
        gate = jax.nn.sigmoid(pre[:, channels:])
        hid[rows, :] = (filt * gate).astype(BF16)
        a1[rows, :] = gate * (1.0 - filt * filt)
        a2[rows, :] = filt * gate * (1.0 - gate)
        if not puts:
            get_skip.wait()
            for copy in get_mix:
                copy.wait()
            puts.append(start(w, w_hbm))
        hs[rows, :] = lax.dot_general(
            skip[rows, :], w[3 * channels :, channels:], NT, preferred_element_type=F32
        )
        for source, target in ((a1, a1_hbm), (a2, a2_hbm), (hs, hs_hbm), (hid, hid_hbm)):
            puts.append(start(source.at[rows, :], target.at[rows, :]))
    for copy in puts:
        copy.wait()


def forward_call(owners, taps, skip, pieces, shards):
    samples, channels = skip.shape
    tile = (samples, channels)
    full = (4 * channels, 2 * channels)
    return pl.pallas_call(
        functools.partial(forward_kernel, pieces),
        out_shape=[jax.ShapeDtypeStruct(tile, F32)] * 3
        + [jax.ShapeDtypeStruct(tile, BF16), jax.ShapeDtypeStruct(full, BF16)],
        in_specs=[SMEM] + [ANY] * (2 + len(shards)),
        out_specs=[ANY] * 5,
        scratch_shapes=[
            pltpu.VMEM(taps.shape, BF16),
            pltpu.VMEM(tile, BF16),
            pltpu.VMEM(full, BF16),
            pltpu.VMEM(tile, F32),
            pltpu.VMEM(tile, F32),
            pltpu.VMEM(tile, F32),
            pltpu.VMEM(tile, BF16),
            pltpu.SemaphoreType.DMA((2 + sum(s.shape[0] for s in shards) + 9,)),
        ],
        compiler_params=pltpu.CompilerParams(vmem_limit_bytes=VMEM_BYTES),
        cost_estimate=pl.CostEstimate(
            flops=8 * samples * channels * channels * 2, bytes_accessed=16 * 2**20, transcendentals=0
        ),
    )(owners, taps, skip, *shards)


def chain_kernel(dilation, held, flags, g_hbm, hs_hbm, a1_hbm, a2_hbm, w_hbm, *refs):
    pg_hbm, ig_hbm, gk_hbm, g, hs, a1, a2, wm, wc, pg, ig, bt, sems = refs[held:]
    samples, channels = g.shape
    padding = bt.shape[1] - samples

    @pl.when(flags[0] == 1)
    def _():
        start = starter(sems)
        get_g = start(g_hbm, g)
        get_wm = start(w_hbm.at[pl.ds(3 * channels, channels), pl.ds(0, channels)], wm)
        get_hs = start(hs_hbm, hs)
        get_a1 = start(a1_hbm, a1)
        get_a2 = start(a2_hbm, a2)
        get_wc = [start(w_hbm.at[pl.ds(k * channels, channels), :], wc.at[k]) for k in range(3)]
        for k in (1, 2):
            bt[k, samples:, :] = jnp.zeros((padding, channels), F32)
        get_g.wait()
        puts = [start(g, gk_hbm)]
        get_wm.wait()
        get_hs.wait()
        chunk = samples // 2
        for at in range(samples - chunk, -1, -chunk):
            rows = slice(at, at + chunk)
            hid = lax.dot_general(g[rows, :], wm[...], NT, preferred_element_type=F32) + hs[rows, :]
            if at == samples - chunk:
                get_a1.wait()
                get_a2.wait()
            pg[rows, :channels] = (hid * a1[rows, :]).astype(BF16)
            pg[rows, channels:] = (hid * a2[rows, :]).astype(BF16)
            for k in range(3):
                if at == samples - chunk:
                    get_wc[k].wait()
                bt[k, rows, :] = lax.dot_general(pg[rows, :], wc[k], NT, preferred_element_type=F32)
            piece = 64
            for first in range(at + chunk - piece, at - 1, -piece):
                last = first + piece
                total = g[first:last, :].astype(F32) + bt[0, first:last, :]
                total = total + bt[1, first + dilation : last + dilation, :]
                total = total + bt[2, first + 2 * dilation : last + 2 * dilation, :]
                ig[first:last, :] = total.astype(BF16)
            puts.append(start(ig.at[rows, :], ig_hbm.at[rows, :]))
            puts.append(start(pg.at[rows, :], pg_hbm.at[rows, :]))
        for copy in puts:
            copy.wait()


def chain_call(dilation, flags, g, hs, a1, a2, w_full, held, padding):
    samples, channels = g.shape
    tile = (samples, channels)
    return pl.pallas_call(
        functools.partial(chain_kernel, dilation, len(held)),
        out_shape=[
            jax.ShapeDtypeStruct((samples, 2 * channels), BF16),
            jax.ShapeDtypeStruct(tile, BF16),
            jax.ShapeDtypeStruct(tile, BF16),
        ],
        in_specs=[SMEM] + [ANY] * (5 + len(held)),
        out_specs=[ANY] * 3,
        scratch_shapes=[
            pltpu.VMEM(tile, BF16),
            pltpu.VMEM(tile, F32),
            pltpu.VMEM(tile, F32),
            pltpu.VMEM(tile, F32),
            pltpu.VMEM((channels, channels), BF16),
            pltpu.VMEM((3, channels, 2 * channels), BF16),
            pltpu.VMEM((samples, 2 * channels), BF16),
            pltpu.VMEM(tile, BF16),
            pltpu.VMEM((3, samples + padding, channels), F32),
            pltpu.SemaphoreType.DMA((13,)),
        ],
        input_output_aliases={6 + i: i for i in range(len(held))},
        compiler_params=pltpu.CompilerParams(vmem_limit_bytes=VMEM_BYTES),
        cost_estimate=pl.CostEstimate(
            flops=8 * samples * channels * channels, bytes_accessed=8 * 2**20, transcendentals=0
        ),
    )(flags, g, hs, a1, a2, w_full, *held)


def local(x_ckpt, top_cot, skip_cot, w_conv, w_mix):
    sections = lax.axis_size("pipe")
    section = lax.axis_index("pipe")
    replicas = lax.axis_size("dp")
    replica = lax.axis_index("dp")
    micro, seqs, samples, channels = x_ckpt.shape[1:]
    rows = micro * seqs * samples
    block = seqs * samples
    part = w_conv.shape[1]
    half = replicas // 2
    dilation = jnp.left_shift(jnp.int32(1), section)
    right, left = ring_pairs(replicas)
    place = jnp.where(replica % 2 == 0, replica // 2, replicas - 1 - replica // 2)

    def owner(offset):
        at = lax.rem(place + (offset + replicas), replicas)
        return jnp.where(at < half, 2 * at, 2 * (replicas - 1 - at) + 1)

    conv = w_conv[0].transpose(1, 0, 2)
    conv_r, conv_l, mix_r, mix_l = conv, conv, w_mix, w_mix
    pieces, shards = [(0, 0), (0, 3)], [conv, w_mix]
    offsets = [0]

    def keep(offset, *blocks):
        offsets.append(offset)
        for first, shard in blocks:
            pieces.append((len(offsets) - 1, first))
            shards.append(shard)

    for step in range(1, half):
        conv_r = lax.ppermute(conv_r, "dp", right)
        conv_l = lax.ppermute(conv_l, "dp", left)
        mix_r = lax.ppermute(mix_r, "dp", right)
        mix_l = lax.ppermute(mix_l, "dp", left)
        keep(-step, (0, conv_r), (3, mix_r))
        keep(step, (0, conv_l), (3, mix_l))
    conv_r = lax.ppermute(conv_r[:2], "dp", right)
    conv_l = lax.ppermute(conv_l[2:], "dp", left)
    mix_l = lax.ppermute(mix_l, "dp", left)
    keep(half, (0, conv_r), (2, conv_l), (3, mix_l))
    owners = jnp.stack([owner(offset) for offset in offsets])

    x_rows = x_ckpt[0].reshape(micro * seqs, samples, channels)
    positions = lax.broadcasted_iota(jnp.int32, (1, samples, 1), 1)
    taps = [x_rows]
    for k in (1, 2):
        rolled = jnp.roll(x_rows, k * dilation, axis=1)
        taps.append(jnp.where(positions >= k * dilation, rolled, jnp.zeros_like(rolled)))
    taps = jnp.concatenate(taps, axis=2).reshape(micro, block, 3 * channels)
    skip = skip_cot.reshape(micro, block, channels)
    g = list(top_cot.reshape(micro, block, channels))
    padding = max(16, 2 * 2 ** (sections - 1))

    hidden, held, ready = [], [()] * micro, []
    for m in range(micro):
        a1, a2, hs, hid, w_full = forward_call(owners, taps[m], skip[m], pieces, shards)
        hidden.append(hid)
        ready.append((hs, a1, a2, w_full))
    for stage in range(sections - 1, -1, -1):
        flags = (section == stage).astype(jnp.int32).reshape(1)
        for m in range(micro):
            held[m] = chain_call(2**stage, flags, g[m], *ready[m], held[m], padding)
            if stage:
                g[m] = lax.ppermute(held[m][1], "pipe", [(stage, stage - 1)])

    pre_grad = jnp.concatenate([h[0] for h in held], axis=0)
    cot = jnp.stack([h[1] for h in held], axis=0)
    g_all = jnp.concatenate([h[2] for h in held], axis=0)
    pair = jnp.concatenate([g_all, skip.reshape(rows, channels)], axis=1)
    over_rows = (((0,), (0,)), ((), ()))
    conv_term = lax.dot_general(
        taps.reshape(rows, 3 * channels), pre_grad, over_rows, preferred_element_type=F32
    ).astype(BF16)
    mix_term = lax.dot_general(
        jnp.concatenate(hidden, axis=0), pair, over_rows, preferred_element_type=F32
    ).astype(BF16)
    terms = jnp.concatenate([conv_term, mix_term], axis=0).reshape(4, channels, 2 * channels)

    def term(offset, first):
        return lax.dynamic_slice(terms, (first, owner(offset) * part, 0), (2, part, 2 * channels))

    def add(mine, theirs):
        if theirs is None:
            return mine
        return (mine.astype(F32) + theirs.astype(F32)).astype(BF16)

    sums = {(1, 0): None, (1, 2): None, (-1, 0): None, (-1, 2): None}
    for dist in range(half, 0, -1):
        for way, first in ((1, 0), (-1, 2), (1, 2), (-1, 0)):
            if dist == half and (way, first) in ((1, 2), (-1, 0)):
                continue
            message = add(term(way * dist, first), sums[way, first])
            sums[way, first] = lax.ppermute(message, "dp", right if way == 1 else left)
    share = [
        term(0, first).astype(F32) + sums[1, first].astype(F32) + sums[-1, first].astype(F32)
        for first in (0, 2)
    ]
    share_conv = jnp.concatenate([share[0], share[1][:1]], axis=0)
    return (
        cot.reshape(1, micro, seqs, samples, channels),
        share_conv.transpose(1, 0, 2)[None],
        share[1][1][None],
    )


def solution(mesh):
    placed = (
        P("pipe", None, "dp", None, None),
        P(None, "dp", None, None),
        P(None, "dp", None, None),
        P("pipe", "dp", None, None),
        P("pipe", "dp", None),
    )
    return jax.shard_map(
        local,
        mesh=mesh,
        in_specs=placed,
        out_specs=(
            P("pipe", None, "dp", None, None),
            P("pipe", "dp", None, None),
            P("pipe", "dp", None),
        ),
        check_vma=False,
    )
```

```python
import functools

import jax
import jax.numpy as jnp
from jax import lax
from jax.experimental import pallas as pl
from jax.experimental.pallas import tpu as pltpu
from jax.sharding import PartitionSpec as P

F32 = jnp.float32
BF16 = jnp.bfloat16
NT = (((1,), (1,)), ((), ()))
VMEM_BYTES = 56 * 2**20
ANY = pl.BlockSpec(memory_space=pl.ANY)
SMEM = pl.BlockSpec(memory_space=pltpu.SMEM)


def ring_pairs(count):
    order = list(range(0, count, 2)) + list(range(count - 1 - count % 2, 0, -2))
    right = [(order[i], order[(i + 1) % count]) for i in range(count)]
    return right, [(b, a) for a, b in right]


def starter(sems):
    number = iter(range(sems.shape[0]))

    def start(source, target):
        copy = pltpu.make_async_copy(source, target, sems.at[next(number)])
        copy.start()
        return copy

    return start


def partial_kernel(count, first, owners, *refs):
    taps, convs, mixes = refs[:count], refs[count : 2 * count], refs[2 * count : 3 * count]
    refs = refs[3 * count :]
    acc_in = None if first else refs[0]
    acc, w, sems = refs[-3:]
    channels = w.shape[0] // 4
    part = convs[0].shape[1]

    def copies():
        start = starter(sems)
        found = []
        for slot, conv, mix in zip(range(count), convs, mixes):
            offset = pl.multiple_of(owners[slot] * part, part)
            for k in range(3):
                found.append(start(conv.at[k], w.at[pl.ds(k * channels + offset, part), :]))
            found.append(start(mix.at[0], w.at[pl.ds(3 * channels + offset, part), :]))
        return found

    total = None if first else acc_in[...]
    for tap, conv in zip(taps, convs):
        term = jnp.dot(tap[...], conv[...].reshape(3 * part, -1), preferred_element_type=F32)
        total = term if total is None else total + term
    acc[...] = total

    @pl.when(pl.program_id(0) == 0)
    def _():
        for copy in copies():
            copy.wait()


def partial_call(owners, taps, convs, mixes, acc, w):
    count = len(convs)
    replicas, rows, depth = taps.shape
    channels = depth * replicas // 3
    wide = 2 * channels
    chunk = 256
    first = acc is None
    tap_specs = [
        pl.BlockSpec((None, chunk, depth), functools.partial(lambda slot, i, own: (own[slot], i, 0), slot))
        for slot in range(count)
    ]
    shard_specs = [pl.BlockSpec(a.shape, lambda i, own: (0, 0, 0)) for a in (*convs, *mixes)]
    acc_spec = pl.BlockSpec((chunk, wide), lambda i, own: (i, 0))
    held = [] if first else [acc, w]
    return pl.pallas_call(
        functools.partial(partial_kernel, count, first),
        out_shape=[
            jax.ShapeDtypeStruct((rows, wide), F32),
            jax.ShapeDtypeStruct((4 * channels, wide), BF16),
        ],
        grid_spec=pltpu.PrefetchScalarGridSpec(
            num_scalar_prefetch=1,
            grid=(rows // chunk,),
            in_specs=tap_specs + shard_specs + ([] if first else [acc_spec, ANY]),
            out_specs=[acc_spec, ANY],
            scratch_shapes=[pltpu.SemaphoreType.DMA((4 * count,))],
        ),
        input_output_aliases={} if first else {1 + 3 * count: 0, 2 + 3 * count: 1},
        compiler_params=pltpu.CompilerParams(vmem_limit_bytes=VMEM_BYTES),
        cost_estimate=pl.CostEstimate(
            flops=2 * rows * depth * count * wide, bytes_accessed=8 * rows * wide, transcendentals=0
        ),
    )(owners, *([taps] * count), *convs, *mixes, *held)


def forward_kernel(store, owners, taps, conv_a, conv_b, mix, acc, _w, *refs):
    a1, a2, hid_t = refs[:3]
    part = mix.shape[1]
    depth_a = conv_a.shape[0] * part
    channels = a1.shape[1]
    pre = acc[...] + jnp.dot(
        taps[:, :depth_a], conv_a[...].reshape(depth_a, -1), preferred_element_type=F32
    )
    pre = pre + jnp.dot(
        taps[:, depth_a:], conv_b[...].reshape(3 * part - depth_a, -1), preferred_element_type=F32
    )
    filt = jnp.tanh(pre[:, :channels])
    gate = jax.nn.sigmoid(pre[:, channels:])
    a1[...] = (gate * (1.0 - filt * filt)).astype(BF16)
    a2[...] = (filt * gate * (1.0 - gate)).astype(BF16)
    hid_t[...] = (filt * gate).T.astype(BF16)
    if store:
        w, sems = refs[3:]

        @pl.when(pl.program_id(0) == 0)
        def _():
            start = starter(sems)
            offset = pl.multiple_of(owners[0] * part, part)
            blocks = [conv_a.at[k] for k in range(conv_a.shape[0])]
            blocks += [conv_b.at[k] for k in range(conv_b.shape[0])] + [mix.at[0]]
            copies = [
                start(block, w.at[pl.ds(k * channels + offset, part), :]) for k, block in enumerate(blocks)
            ]
            for copy in copies:
                copy.wait()


def forward_call(owners, taps, conv_a, conv_b, mix, acc, w, index, micro, store):
    rows, wide = acc.shape
    channels = wide // 2
    samples = rows // micro
    chunk = 256
    steps = samples // chunk
    shift = index * steps
    tile = pl.BlockSpec((chunk, channels), lambda i, own: (i, 0))
    shapes = [jax.ShapeDtypeStruct((samples, channels), BF16)] * 2
    shapes.append(jax.ShapeDtypeStruct((channels, samples), BF16))
    specs = [tile, tile, pl.BlockSpec((channels, chunk), lambda i, own: (0, i))]
    return pl.pallas_call(
        functools.partial(forward_kernel, store),
        out_shape=shapes + ([jax.ShapeDtypeStruct(w.shape, BF16)] if store else []),
        grid_spec=pltpu.PrefetchScalarGridSpec(
            num_scalar_prefetch=1,
            grid=(steps,),
            in_specs=[pl.BlockSpec((None, chunk, taps.shape[2]), lambda i, own: (own[0], i + shift, 0))]
            + [pl.BlockSpec(a.shape, lambda i, own: (0, 0, 0)) for a in (conv_a, conv_b, mix)]
            + [pl.BlockSpec((chunk, wide), lambda i, own: (i + shift, 0)), ANY],
            out_specs=specs + ([ANY] if store else []),
            scratch_shapes=[pltpu.SemaphoreType.DMA((4,))] if store else [],
        ),
        input_output_aliases={6: 3} if store else {},
        compiler_params=pltpu.CompilerParams(vmem_limit_bytes=VMEM_BYTES),
        cost_estimate=pl.CostEstimate(
            flops=2 * samples * taps.shape[2] * wide, bytes_accessed=6 * samples * wide, transcendentals=0
        ),
    )(owners, taps, conv_a, conv_b, mix, acc, w)


def chain_kernel(dilation, held, flags, g_hbm, skip_hbm, a1_hbm, a2_hbm, w_hbm, *refs):
    pg_hbm, ig_hbm, gk_hbm, pair, a1, a2, w, pg, ig, bt, sems = refs[held:]
    samples, channels = ig.shape
    padding = bt.shape[1] - samples

    @pl.when(flags[0] == 1)
    def _():
        start = starter(sems)
        get_g = start(g_hbm, pair.at[:, pl.ds(0, channels)])
        get_wm = start(w_hbm.at[pl.ds(3 * channels, channels), :], w.at[3])
        get_skip = start(skip_hbm, pair.at[:, pl.ds(channels, channels)])
        get_a1 = start(a1_hbm, a1)
        get_a2 = start(a2_hbm, a2)
        get_wc = [start(w_hbm.at[pl.ds(k * channels, channels), :], w.at[k]) for k in range(3)]
        for k in (1, 2):
            bt[k, samples:, :] = jnp.zeros((padding, channels), F32)
        get_g.wait()
        puts = [start(pair.at[:, pl.ds(0, channels)], gk_hbm)]
        get_wm.wait()
        get_skip.wait()
        chunk = samples // 2
        for at in range(samples - chunk, -1, -chunk):
            rows = slice(at, at + chunk)
            hid = lax.dot_general(pair[rows, :], w[3], NT, preferred_element_type=F32)
            if at == samples - chunk:
                get_a1.wait()
                get_a2.wait()
            pg[rows, :channels] = (hid * a1[rows, :].astype(F32)).astype(BF16)
            pg[rows, channels:] = (hid * a2[rows, :].astype(F32)).astype(BF16)
            for k in range(3):
                if at == samples - chunk:
                    get_wc[k].wait()
                bt[k, rows, :] = lax.dot_general(pg[rows, :], w[k], NT, preferred_element_type=F32)
            piece = 64
            for first in range(at + chunk - piece, at - 1, -piece):
                last = first + piece
                total = pair[first:last, :channels].astype(F32) + bt[0, first:last, :]
                total = total + bt[1, first + dilation : last + dilation, :]
                total = total + bt[2, first + 2 * dilation : last + 2 * dilation, :]
                ig[first:last, :] = total.astype(BF16)
            puts.append(start(ig.at[rows, :], ig_hbm.at[rows, :]))
            puts.append(start(pg.at[rows, :], pg_hbm.at[rows, :]))
        for copy in puts:
            copy.wait()


def chain_call(dilation, flags, g, skip, a1, a2, w_full, held, padding):
    samples, channels = g.shape
    tile = (samples, channels)
    return pl.pallas_call(
        functools.partial(chain_kernel, dilation, len(held)),
        out_shape=[
            jax.ShapeDtypeStruct((samples, 2 * channels), BF16),
            jax.ShapeDtypeStruct(tile, BF16),
            jax.ShapeDtypeStruct(tile, BF16),
        ],
        in_specs=[SMEM] + [ANY] * (5 + len(held)),
        out_specs=[ANY] * 3,
        scratch_shapes=[
            pltpu.VMEM((samples, 2 * channels), BF16),
            pltpu.VMEM(tile, BF16),
            pltpu.VMEM(tile, BF16),
            pltpu.VMEM((4, channels, 2 * channels), BF16),
            pltpu.VMEM((samples, 2 * channels), BF16),
            pltpu.VMEM(tile, BF16),
            pltpu.VMEM((3, samples + padding, channels), F32),
            pltpu.SemaphoreType.DMA((13,)),
        ],
        input_output_aliases={6 + i: i for i in range(len(held))},
        compiler_params=pltpu.CompilerParams(vmem_limit_bytes=VMEM_BYTES),
        cost_estimate=pl.CostEstimate(
            flops=8 * samples * channels * channels, bytes_accessed=8 * 2**20, transcendentals=0
        ),
    )(flags, g, skip, a1, a2, w_full, *held)


def term_kernel(count, micro, tokens, owners, taps_hbm, skip_hbm, *refs):
    hids, refs = refs[:micro], refs[micro:]
    pgs, refs = refs[:micro], refs[micro:]
    gs, refs = refs[:micro], refs[micro + tokens :]
    outs, refs = refs[:count], refs[count:]
    lhs, lhs_mix, pg, pair, sems = refs
    rows, wide = pg.shape
    channels = wide // 2
    samples = rows // micro
    part = lhs.shape[0] // (3 * count)
    start = starter(sems)
    gets = []
    for m in range(micro):
        here = pl.ds(m * samples, samples)
        gets.append(start(pgs[m], pg.at[here, :]))
    for slot in range(count):
        offset = pl.multiple_of(owners[slot] * part, part)
        for k in range(3):
            to = lhs.at[pl.ds((slot * 3 + k) * part, part), :]
            gets.append(start(taps_hbm.at[pl.ds(k * channels + offset, part), :], to))
    late = [start(skip_hbm, pair.at[:, pl.ds(channels, channels)])]
    for m in range(micro):
        here = pl.ds(m * samples, samples)
        late.append(start(gs[m], pair.at[here, pl.ds(0, channels)]))
        for slot in range(count):
            offset = pl.multiple_of(owners[slot] * part, part)
            to = lhs_mix.at[pl.ds(slot * part, part), here]
            late.append(start(hids[m].at[pl.ds(offset, part), :], to))
    for copy in gets:
        copy.wait()
    conv = jnp.dot(lhs[...], pg[...], preferred_element_type=F32)
    for copy in late:
        copy.wait()
    mix = jnp.dot(lhs_mix[...], pair[...], preferred_element_type=F32)
    for slot, out in enumerate(outs):
        kind = out.dtype
        out[0:3] = conv[slot * 3 * part : (slot + 1) * 3 * part, :].reshape(3, part, wide).astype(kind)
        out[3] = mix[slot * part : (slot + 1) * part, :].astype(kind)


def term_call(owners, taps_t, skip, hid_t, pre_grads, gs, tokens, kind):
    count = owners.shape[0]
    micro = len(gs)
    rows, channels = skip.shape
    wide = 2 * channels
    part = channels // lax.axis_size("dp")
    copies = micro + 3 * count + 1 + micro + micro * count
    return pl.pallas_call(
        functools.partial(term_kernel, count, micro, len(tokens)),
        out_shape=[jax.ShapeDtypeStruct((4, part, wide), kind)] * count,
        in_specs=[SMEM] + [ANY] * (2 + 3 * micro + len(tokens)),
        out_specs=[pl.BlockSpec(memory_space=pltpu.VMEM)] * count,
        scratch_shapes=[
            pltpu.VMEM((3 * part * count, rows), BF16),
            pltpu.VMEM((part * count, rows), BF16),
            pltpu.VMEM((rows, wide), BF16),
            pltpu.VMEM((rows, wide), BF16),
            pltpu.SemaphoreType.DMA((copies,)),
        ],
        compiler_params=pltpu.CompilerParams(vmem_limit_bytes=VMEM_BYTES),
        cost_estimate=pl.CostEstimate(
            flops=8 * part * count * rows * wide, bytes_accessed=6 * 2**20, transcendentals=0
        ),
    )(owners, taps_t, skip, *hid_t, *pre_grads, *gs, *tokens)


def add_kernel(mine_r, mine_l, got_r, got_l, *refs):
    out_r, out_l = refs[-2:]
    out_r[...] = (mine_r[...].astype(F32) + got_r[...].astype(F32)).astype(BF16)
    out_l[...] = (mine_l[...].astype(F32) + got_l[...].astype(F32)).astype(BF16)


def add_call(mine, got, firsts, tokens):
    shape = got[0].shape
    specs = [
        pl.BlockSpec(shape, functools.partial(lambda at, i: (at, 0, 0), first // 2)) for first in firsts
    ]
    here = pl.BlockSpec(shape, lambda i: (0, 0, 0))
    return pl.pallas_call(
        add_kernel,
        grid=(1,),
        out_shape=[jax.ShapeDtypeStruct(shape, BF16)] * 2,
        in_specs=specs + [here, here] + [ANY] * len(tokens),
        out_specs=[here, here],
        compiler_params=pltpu.CompilerParams(vmem_limit_bytes=VMEM_BYTES),
        cost_estimate=pl.CostEstimate(flops=2**18, bytes_accessed=3 * 2**19, transcendentals=0),
    )(*mine, *got, *tokens)


def final_kernel(mine, low_r, low_l, high_r, high_l, conv, mix):
    low = low_r[...].astype(F32) + low_l[...].astype(F32)
    high = high_r[...].astype(F32) + high_l[...].astype(F32)
    conv[0:2] = mine[0:2] + low
    conv[2] = mine[2] + high[0]
    mix[...] = mine[3] + high[1]


def final_call(mine, low_r, low_l, high_r, high_l):
    part, wide = mine.shape[1:]
    spec = pl.BlockSpec(memory_space=pltpu.VMEM)
    return pl.pallas_call(
        final_kernel,
        out_shape=[jax.ShapeDtypeStruct((3, part, wide), F32), jax.ShapeDtypeStruct((part, wide), F32)],
        in_specs=[spec] * 5,
        out_specs=[spec] * 2,
        compiler_params=pltpu.CompilerParams(vmem_limit_bytes=VMEM_BYTES),
        cost_estimate=pl.CostEstimate(flops=2**19, bytes_accessed=3 * 2**20, transcendentals=0),
    )(mine, low_r, low_l, high_r, high_l)


def local(x_ckpt, top_cot, skip_cot, w_conv, w_mix):
    sections = lax.axis_size("pipe")
    section = lax.axis_index("pipe")
    replicas = lax.axis_size("dp")
    replica = lax.axis_index("dp")
    micro, seqs, samples, channels = x_ckpt.shape[1:]
    rows = micro * seqs * samples
    block = seqs * samples
    part = w_conv.shape[1]
    half = replicas // 2
    dilation = jnp.left_shift(jnp.int32(1), section)
    right, left = ring_pairs(replicas)
    place = jnp.where(replica % 2 == 0, replica // 2, replicas - 1 - replica // 2)

    def owner(offset):
        at = lax.rem(place + (offset + replicas), replicas)
        return jnp.where(at < half, 2 * at, 2 * (replicas - 1 - at) + 1)

    def owners(*offsets):
        return jnp.stack([owner(offset) for offset in offsets])

    x_rows = x_ckpt[0].reshape(micro * seqs, samples, channels)
    positions = lax.broadcasted_iota(jnp.int32, (1, samples, 1), 1)
    taps = [x_rows]
    for k in (1, 2):
        rolled = jnp.roll(x_rows, k * dilation, axis=1)
        taps.append(jnp.where(positions >= k * dilation, rolled, jnp.zeros_like(rolled)))
    taps = jnp.stack(taps, axis=2).reshape(rows, 3, replicas, part)
    taps_t = taps.transpose(1, 2, 3, 0).reshape(3 * channels, rows)
    taps = taps.transpose(2, 0, 1, 3).reshape(replicas, rows, 3 * part)

    conv = w_conv[0].transpose(1, 0, 2)
    conv_r, conv_l, mix_r, mix_l = conv, conv, w_mix, w_mix
    acc, w_full = partial_call(owners(0), taps, [conv], [w_mix], None, None)
    for step in range(1, half):
        conv_r = lax.ppermute(conv_r, "dp", right)
        conv_l = lax.ppermute(conv_l, "dp", left)
        mix_r = lax.ppermute(mix_r, "dp", right)
        mix_l = lax.ppermute(mix_l, "dp", left)
        acc, w_full = partial_call(
            owners(-step, step), taps, [conv_r, conv_l], [mix_r, mix_l], acc, w_full
        )
    conv_r = lax.ppermute(conv_r[:2], "dp", right)
    conv_l = lax.ppermute(conv_l[2:], "dp", left)
    mix_l = lax.ppermute(mix_l, "dp", left)

    skip = skip_cot.reshape(micro, block, channels)
    g = list(top_cot.reshape(micro, block, channels))
    padding = max(16, 2 * 2 ** (sections - 1))
    hid_t, held, ready = [], [()] * micro, []
    for m in range(micro):
        a1, a2, hid, *stored = forward_call(
            owners(half), taps, conv_r, conv_l, mix_l, acc, w_full, m, micro, m == 0
        )
        if stored:
            w_full = stored[0]
        hid_t.append(hid)
        ready.append((skip[m], a1, a2))
    for stage in range(sections - 1, -1, -1):
        flags = (section == stage).astype(jnp.int32).reshape(1)
        for m in range(micro):
            held[m] = chain_call(2**stage, flags, g[m], *ready[m], w_full, held[m], padding)
            if stage:
                g[m] = lax.ppermute(held[m][1], "pipe", [(stage, stage - 1)])
    pre_grads, cots, gs = zip(*held)
    cot = jnp.stack(cots, axis=0)

    def terms(dist, tokens, kind=BF16):
        numbers = owners(dist) if dist in (0, half) else owners(dist, -dist)
        skip_rows = skip.reshape(rows, channels)
        return term_call(numbers, taps_t, skip_rows, hid_t, pre_grads, gs, tokens, kind)

    def send(to_right, to_left):
        return lax.ppermute(to_right, "dp", right), lax.ppermute(to_left, "dp", left)

    (mine,) = terms(half, ())
    got_one = send(mine[:2], mine[2:])
    mine = terms(half - 1, (mine,))
    got_two = send(mine[0][2:], mine[1][:2])
    token = ()
    for dist in range(half - 1, 0, -1):
        if dist < half - 1:
            out = add_call(mine, got_two, (2, 0), token)
            token = out[:1]
            got_two = send(*out)
        out = add_call(mine, got_one, (0, 2), token)
        token = out[:1]
        got_one = send(*out)
        if dist > 1:
            mine = terms(dist - 1, token)
    (mine,) = terms(0, token, F32)
    share_conv, share_mix = final_call(mine, got_one[0], got_two[1], got_two[0], got_one[1])
    return (
        cot.reshape(1, micro, seqs, samples, channels),
        share_conv.transpose(1, 0, 2)[None],
        share_mix[None],
    )


def solution(mesh):
    placed = (
        P("pipe", None, "dp", None, None),
        P(None, "dp", None, None),
        P(None, "dp", None, None),
        P("pipe", "dp", None, None),
        P("pipe", "dp", None),
    )
    return jax.shard_map(
        local,
        mesh=mesh,
        in_specs=placed,
        out_specs=(
            P("pipe", None, "dp", None, None),
            P("pipe", "dp", None, None),
            P("pipe", "dp", None),
        ),
        check_vma=False,
    )
```

```python
import functools

import jax
import jax.numpy as jnp
from jax import lax
from jax.experimental import pallas as pl
from jax.experimental.pallas import tpu as pltpu
from jax.sharding import PartitionSpec as P

F32 = jnp.float32
BF16 = jnp.bfloat16
NT = (((1,), (1,)), ((), ()))
TN = (((0,), (0,)), ((), ()))
SMEM = pl.BlockSpec(memory_space=pltpu.SMEM)
VMEM = pl.BlockSpec(memory_space=pltpu.VMEM)
PARAMS = pltpu.CompilerParams(vmem_limit_bytes=24 * 2**20)


def ring_pairs(count):
    order = list(range(0, count, 2)) + list(range(count - 1 - count % 2, 0, -2))
    right = [(order[i], order[(i + 1) % count]) for i in range(count)]
    return right, [(b, a) for a, b in right]


def in_vmem(*arrays):
    return [pltpu.with_memory_space_constraint(array, pltpu.VMEM) for array in arrays]


def cost(flops, moved):
    return pl.CostEstimate(flops=flops, bytes_accessed=moved, transcendentals=0)


def owner_row(where, replicas, part, offset):
    at = lax.rem(where[0] + (offset + replicas), replicas)
    owner = jnp.where(at < replicas // 2, 2 * at, 2 * (replicas - 1 - at) + 1)
    return pl.multiple_of(owner * part, part)


def prepare_kernel(where, x, taps_t):
    seqs, samples, channels = x.shape
    dilation = jnp.left_shift(jnp.int32(1), where[1])
    wide = 128
    for s in range(seqs):
        columns = slice(s * samples, (s + 1) * samples)
        for at in range(0, channels, wide):
            turned = x[s, :, at : at + wide].astype(F32).T
            position = lax.broadcasted_iota(jnp.int32, turned.shape, 1)
            taps_t[at : at + wide, columns] = turned.astype(BF16)
            for k in (1, 2):
                delayed = jnp.where(position >= k * dilation, pltpu.roll(turned, k * dilation, 1), 0.0)
                taps_t[k * channels + at : k * channels + at + wide, columns] = delayed.astype(BF16)


def prepare_call(where, x):
    seqs, samples, channels = x.shape
    return pl.pallas_call(
        prepare_kernel,
        out_shape=pltpu.VMEM((3 * channels, seqs * samples), BF16),
        in_specs=[SMEM, VMEM],
        out_specs=VMEM,
        compiler_params=PARAMS,
        cost_estimate=cost(2**20, 2**22),
    )(where, x)


def tap_rows(taps_t, row, part, columns, first=0, last=3):
    channels = taps_t.shape[0] // 3
    return jnp.concatenate(
        [taps_t[pl.ds(k * channels + row, part), columns] for k in range(first, last)], axis=0
    )


def partial_kernel(replicas, offsets, where, taps_t, *refs):
    count = len(offsets)
    convs, mixes, refs = refs[:count], refs[count : 2 * count], refs[2 * count :]
    acc, w = refs[-2:]
    rows = taps_t.shape[1]
    channels = w.shape[0] // 4
    part = convs[0].shape[1]
    chunk = min(256, rows)
    places = [owner_row(where, replicas, part, offset) for offset in offsets]
    for at in range(0, rows, chunk):
        columns = slice(at, at + chunk)
        total = refs[0][columns, :] if len(refs) == 4 else None
        for row, conv in zip(places, convs):
            term = lax.dot_general(
                tap_rows(taps_t, row, part, columns),
                conv[...].reshape(3 * part, -1),
                TN,
                preferred_element_type=F32,
            )
            total = term if total is None else total + term
        acc[columns, :] = total
    for row, conv, mix in zip(places, convs, mixes):
        for k in range(3):
            w[pl.ds(k * channels + row, part), :] = conv[k]
        w[pl.ds(3 * channels + row, part), :] = mix[0]


def partial_call(replicas, offsets, where, taps_t, convs, mixes, held):
    part, wide = convs[0].shape[1:]
    rows = taps_t.shape[1]
    count = len(offsets)
    inputs = in_vmem(taps_t, *convs, *mixes, *held)
    return pl.pallas_call(
        functools.partial(partial_kernel, replicas, offsets),
        out_shape=[pltpu.VMEM((rows, wide), F32), pltpu.VMEM((2 * wide, wide), BF16)],
        in_specs=[SMEM] + [VMEM] * len(inputs),
        out_specs=[VMEM] * 2,
        input_output_aliases={len(inputs) - 1 + i: i for i in range(len(held))},
        compiler_params=PARAMS,
        cost_estimate=cost(6 * rows * part * count * wide, 2**20),
    )(where, *inputs)


def forward_kernel(replicas, index, store, where, taps_t, conv_a, conv_b, mix, acc, w_in, *refs):
    a1, a2, hid_t = refs[:3]
    samples, channels = a1.shape
    part = mix.shape[1]
    row = owner_row(where, replicas, part, replicas // 2)
    ahead = conv_a.shape[0]
    chunk = min(256, samples)
    for at in range(0, samples, chunk):
        columns = slice(index * samples + at, index * samples + at + chunk)
        pre = acc[columns, :]
        for conv, first, last in ((conv_a, 0, ahead), (conv_b, ahead, 3)):
            pre = pre + lax.dot_general(
                tap_rows(taps_t, row, part, columns, first, last),
                conv[...].reshape((last - first) * part, -1),
                TN,
                preferred_element_type=F32,
            )
        filt = jnp.tanh(pre[:, :channels])
        gate = jax.nn.sigmoid(pre[:, channels:])
        a1[at : at + chunk, :] = (gate * (1.0 - filt * filt)).astype(BF16)
        a2[at : at + chunk, :] = (filt * gate * (1.0 - gate)).astype(BF16)
        hid_t[:, at : at + chunk] = (filt * gate).T.astype(BF16)
    if store:
        w = refs[3]
        blocks = [conv_a[k] for k in range(ahead)] + [conv_b[k] for k in range(3 - ahead)] + [mix[0]]
        for k, block in enumerate(blocks):
            w[pl.ds(k * channels + row, part), :] = block


def forward_call(replicas, index, micro, store, where, taps_t, conv_a, conv_b, mix, acc, w):
    rows, wide = acc.shape
    channels = wide // 2
    samples = rows // micro
    inputs = in_vmem(taps_t, conv_a, conv_b, mix, acc, w)
    return pl.pallas_call(
        functools.partial(forward_kernel, replicas, index, store),
        out_shape=[pltpu.VMEM((samples, channels), BF16)] * 2
        + [pltpu.VMEM((channels, samples), BF16)]
        + ([pltpu.VMEM(w.shape, BF16)] if store else []),
        in_specs=[SMEM] + [VMEM] * 6,
        out_specs=[VMEM] * (4 if store else 3),
        input_output_aliases={6: 3} if store else {},
        compiler_params=PARAMS,
        cost_estimate=cost(2**28, 2**22),
    )(where, *inputs)


def chain_kernel(stage, index, where, g, skip, a1, a2, w, *refs):
    pg, ig, gk, bt = refs[-4:]
    samples, channels = g.shape
    padding = bt.shape[1] - samples
    dilation = 2**stage

    @pl.when(where[1] == stage)
    def _():
        for k in (1, 2):
            bt[k, samples:, :] = jnp.zeros((padding, channels), F32)
        chunk = samples // 2
        for at in range(samples - chunk, -1, -chunk):
            rows = slice(at, at + chunk)
            hid = lax.dot_general(
                g[rows, :], w[3 * channels :, :channels], NT, preferred_element_type=F32
            ) + lax.dot_general(
                skip[index, rows, :], w[3 * channels :, channels:], NT, preferred_element_type=F32
            )
            pg[rows, :channels] = (hid * a1[rows, :].astype(F32)).astype(BF16)
            pg[rows, channels:] = (hid * a2[rows, :].astype(F32)).astype(BF16)
            for k in range(3):
                bt[k, rows, :] = lax.dot_general(
                    pg[rows, :], w[k * channels : (k + 1) * channels, :], NT, preferred_element_type=F32
                )
            piece = 64
            for first in range(at + chunk - piece, at - 1, -piece):
                last = first + piece
                total = g[first:last, :].astype(F32) + bt[0, first:last, :]
                total = total + bt[1, first + dilation : last + dilation, :]
                total = total + bt[2, first + 2 * dilation : last + 2 * dilation, :]
                ig[first:last, :] = total.astype(BF16)
        gk[...] = g[...]


def chain_call(stage, index, padding, where, g, skip, a1, a2, w, held):
    samples, channels = g.shape
    tile = (samples, channels)
    inputs = in_vmem(g, skip, a1, a2, w, *held)
    return pl.pallas_call(
        functools.partial(chain_kernel, stage, index),
        out_shape=[pltpu.VMEM((samples, 2 * channels), BF16), pltpu.VMEM(tile, BF16), pltpu.VMEM(tile, BF16)],
        in_specs=[SMEM] + [VMEM] * len(inputs),
        out_specs=[VMEM] * 3,
        scratch_shapes=[pltpu.VMEM((3, samples + padding, channels), F32)],
        input_output_aliases={6 + i: i for i in range(len(held))},
        compiler_params=PARAMS,
        cost_estimate=cost(8 * samples * channels * channels, 2**22),
    )(where, *inputs)


def term_kernel(replicas, offsets, micro, where, taps_t, skip, *refs):
    hids, refs = refs[:micro], refs[micro:]
    pgs, refs = refs[:micro], refs[micro:]
    gs, refs = refs[:micro], refs[micro:]
    outs = refs[-2 * len(offsets) :]
    samples, wide = pgs[0].shape
    channels = wide // 2
    part = channels // replicas
    places = [owner_row(where, replicas, part, offset) for offset in offsets]
    conv, mix_g, mix_s = None, None, None
    for m in range(micro):
        columns = slice(m * samples, (m + 1) * samples)
        lhs = jnp.concatenate([tap_rows(taps_t, row, part, columns) for row in places], axis=0)
        lhs_mix = jnp.concatenate([hids[m][pl.ds(row, part), :] for row in places], axis=0)
        new = [
            jnp.dot(lhs, pgs[m][...], preferred_element_type=F32),
            jnp.dot(lhs_mix, gs[m][...], preferred_element_type=F32),
            jnp.dot(lhs_mix, skip[m], preferred_element_type=F32),
        ]
        conv, mix_g, mix_s = new if m == 0 else (conv + new[0], mix_g + new[1], mix_s + new[2])
    for slot in range(len(offsets)):
        low, high = outs[2 * slot : 2 * slot + 2]
        at = slot * 3 * part
        for k, target in enumerate((low.at[0], low.at[1], high.at[0])):
            target[...] = conv[at + k * part : at + (k + 1) * part, :].astype(low.dtype)
        here = slice(slot * part, (slot + 1) * part)
        high[1, :, :channels] = mix_g[here, :].astype(low.dtype)
        high[1, :, channels:] = mix_s[here, :].astype(low.dtype)


def term_call(replicas, offsets, kind, where, taps_t, skip, hid_t, pre_grads, gs, tokens):
    micro, samples, channels = skip.shape
    part = channels // replicas
    inputs = in_vmem(taps_t, skip, *hid_t, *pre_grads, *gs, *tokens)
    outs = 2 * len(offsets)
    return pl.pallas_call(
        functools.partial(term_kernel, replicas, offsets, micro),
        out_shape=[pltpu.VMEM((2, part, 2 * channels), kind)] * outs,
        in_specs=[SMEM] + [VMEM] * len(inputs),
        out_specs=[VMEM] * outs,
        compiler_params=PARAMS,
        cost_estimate=cost(2**29 * len(offsets), 2**20),
    )(where, *inputs)


def add_kernel(mine_r, mine_l, got_r, got_l, *refs):
    out_r, out_l = refs[-2:]
    out_r[...] = (mine_r[...].astype(F32) + got_r[...].astype(F32)).astype(BF16)
    out_l[...] = (mine_l[...].astype(F32) + got_l[...].astype(F32)).astype(BF16)


def add_call(mine, got, tokens):
    inputs = in_vmem(*mine, *got, *tokens)
    return pl.pallas_call(
        add_kernel,
        out_shape=[pltpu.VMEM(got[0].shape, BF16)] * 2,
        in_specs=[VMEM] * len(inputs),
        out_specs=[VMEM] * 2,
        compiler_params=PARAMS,
        cost_estimate=cost(2**18, 2**19),
    )(*inputs)


def final_kernel(low, high, low_r, low_l, high_r, high_l, conv, mix):
    conv[0:2] = low[...] + (low_r[...].astype(F32) + low_l[...].astype(F32))
    total = high[...] + (high_r[...].astype(F32) + high_l[...].astype(F32))
    conv[2] = total[0]
    mix[...] = total[1]


def final_call(*blocks):
    part, wide = blocks[0].shape[1:]
    return pl.pallas_call(
        final_kernel,
        out_shape=[jax.ShapeDtypeStruct((3, part, wide), F32), jax.ShapeDtypeStruct((part, wide), F32)],
        in_specs=[VMEM] * 6,
        out_specs=[VMEM] * 2,
        compiler_params=PARAMS,
        cost_estimate=cost(2**19, 2**20),
    )(*in_vmem(*blocks))


def local(x_ckpt, top_cot, skip_cot, w_conv, w_mix):
    sections = lax.axis_size("pipe")
    replicas = lax.axis_size("dp")
    replica = lax.axis_index("dp")
    micro, seqs, samples, channels = x_ckpt.shape[1:]
    block = seqs * samples
    half = replicas // 2
    right, left = ring_pairs(replicas)
    place = jnp.where(replica % 2 == 0, replica // 2, replicas - 1 - replica // 2)
    where = jnp.stack([place, lax.axis_index("pipe")]).astype(jnp.int32)

    taps_t = prepare_call(where, x_ckpt[0].reshape(micro * seqs, samples, channels))
    conv = w_conv[0].transpose(1, 0, 2)
    conv_r, conv_l, mix_r, mix_l = conv, conv, w_mix, w_mix
    held = partial_call(replicas, (0,), where, taps_t, [conv], [w_mix], [])
    for step in range(1, half):
        conv_r = lax.ppermute(conv_r, "dp", right)
        conv_l = lax.ppermute(conv_l, "dp", left)
        mix_r = lax.ppermute(mix_r, "dp", right)
        mix_l = lax.ppermute(mix_l, "dp", left)
        held = partial_call(
            replicas, (-step, step), where, taps_t, [conv_r, conv_l], [mix_r, mix_l], held
        )
    acc, w_full = held
    conv_r = lax.ppermute(conv_r[:2], "dp", right)
    conv_l = lax.ppermute(conv_l[2:], "dp", left)
    mix_l = lax.ppermute(mix_l, "dp", left)

    skip = skip_cot.reshape(micro, block, channels)
    g = list(top_cot.reshape(micro, block, channels))
    padding = max(16, 2 * 2 ** (sections - 1))
    hid_t, held, ready = [], [()] * micro, []
    for m in range(micro):
        a1, a2, hid, *stored = forward_call(
            replicas, m, micro, m == 0, where, taps_t, conv_r, conv_l, mix_l, acc, w_full
        )
        if stored:
            w_full = stored[0]
        hid_t.append(hid)
        ready.append((a1, a2))
    for stage in range(sections - 1, -1, -1):
        for m in range(micro):
            held[m] = chain_call(stage, m, padding, where, g[m], skip, *ready[m], w_full, held[m])
            if stage:
                g[m] = lax.ppermute(held[m][1], "pipe", [(stage, stage - 1)])
    pre_grads, cots, gs = zip(*held)
    cot = jnp.stack(cots, axis=0)

    def terms(dist, tokens, kind=BF16):
        offsets = (dist,) if dist in (0, half) else (dist, -dist)
        return term_call(replicas, offsets, kind, where, taps_t, skip, hid_t, pre_grads, gs, tokens)

    def send(to_right, to_left):
        return lax.ppermute(to_right, "dp", right), lax.ppermute(to_left, "dp", left)

    low, high = terms(half, ())
    got_one = send(low, high)
    mine = terms(half - 1, (low,))
    got_two = send(mine[1], mine[2])
    token = ()
    for dist in range(half - 1, 0, -1):
        if dist < half - 1:
            out = add_call((mine[1], mine[2]), got_two, token)
            token = out[:1]
            got_two = send(*out)
        out = add_call((mine[0], mine[3]), got_one, token)
        token = out[:1]
        got_one = send(*out)
        if dist > 1:
            mine = terms(dist - 1, token)
    low, high = terms(0, token, F32)
    share_conv, share_mix = final_call(low, high, got_one[0], got_two[1], got_two[0], got_one[1])
    return (
        cot.reshape(1, micro, seqs, samples, channels),
        share_conv.transpose(1, 0, 2)[None],
        share_mix[None],
    )


def solution(mesh):
    placed = (
        P("pipe", None, "dp", None, None),
        P(None, "dp", None, None),
        P(None, "dp", None, None),
        P("pipe", "dp", None, None),
        P("pipe", "dp", None),
    )
    return jax.shard_map(
        local,
        mesh=mesh,
        in_specs=placed,
        out_specs=(
            P("pipe", None, "dp", None, None),
            P("pipe", "dp", None, None),
            P("pipe", "dp", None),
        ),
        check_vma=False,
    )
```

```python
import functools

import jax
import jax.numpy as jnp
from jax import lax
from jax.experimental import pallas as pl
from jax.experimental.pallas import tpu as pltpu
from jax.sharding import PartitionSpec as P

F32 = jnp.float32
BF16 = jnp.bfloat16
NT = (((1,), (1,)), ((), ()))
TN = (((0,), (0,)), ((), ()))
VMEM = pl.BlockSpec(memory_space=pltpu.VMEM)
PARAMS = pltpu.CompilerParams(vmem_limit_bytes=24 * 2**20)


def ring_pairs(count):
    order = list(range(0, count, 2)) + list(range(count - 1 - count % 2, 0, -2))
    right = [(order[i], order[(i + 1) % count]) for i in range(count)]
    return right, [(b, a) for a, b in right]


def in_vmem(*arrays):
    return [pltpu.with_memory_space_constraint(array, pltpu.VMEM) for array in arrays]


def cost(flops, moved):
    return pl.CostEstimate(flops=flops, bytes_accessed=moved, transcendentals=0)


def owner_row(replicas, part, offset):
    replica = lax.axis_index("dp")
    step = replica // 2
    place = jnp.where(lax.rem(replica, 2) == 0, step, replicas - 1 - step)
    at = lax.rem(place + (offset + replicas), replicas)
    owner = jnp.where(at < replicas // 2, 2 * at, 2 * (replicas - 1 - at) + 1)
    return pl.multiple_of(owner * part, part)


def prepare_kernel(x, taps_t):
    seqs, samples, channels = x.shape
    dilation = jnp.left_shift(jnp.int32(1), lax.axis_index("pipe"))
    wide = 128
    for s in range(seqs):
        columns = slice(s * samples, (s + 1) * samples)
        for at in range(0, channels, wide):
            turned = x[s, :, at : at + wide].astype(F32).T
            position = lax.broadcasted_iota(jnp.int32, turned.shape, 1)
            taps_t[at : at + wide, columns] = turned.astype(BF16)
            for k in (1, 2):
                delayed = jnp.where(position >= k * dilation, pltpu.roll(turned, k * dilation, 1), 0.0)
                taps_t[k * channels + at : k * channels + at + wide, columns] = delayed.astype(BF16)


def prepare_call(x):
    seqs, samples, channels = x.shape
    return pl.pallas_call(
        prepare_kernel,
        out_shape=pltpu.VMEM((3 * channels, seqs * samples), BF16),
        in_specs=[VMEM],
        out_specs=VMEM,
        compiler_params=PARAMS,
        cost_estimate=cost(2**20, 2**22),
    )(x)


def tap_rows(taps_t, row, part, columns, first=0, last=3):
    channels = taps_t.shape[0] // 3
    return jnp.concatenate(
        [taps_t[pl.ds(k * channels + row, part), columns] for k in range(first, last)], axis=0
    )


def partial_kernel(replicas, offsets, taps_t, *refs):
    count = len(offsets)
    convs, mixes, refs = refs[:count], refs[count : 2 * count], refs[2 * count :]
    first = len(refs) == 2
    acc, w = refs[:2] if first else refs[2:4]
    rows = taps_t.shape[1]
    channels = w.shape[0] // 4
    part = convs[0].shape[1]
    chunk = min(256, rows)
    places = [owner_row(replicas, part, offset) for offset in offsets]
    for at in range(0, rows, chunk):
        columns = slice(at, at + chunk)
        total = None if first else refs[0][columns, :]
        for row, conv in zip(places, convs):
            term = lax.dot_general(
                tap_rows(taps_t, row, part, columns),
                conv[...].reshape(3 * part, -1),
                TN,
                preferred_element_type=F32,
            )
            total = term if total is None else total + term
        acc[columns, :] = total
    for row, conv, mix in zip(places, convs, mixes):
        for k in range(3):
            w[pl.ds(k * channels + row, part), :] = conv[k]
        w[pl.ds(3 * channels + row, part), :] = mix[0]


def partial_call(replicas, offsets, taps_t, convs, mixes, held):
    part, wide = convs[0].shape[1:]
    rows = taps_t.shape[1]
    count = len(offsets)
    inputs = in_vmem(taps_t, *convs, *mixes, *held)
    return pl.pallas_call(
        functools.partial(partial_kernel, replicas, offsets),
        out_shape=[pltpu.VMEM((rows, wide), F32), pltpu.VMEM((2 * wide, wide), BF16)]
        + [pltpu.VMEM(mix.shape, BF16) for mix in mixes if held],
        in_specs=[VMEM] * len(inputs),
        out_specs=[VMEM] * (2 + count if held else 2),
        input_output_aliases={1 + 2 * count: 0, 2 + 2 * count: 1, **{1 + count + i: 2 + i for i in range(count)}}
        if held
        else {},
        compiler_params=PARAMS,
        cost_estimate=cost(6 * rows * part * count * wide, 2**20),
    )(*inputs)


def forward_kernel(replicas, index, store, taps_t, conv_a, conv_b, mix, acc, w_in, *refs):
    a1, a2, hid_t = refs[:3]
    samples, channels = a1.shape
    part = mix.shape[1]
    row = owner_row(replicas, part, replicas // 2)
    ahead = conv_a.shape[0]
    chunk = min(256, samples)
    for at in range(0, samples, chunk):
        columns = slice(index * samples + at, index * samples + at + chunk)
        pre = acc[columns, :]
        for conv, first, last in ((conv_a, 0, ahead), (conv_b, ahead, 3)):
            pre = pre + lax.dot_general(
                tap_rows(taps_t, row, part, columns, first, last),
                conv[...].reshape((last - first) * part, -1),
                TN,
                preferred_element_type=F32,
            )
        filt = jnp.tanh(pre[:, :channels])
        gate = jax.nn.sigmoid(pre[:, channels:])
        a1[at : at + chunk, :] = (gate * (1.0 - filt * filt)).astype(BF16)
        a2[at : at + chunk, :] = (filt * gate * (1.0 - gate)).astype(BF16)
        hid_t[:, at : at + chunk] = (filt * gate).T.astype(BF16)
    if store:
        w = refs[3]
        blocks = [conv_a[k] for k in range(ahead)] + [conv_b[k] for k in range(3 - ahead)] + [mix[0]]
        for k, block in enumerate(blocks):
            w[pl.ds(k * channels + row, part), :] = block


def forward_call(replicas, index, micro, store, taps_t, conv_a, conv_b, mix, acc, w):
    rows, wide = acc.shape
    channels = wide // 2
    samples = rows // micro
    inputs = in_vmem(taps_t, conv_a, conv_b, mix, acc, w)
    return pl.pallas_call(
        functools.partial(forward_kernel, replicas, index, store),
        out_shape=[pltpu.VMEM((samples, channels), BF16)] * 2
        + [pltpu.VMEM((channels, samples), BF16)]
        + ([pltpu.VMEM(w.shape, BF16)] if store else []),
        in_specs=[VMEM] * 6,
        out_specs=[VMEM] * (4 if store else 3),
        input_output_aliases={5: 3} if store else {},
        compiler_params=PARAMS,
        cost_estimate=cost(2**28, 2**22),
    )(*inputs)


def chain_kernel(stage, index, g_low, g_high, skip, a1, a2, w, *refs):
    pg, ig_low, ig_high, gk, bt = refs[-5:]
    samples, channels = gk.shape
    chunk = samples // 2
    padding = bt.shape[1] - samples
    dilation = 2**stage

    @pl.when(lax.axis_index("pipe") == stage)
    def _():
        for k in (1, 2):
            bt[k, samples:, :] = jnp.zeros((padding, channels), F32)
        for at, g, ig in ((chunk, g_high, ig_high), (0, g_low, ig_low)):
            rows = slice(at, at + chunk)
            hid = lax.dot_general(
                g[...], w[3 * channels :, :channels], NT, preferred_element_type=F32
            ) + lax.dot_general(
                skip[index, rows, :], w[3 * channels :, channels:], NT, preferred_element_type=F32
            )
            pg[rows, :channels] = (hid * a1[rows, :].astype(F32)).astype(BF16)
            pg[rows, channels:] = (hid * a2[rows, :].astype(F32)).astype(BF16)
            for k in range(3):
                bt[k, rows, :] = lax.dot_general(
                    pg[rows, :], w[k * channels : (k + 1) * channels, :], NT, preferred_element_type=F32
                )
            piece = 64
            for first in range(at + chunk - piece, at - 1, -piece):
                last = first + piece
                here = slice(first - at, last - at)
                total = g[here, :].astype(F32) + bt[0, first:last, :]
                total = total + bt[1, first + dilation : last + dilation, :]
                total = total + bt[2, first + 2 * dilation : last + 2 * dilation, :]
                ig[here, :] = total.astype(BF16)
            gk[rows, :] = g[...]


def chain_call(stage, index, padding, g, skip, a1, a2, w, held):
    samples, channels = a1.shape
    half = pltpu.VMEM((samples // 2, channels), BF16)
    inputs = in_vmem(*g, skip, a1, a2, w, *held)
    return pl.pallas_call(
        functools.partial(chain_kernel, stage, index),
        out_shape=[pltpu.VMEM((samples, 2 * channels), BF16), half, half, pltpu.VMEM((samples, channels), BF16)],
        in_specs=[VMEM] * len(inputs),
        out_specs=[VMEM] * 4,
        scratch_shapes=[pltpu.VMEM((3, samples + padding, channels), F32)],
        input_output_aliases={6 + i: i for i in range(len(held))},
        compiler_params=PARAMS,
        cost_estimate=cost(8 * samples * channels * channels, 2**22),
    )(*inputs)


def term_kernel(replicas, offsets, micro, taps_t, skip, *refs):
    hids, refs = refs[:micro], refs[micro:]
    pgs, refs = refs[:micro], refs[micro:]
    gs, refs = refs[:micro], refs[micro:]
    outs = refs[-2 * len(offsets) :]
    samples, wide = pgs[0].shape
    channels = wide // 2
    part = channels // replicas
    places = [owner_row(replicas, part, offset) for offset in offsets]
    conv, mix_g, mix_s = None, None, None
    for m in range(micro):
        columns = slice(m * samples, (m + 1) * samples)
        lhs = jnp.concatenate([tap_rows(taps_t, row, part, columns) for row in places], axis=0)
        lhs_mix = jnp.concatenate([hids[m][pl.ds(row, part), :] for row in places], axis=0)
        new = [
            jnp.dot(lhs, pgs[m][...], preferred_element_type=F32),
            jnp.dot(lhs_mix, gs[m][...], preferred_element_type=F32),
            jnp.dot(lhs_mix, skip[m], preferred_element_type=F32),
        ]
        conv, mix_g, mix_s = new if m == 0 else (conv + new[0], mix_g + new[1], mix_s + new[2])
    for slot in range(len(offsets)):
        low, high = outs[2 * slot : 2 * slot + 2]
        at = slot * 3 * part
        for k, target in enumerate((low.at[0], low.at[1], high.at[0])):
            target[...] = conv[at + k * part : at + (k + 1) * part, :].astype(low.dtype)
        here = slice(slot * part, (slot + 1) * part)
        high[1, :, :channels] = mix_g[here, :].astype(low.dtype)
        high[1, :, channels:] = mix_s[here, :].astype(low.dtype)


def term_call(replicas, offsets, kind, taps_t, skip, hid_t, pre_grads, gs, tokens):
    micro, samples, channels = skip.shape
    part = channels // replicas
    inputs = in_vmem(taps_t, skip, *hid_t, *pre_grads, *gs, *tokens)
    outs = 2 * len(offsets)
    return pl.pallas_call(
        functools.partial(term_kernel, replicas, offsets, micro),
        out_shape=[pltpu.VMEM((2, part, 2 * channels), kind)] * outs,
        in_specs=[VMEM] * len(inputs),
        out_specs=[VMEM] * outs,
        compiler_params=PARAMS,
        cost_estimate=cost(2**29 * len(offsets), 2**20),
    )(*inputs)


def add_kernel(mine_r, mine_l, got_r, got_l, *refs):
    out_r, out_l = refs[-2:]
    out_r[...] = (mine_r[...].astype(F32) + got_r[...].astype(F32)).astype(BF16)
    out_l[...] = (mine_l[...].astype(F32) + got_l[...].astype(F32)).astype(BF16)


def add_call(mine, got, tokens):
    inputs = in_vmem(*mine, *got, *tokens)
    return pl.pallas_call(
        add_kernel,
        out_shape=[pltpu.VMEM(got[0].shape, BF16)] * 2,
        in_specs=[VMEM] * len(inputs),
        out_specs=[VMEM] * 2,
        compiler_params=PARAMS,
        cost_estimate=cost(2**18, 2**19),
    )(*inputs)


def final_kernel(low, high, low_r, low_l, high_r, high_l, conv, mix):
    conv[0:2] = low[...] + (low_r[...].astype(F32) + low_l[...].astype(F32))
    total = high[...] + (high_r[...].astype(F32) + high_l[...].astype(F32))
    conv[2] = total[0]
    mix[...] = total[1]


def final_call(*blocks):
    part, wide = blocks[0].shape[1:]
    return pl.pallas_call(
        final_kernel,
        out_shape=[jax.ShapeDtypeStruct((3, part, wide), F32), jax.ShapeDtypeStruct((part, wide), F32)],
        in_specs=[VMEM] * 6,
        out_specs=[VMEM] * 2,
        compiler_params=PARAMS,
        cost_estimate=cost(2**19, 2**20),
    )(*in_vmem(*blocks))


def local(x_ckpt, top_cot, skip_cot, w_conv, w_mix):
    sections = lax.axis_size("pipe")
    replicas = lax.axis_size("dp")
    micro, seqs, samples, channels = x_ckpt.shape[1:]
    block = seqs * samples
    half = replicas // 2
    right, left = ring_pairs(replicas)

    taps_t = prepare_call(x_ckpt[0].reshape(micro * seqs, samples, channels))
    conv = w_conv[0].transpose(1, 0, 2)
    conv_r, conv_l, mix_r, mix_l = conv, conv, w_mix, w_mix
    held = partial_call(replicas, (0,), taps_t, [conv], [w_mix], [])
    for step in range(1, half):
        conv_r = lax.ppermute(conv_r, "dp", right)
        conv_l = lax.ppermute(conv_l, "dp", left)
        mix_r = lax.ppermute(mix_r, "dp", right)
        mix_l = lax.ppermute(mix_l, "dp", left)
        *held, mix_r, mix_l = partial_call(
            replicas, (-step, step), taps_t, [conv_r, conv_l], [mix_r, mix_l], held
        )
    acc, w_full = held
    conv_r = lax.ppermute(conv_r[:2], "dp", right)
    conv_l = lax.ppermute(conv_l[2:], "dp", left)
    mix_l = lax.ppermute(mix_l, "dp", left)

    skip = skip_cot.reshape(micro, block, channels)
    top = top_cot.reshape(micro, 2, block // 2, channels)
    g = [(top[m, 0], top[m, 1]) for m in range(micro)]
    padding = max(16, 2 * 2 ** (sections - 1))
    hid_t, held, ready = [], [()] * micro, []
    for m in range(micro):
        a1, a2, hid, *stored = forward_call(
            replicas, m, micro, m == 0, taps_t, conv_r, conv_l, mix_l, acc, w_full
        )
        if stored:
            w_full = stored[0]
        hid_t.append(hid)
        ready.append((a1, a2))
    for stage in range(sections - 1, -1, -1):
        for m in range(micro):
            held[m] = chain_call(stage, m, padding, g[m], skip, *ready[m], w_full, held[m])
            if stage:
                hop = [(stage, stage - 1)]
                g[m] = [lax.ppermute(piece, "pipe", hop) for piece in held[m][1:3]]
    pre_grads, lows, highs, gs = zip(*held)
    cot = jnp.concatenate([piece for pieces in zip(lows, highs) for piece in pieces], axis=0)

    def terms(dist, tokens, kind=BF16):
        offsets = (dist,) if dist in (0, half) else (dist, -dist)
        return term_call(replicas, offsets, kind, taps_t, skip, hid_t, pre_grads, gs, tokens)

    def send(to_right, to_left):
        return lax.ppermute(to_right, "dp", right), lax.ppermute(to_left, "dp", left)

    low, high = terms(half, ())
    got_one = send(low, high)
    mine = terms(half - 1, (low,))
    got_two = send(mine[1], mine[2])
    token = ()
    for dist in range(half - 1, 0, -1):
        if dist < half - 1:
            out = add_call((mine[1], mine[2]), got_two, token)
            token = out[:1]
            got_two = send(*out)
        out = add_call((mine[0], mine[3]), got_one, token)
        token = out[:1]
        got_one = send(*out)
        if dist > 1:
            mine = terms(dist - 1, token)
    low, high = terms(0, token, F32)
    share_conv, share_mix = final_call(low, high, got_one[0], got_two[1], got_two[0], got_one[1])
    return (
        cot.reshape(1, micro, seqs, samples, channels),
        share_conv.transpose(1, 0, 2)[None],
        share_mix[None],
    )


def solution(mesh):
    placed = (
        P("pipe", None, "dp", None, None),
        P(None, "dp", None, None),
        P(None, "dp", None, None),
        P("pipe", "dp", None, None),
        P("pipe", "dp", None),
    )
    return jax.shard_map(
        local,
        mesh=mesh,
        in_specs=placed,
        out_specs=(
            P("pipe", None, "dp", None, None),
            P("pipe", "dp", None, None),
            P("pipe", "dp", None),
        ),
        check_vma=False,
    )
```

```python
import functools

import jax
import jax.numpy as jnp
from jax import lax
from jax.experimental import pallas as pl
from jax.experimental.pallas import tpu as pltpu
from jax.sharding import PartitionSpec as P

F32 = jnp.float32
BF16 = jnp.bfloat16
NT = (((1,), (1,)), ((), ()))
TN = (((0,), (0,)), ((), ()))
VMEM = pl.BlockSpec(memory_space=pltpu.VMEM)
PARAMS = pltpu.CompilerParams(vmem_limit_bytes=24 * 2**20)


def ring_pairs(count):
    order = list(range(0, count, 2)) + list(range(count - 1 - count % 2, 0, -2))
    right = [(order[i], order[(i + 1) % count]) for i in range(count)]
    return right, [(b, a) for a, b in right]


def in_vmem(*arrays):
    return [pltpu.with_memory_space_constraint(array, pltpu.VMEM) for array in arrays]


def cost(flops, moved):
    return pl.CostEstimate(flops=flops, bytes_accessed=moved, transcendentals=0)


def owner_row(replicas, part, offset):
    replica = lax.axis_index("dp")
    step = replica // 2
    place = jnp.where(lax.rem(replica, 2) == 0, step, replicas - 1 - step)
    at = lax.rem(place + (offset + replicas), replicas)
    owner = jnp.where(at < replicas // 2, 2 * at, 2 * (replicas - 1 - at) + 1)
    return pl.multiple_of(owner * part, part)


def prepare_kernel(x, taps_t):
    seqs, samples, channels = x.shape
    dilation = jnp.left_shift(jnp.int32(1), lax.axis_index("pipe"))
    wide = 128
    for s in range(seqs):
        columns = slice(s * samples, (s + 1) * samples)
        for at in range(0, channels, wide):
            turned = x[s, :, at : at + wide].astype(F32).T
            position = lax.broadcasted_iota(jnp.int32, turned.shape, 1)
            taps_t[at : at + wide, columns] = turned.astype(BF16)
            for k in (1, 2):
                delayed = jnp.where(position >= k * dilation, pltpu.roll(turned, k * dilation, 1), 0.0)
                taps_t[k * channels + at : k * channels + at + wide, columns] = delayed.astype(BF16)


def prepare_call(x):
    seqs, samples, channels = x.shape
    return pl.pallas_call(
        prepare_kernel,
        out_shape=pltpu.VMEM((3 * channels, seqs * samples), BF16),
        in_specs=[VMEM],
        out_specs=VMEM,
        compiler_params=PARAMS,
        cost_estimate=cost(2**20, 2**22),
    )(x)


def tap_rows(taps_t, row, part, columns):
    channels = taps_t.shape[0] // 3
    return jnp.concatenate([taps_t[pl.ds(k * channels + row, part), columns] for k in range(3)], axis=0)


def place_rows(replicas, items, blocks):
    part = blocks[0].shape[1]
    return [(owner_row(replicas, part, offset), first, block) for (offset, first), block in zip(items, blocks)]


def shard_term(taps_t, columns, placed):
    channels = taps_t.shape[0] // 3
    part, wide = placed[0][2].shape[1:]
    rows, weights = [], []
    for row, first, block in placed:
        count = min(2, 3 - first)
        rows += [taps_t[pl.ds((first + k) * channels + row, part), columns] for k in range(count)]
        weights.append(block[:count].reshape(count * part, wide))
    return lax.dot_general(
        jnp.concatenate(rows, axis=0), jnp.concatenate(weights, axis=0), TN, preferred_element_type=F32
    )


def store_shards(w, placed):
    channels = w.shape[0] // 4
    for row, first, block in placed:
        for k in range(2):
            w[pl.ds((first + k) * channels + row, block.shape[1]), :] = block[k]


def partial_kernel(replicas, items, first, taps_t, *refs):
    count = len(items)
    placed = place_rows(replicas, items, refs[:count])
    refs = refs[count:]
    acc, w = refs[:2] if first else refs[2:4]
    rows = taps_t.shape[1]
    chunk = min(256, rows)
    for at in range(0, rows, chunk):
        columns = slice(at, at + chunk)
        term = shard_term(taps_t, columns, placed)
        acc[columns, :] = term if first else refs[0][columns, :] + term
    store_shards(w, placed)


def partial_call(replicas, items, taps_t, blocks, held):
    part, wide = blocks[0].shape[1:]
    rows = taps_t.shape[1]
    count = len(items)
    inputs = in_vmem(taps_t, *blocks, *held)
    aliases = {1 + count + i: i for i in range(len(held))}
    if held:
        aliases |= {1 + i: 2 + i for i in range(count)}
    return pl.pallas_call(
        functools.partial(partial_kernel, replicas, items, not held),
        out_shape=[pltpu.VMEM((rows, wide), F32), pltpu.VMEM((2 * wide, wide), BF16)]
        + [pltpu.VMEM(block.shape, BF16) for block in blocks if held],
        in_specs=[VMEM] * len(inputs),
        out_specs=[VMEM] * (2 + count if held else 2),
        input_output_aliases=aliases,
        compiler_params=PARAMS,
        cost_estimate=cost(3 * rows * part * count * wide, 2**20),
    )(*inputs)


def forward_kernel(replicas, index, store, taps_t, low, high, acc, w_in, *refs):
    a1, a2, hid_t = refs[:3]
    samples, channels = a1.shape
    placed = place_rows(replicas, ((replicas // 2, 0), (replicas // 2, 2)), (low, high))
    chunk = min(256, samples)
    for at in range(0, samples, chunk):
        columns = slice(index * samples + at, index * samples + at + chunk)
        pre = acc[columns, :] + shard_term(taps_t, columns, placed)
        filt = jnp.tanh(pre[:, :channels])
        gate = jax.nn.sigmoid(pre[:, channels:])
        a1[at : at + chunk, :] = (gate * (1.0 - filt * filt)).astype(BF16)
        a2[at : at + chunk, :] = (filt * gate * (1.0 - gate)).astype(BF16)
        hid_t[:, at : at + chunk] = (filt * gate).T.astype(BF16)
    if store:
        store_shards(refs[3], placed)


def forward_call(replicas, index, micro, store, taps_t, low, high, acc, w):
    rows, wide = acc.shape
    channels = wide // 2
    samples = rows // micro
    inputs = in_vmem(taps_t, low, high, acc, w)
    return pl.pallas_call(
        functools.partial(forward_kernel, replicas, index, store),
        out_shape=[pltpu.VMEM((samples, channels), BF16)] * 2
        + [pltpu.VMEM((channels, samples), BF16)]
        + ([pltpu.VMEM(w.shape, BF16)] if store else []),
        in_specs=[VMEM] * 5,
        out_specs=[VMEM] * (4 if store else 3),
        input_output_aliases={4: 3} if store else {},
        compiler_params=PARAMS,
        cost_estimate=cost(2**28, 2**22),
    )(*inputs)


def chain_kernel(stage, index, g, skip, a1, a2, w, *refs):
    pg, ig, gk, bt = refs[-4:]
    samples, channels = gk.shape
    chunk = samples // 2
    padding = bt.shape[1] - samples
    dilation = 2**stage

    @pl.when(lax.axis_index("pipe") == stage)
    def _():
        for k in (1, 2):
            bt[k, samples:, :] = jnp.zeros((padding, channels), F32)
        for at in (chunk, 0):
            rows = slice(at, at + chunk)
            hid = lax.dot_general(
                g[rows, :], w[3 * channels :, :channels], NT, preferred_element_type=F32
            ) + lax.dot_general(
                skip[index, rows, :], w[3 * channels :, channels:], NT, preferred_element_type=F32
            )
            pg[rows, :channels] = (hid * a1[rows, :].astype(F32)).astype(BF16)
            pg[rows, channels:] = (hid * a2[rows, :].astype(F32)).astype(BF16)
            for k in range(3):
                bt[k, rows, :] = lax.dot_general(
                    pg[rows, :], w[k * channels : (k + 1) * channels, :], NT, preferred_element_type=F32
                )
            piece = 64
            for first in range(at + chunk - piece, at - 1, -piece):
                last = first + piece
                total = g[first:last, :].astype(F32) + bt[0, first:last, :]
                total = total + bt[1, first + dilation : last + dilation, :]
                total = total + bt[2, first + 2 * dilation : last + 2 * dilation, :]
                ig[first:last, :] = total.astype(BF16)
            gk[rows, :] = g[rows, :]


def chain_call(stage, index, padding, g, skip, a1, a2, w, held):
    samples, channels = a1.shape
    tile = pltpu.VMEM((samples, channels), BF16)
    inputs = in_vmem(g, skip, a1, a2, w, *held)
    return pl.pallas_call(
        functools.partial(chain_kernel, stage, index),
        out_shape=[pltpu.VMEM((samples, 2 * channels), BF16), tile, tile],
        in_specs=[VMEM] * len(inputs),
        out_specs=[VMEM] * 3,
        scratch_shapes=[pltpu.VMEM((3, samples + padding, channels), F32)],
        input_output_aliases={5 + i: i for i in range(len(held))},
        compiler_params=PARAMS,
        cost_estimate=cost(8 * samples * channels * channels, 2**22),
    )(*inputs)


def term_kernel(replicas, offsets, micro, taps_t, skip, *refs):
    hids, refs = refs[:micro], refs[micro:]
    pgs, refs = refs[:micro], refs[micro:]
    gs, refs = refs[:micro], refs[micro:]
    outs = refs[-2 * len(offsets) :]
    samples, wide = pgs[0].shape
    channels = wide // 2
    part = channels // replicas
    places = [owner_row(replicas, part, offset) for offset in offsets]
    conv, mix_g, mix_s = None, None, None
    for m in range(micro):
        columns = slice(m * samples, (m + 1) * samples)
        lhs = jnp.concatenate([tap_rows(taps_t, row, part, columns) for row in places], axis=0)
        lhs_mix = jnp.concatenate([hids[m][pl.ds(row, part), :] for row in places], axis=0)
        new = [
            jnp.dot(lhs, pgs[m][...], preferred_element_type=F32),
            jnp.dot(lhs_mix, gs[m][...], preferred_element_type=F32),
            jnp.dot(lhs_mix, skip[m], preferred_element_type=F32),
        ]
        conv, mix_g, mix_s = new if m == 0 else (conv + new[0], mix_g + new[1], mix_s + new[2])
    for slot in range(len(offsets)):
        low, high = outs[2 * slot : 2 * slot + 2]
        at = slot * 3 * part
        for k, target in enumerate((low.at[0], low.at[1], high.at[0])):
            target[...] = conv[at + k * part : at + (k + 1) * part, :].astype(low.dtype)
        here = slice(slot * part, (slot + 1) * part)
        high[1, :, :channels] = mix_g[here, :].astype(low.dtype)
        high[1, :, channels:] = mix_s[here, :].astype(low.dtype)


def term_call(replicas, offsets, kind, taps_t, skip, hid_t, pre_grads, gs, tokens):
    micro, samples, channels = skip.shape
    part = channels // replicas
    inputs = in_vmem(taps_t, skip, *hid_t, *pre_grads, *gs, *tokens)
    outs = 2 * len(offsets)
    return pl.pallas_call(
        functools.partial(term_kernel, replicas, offsets, micro),
        out_shape=[pltpu.VMEM((2, part, 2 * channels), kind)] * outs,
        in_specs=[VMEM] * len(inputs),
        out_specs=[VMEM] * outs,
        compiler_params=PARAMS,
        cost_estimate=cost(2**29 * len(offsets), 2**20),
    )(*inputs)


def add_kernel(mine_r, mine_l, got_r, got_l, *refs):
    out_r, out_l = refs[-2:]
    out_r[...] = (mine_r[...].astype(F32) + got_r[...].astype(F32)).astype(BF16)
    out_l[...] = (mine_l[...].astype(F32) + got_l[...].astype(F32)).astype(BF16)


def add_call(mine, got, tokens):
    inputs = in_vmem(*mine, *got, *tokens)
    return pl.pallas_call(
        add_kernel,
        out_shape=[pltpu.VMEM(got[0].shape, BF16)] * 2,
        in_specs=[VMEM] * len(inputs),
        out_specs=[VMEM] * 2,
        compiler_params=PARAMS,
        cost_estimate=cost(2**18, 2**19),
    )(*inputs)


def final_kernel(low, high, low_r, low_l, high_r, high_l, conv, mix):
    conv[0:2] = low[...] + (low_r[...].astype(F32) + low_l[...].astype(F32))
    total = high[...] + (high_r[...].astype(F32) + high_l[...].astype(F32))
    conv[2] = total[0]
    mix[...] = total[1]


def final_call(*blocks):
    part, wide = blocks[0].shape[1:]
    return pl.pallas_call(
        final_kernel,
        out_shape=[jax.ShapeDtypeStruct((3, part, wide), F32), jax.ShapeDtypeStruct((part, wide), F32)],
        in_specs=[VMEM] * 6,
        out_specs=[VMEM] * 2,
        compiler_params=PARAMS,
        cost_estimate=cost(2**19, 2**20),
    )(*in_vmem(*blocks))


def local(x_ckpt, top_cot, skip_cot, w_conv, w_mix):
    sections = lax.axis_size("pipe")
    replicas = lax.axis_size("dp")
    micro, seqs, samples, channels = x_ckpt.shape[1:]
    block = seqs * samples
    half = replicas // 2
    right, left = ring_pairs(replicas)

    def send(to_right, to_left):
        return lax.ppermute(to_right, "dp", right), lax.ppermute(to_left, "dp", left)

    taps_t = prepare_call(x_ckpt[0].reshape(micro * seqs, samples, channels))
    conv = w_conv[0].transpose(1, 0, 2)
    low = conv[:2]
    high = jnp.concatenate([conv[2:], w_mix], axis=0)
    streams = {0: (low, low), 2: (high, high)}
    held = partial_call(replicas, ((0, 0), (0, 2)), taps_t, [low, high], [])
    for step in range(1, half):
        for first, (to_right, to_left) in streams.items():
            got = send(to_right, to_left)
            items = ((-step, first), (step, first))
            *held, to_right, to_left = partial_call(replicas, items, taps_t, got, held)
            streams[first] = (to_right, to_left)
    acc, w_full = held
    low = lax.ppermute(streams[0][0], "dp", right)
    high = lax.ppermute(streams[2][1], "dp", left)

    skip = skip_cot.reshape(micro, block, channels)
    g = list(top_cot.reshape(micro, block, channels))
    padding = max(16, 2 * 2 ** (sections - 1))
    hid_t, held, ready = [], [()] * micro, []
    for m in range(micro):
        a1, a2, hid, *stored = forward_call(
            replicas, m, micro, m == 0, taps_t, low, high, acc, w_full
        )
        if stored:
            w_full = stored[0]
        hid_t.append(hid)
        ready.append((a1, a2))
    for stage in range(sections - 1, -1, -1):
        for m in range(micro):
            held[m] = chain_call(stage, m, padding, g[m], skip, *ready[m], w_full, held[m])
            if stage:
                g[m] = lax.ppermute(held[m][1], "pipe", [(stage, stage - 1)])
    pre_grads, cots, gs = zip(*held)
    cot = jnp.stack(cots, axis=0)

    def terms(dist, tokens, kind=BF16):
        offsets = (dist,) if dist in (0, half) else (dist, -dist)
        return term_call(replicas, offsets, kind, taps_t, skip, hid_t, pre_grads, gs, tokens)

    low, high = terms(half, ())
    got_one = send(low, high)
    mine = terms(half - 1, (low,))
    got_two = send(mine[1], mine[2])
    token = ()
    for dist in range(half - 1, 0, -1):
        if dist < half - 1:
            out = add_call((mine[1], mine[2]), got_two, token)
            token = out[:1]
            got_two = send(*out)
        out = add_call((mine[0], mine[3]), got_one, token)
        token = out[:1]
        got_one = send(*out)
        if dist > 1:
            mine = terms(dist - 1, token)
    low, high = terms(0, token, F32)
    share_conv, share_mix = final_call(low, high, got_one[0], got_two[1], got_two[0], got_one[1])
    return (
        cot.reshape(1, micro, seqs, samples, channels),
        share_conv.transpose(1, 0, 2)[None],
        share_mix[None],
    )


def solution(mesh):
    placed = (
        P("pipe", None, "dp", None, None),
        P(None, "dp", None, None),
        P(None, "dp", None, None),
        P("pipe", "dp", None, None),
        P("pipe", "dp", None),
    )
    return jax.shard_map(
        local,
        mesh=mesh,
        in_specs=placed,
        out_specs=(
            P("pipe", None, "dp", None, None),
            P("pipe", "dp", None, None),
            P("pipe", "dp", None),
        ),
        check_vma=False,
    )
```

```python
import functools

import jax
import jax.numpy as jnp
from jax import lax
from jax.experimental import pallas as pl
from jax.experimental.pallas import tpu as pltpu
from jax.sharding import PartitionSpec as P

F32 = jnp.float32
BF16 = jnp.bfloat16
NT = (((1,), (1,)), ((), ()))
TN = (((0,), (0,)), ((), ()))
VMEM = pl.BlockSpec(memory_space=pltpu.VMEM)
PARAMS = pltpu.CompilerParams(vmem_limit_bytes=24 * 2**20)


def ring_pairs(count):
    order = list(range(0, count, 2)) + list(range(count - 1 - count % 2, 0, -2))
    right = [(order[i], order[(i + 1) % count]) for i in range(count)]
    return right, [(b, a) for a, b in right]


def in_vmem(*arrays):
    return [pltpu.with_memory_space_constraint(array, pltpu.VMEM) for array in arrays]


def cost(flops, moved):
    return pl.CostEstimate(flops=flops, bytes_accessed=moved, transcendentals=0)


def owner_row(replicas, part, offset):
    replica = lax.axis_index("dp")
    step = replica // 2
    place = jnp.where(lax.rem(replica, 2) == 0, step, replicas - 1 - step)
    at = lax.rem(place + (offset + replicas), replicas)
    owner = jnp.where(at < replicas // 2, 2 * at, 2 * (replicas - 1 - at) + 1)
    return pl.multiple_of(owner * part, part)


def split_kernel(conv, mix, low, high, sems):
    copies = [
        pltpu.make_async_copy(conv.at[0:2], low, sems.at[0]),
        pltpu.make_async_copy(conv.at[2], high.at[0], sems.at[1]),
        pltpu.make_async_copy(mix.at[0], high.at[1], sems.at[2]),
    ]
    for copy in copies:
        copy.start()
    for copy in copies:
        copy.wait()


def split_call(conv, mix):
    anywhere = pl.BlockSpec(memory_space=pl.ANY)
    return pl.pallas_call(
        split_kernel,
        out_shape=[pltpu.VMEM((2, *conv.shape[1:]), BF16)] * 2,
        in_specs=[anywhere] * 2,
        out_specs=[VMEM] * 2,
        scratch_shapes=[pltpu.SemaphoreType.DMA((3,))],
        compiler_params=PARAMS,
        cost_estimate=cost(0, 2**20),
    )(*[pltpu.with_memory_space_constraint(array, pltpu.HBM) for array in (conv, mix)])


def prepare_kernel(x, taps_t):
    seqs, samples, channels = x.shape
    dilation = jnp.left_shift(jnp.int32(1), lax.axis_index("pipe"))
    wide = 128
    for s in range(seqs):
        columns = slice(s * samples, (s + 1) * samples)
        for at in range(0, channels, wide):
            turned = x[s, :, at : at + wide].astype(F32).T
            position = lax.broadcasted_iota(jnp.int32, turned.shape, 1)
            taps_t[at : at + wide, columns] = turned.astype(BF16)
            for k in (1, 2):
                delayed = jnp.where(position >= k * dilation, pltpu.roll(turned, k * dilation, 1), 0.0)
                taps_t[k * channels + at : k * channels + at + wide, columns] = delayed.astype(BF16)


def prepare_call(x):
    seqs, samples, channels = x.shape
    return pl.pallas_call(
        prepare_kernel,
        out_shape=pltpu.VMEM((3 * channels, seqs * samples), BF16),
        in_specs=[VMEM],
        out_specs=VMEM,
        compiler_params=PARAMS,
        cost_estimate=cost(2**20, 2**22),
    )(x)


def tap_rows(taps_t, row, part, columns):
    channels = taps_t.shape[0] // 3
    return jnp.concatenate([taps_t[pl.ds(k * channels + row, part), columns] for k in range(3)], axis=0)


def place_rows(replicas, items, blocks):
    part = blocks[0].shape[1]
    return [(owner_row(replicas, part, offset), first, block) for (offset, first), block in zip(items, blocks)]


def shard_term(taps_t, columns, placed):
    channels = taps_t.shape[0] // 3
    part, wide = placed[0][2].shape[1:]
    rows, weights = [], []
    for row, first, block in placed:
        count = min(2, 3 - first)
        rows += [taps_t[pl.ds((first + k) * channels + row, part), columns] for k in range(count)]
        weights.append(block[:count].reshape(count * part, wide))
    return lax.dot_general(
        jnp.concatenate(rows, axis=0), jnp.concatenate(weights, axis=0), TN, preferred_element_type=F32
    )


def store_shards(w, placed):
    channels = w.shape[0] // 4
    for row, first, block in placed:
        for k in range(2):
            w[pl.ds((first + k) * channels + row, block.shape[1]), :] = block[k]


def partial_kernel(replicas, items, first, taps_t, *refs):
    count = len(items)
    placed = place_rows(replicas, items, refs[:count])
    refs = refs[count:]
    acc, w = refs[:2] if first else refs[2:4]
    rows = taps_t.shape[1]
    chunk = min(256, rows)
    for at in range(0, rows, chunk):
        columns = slice(at, at + chunk)
        term = shard_term(taps_t, columns, placed)
        acc[columns, :] = term if first else refs[0][columns, :] + term
    store_shards(w, placed)


def partial_call(replicas, items, taps_t, blocks, held):
    part, wide = blocks[0].shape[1:]
    rows = taps_t.shape[1]
    count = len(items)
    inputs = in_vmem(taps_t, *blocks, *held)
    aliases = {1 + count + i: i for i in range(len(held))}
    if held:
        aliases |= {1 + i: 2 + i for i in range(count)}
    return pl.pallas_call(
        functools.partial(partial_kernel, replicas, items, not held),
        out_shape=[pltpu.VMEM((rows, wide), F32), pltpu.VMEM((2 * wide, wide), BF16)]
        + [pltpu.VMEM(block.shape, BF16) for block in blocks if held],
        in_specs=[VMEM] * len(inputs),
        out_specs=[VMEM] * (2 + count if held else 2),
        input_output_aliases=aliases,
        compiler_params=PARAMS,
        cost_estimate=cost(3 * rows * part * count * wide, 2**20),
    )(*inputs)


def forward_kernel(replicas, index, store, taps_t, low, high, acc, w_in, *refs):
    a1, a2, hid_t = refs[:3]
    samples, channels = a1.shape
    placed = place_rows(replicas, ((replicas // 2, 0), (replicas // 2, 2)), (low, high))
    chunk = min(256, samples)
    for at in range(0, samples, chunk):
        columns = slice(index * samples + at, index * samples + at + chunk)
        pre = acc[columns, :] + shard_term(taps_t, columns, placed)
        filt = jnp.tanh(pre[:, :channels])
        gate = jax.nn.sigmoid(pre[:, channels:])
        a1[at : at + chunk, :] = (gate * (1.0 - filt * filt)).astype(BF16)
        a2[at : at + chunk, :] = (filt * gate * (1.0 - gate)).astype(BF16)
        hid_t[:, at : at + chunk] = (filt * gate).T.astype(BF16)
    if store:
        store_shards(refs[3], placed)


def forward_call(replicas, index, micro, store, taps_t, low, high, acc, w):
    rows, wide = acc.shape
    channels = wide // 2
    samples = rows // micro
    inputs = in_vmem(taps_t, low, high, acc, w)
    return pl.pallas_call(
        functools.partial(forward_kernel, replicas, index, store),
        out_shape=[pltpu.VMEM((samples, channels), BF16)] * 2
        + [pltpu.VMEM((channels, samples), BF16)]
        + ([pltpu.VMEM(w.shape, BF16)] if store else []),
        in_specs=[VMEM] * 5,
        out_specs=[VMEM] * (4 if store else 3),
        input_output_aliases={4: 3} if store else {},
        compiler_params=PARAMS,
        cost_estimate=cost(2**28, 2**22),
    )(*inputs)


def chain_kernel(stage, index, halves, padding, before, held, g, skip, a1, a2, w, *refs):
    bt = refs[-1]
    carried = refs[0] if halves == (0,) else None
    pg, ig, gk, *extra = refs[before + held : -1]
    samples, channels = gk.shape
    chunk = samples // 2
    base = min(halves) * chunk
    count = len(halves) * chunk
    dilation = 2**stage
    g_base = base if g.shape[0] == samples else 0

    @pl.when(lax.axis_index("pipe") == stage)
    def _():
        for k in (1, 2):
            bt[k, count:, :] = jnp.zeros((padding, channels), F32) if carried is None else carried[k - 1]
        for half in halves:
            at = half * chunk
            rows = slice(at, at + chunk)
            here = slice(at - base, at - base + chunk)
            g_rows = slice(at - base + g_base, at - base + g_base + chunk)
            hid = lax.dot_general(
                g[g_rows, :], w[3 * channels :, :channels], NT, preferred_element_type=F32
            ) + lax.dot_general(
                skip[index, rows, :], w[3 * channels :, channels:], NT, preferred_element_type=F32
            )
            pg[rows, :channels] = (hid * a1[rows, :].astype(F32)).astype(BF16)
            pg[rows, channels:] = (hid * a2[rows, :].astype(F32)).astype(BF16)
            for k in range(3):
                bt[k, here, :] = lax.dot_general(
                    pg[rows, :], w[k * channels : (k + 1) * channels, :], NT, preferred_element_type=F32
                )
            piece = 64
            for first in range(at - base + chunk - piece, at - base - 1, -piece):
                last = first + piece
                total = g[first + g_base : last + g_base, :].astype(F32) + bt[0, first:last, :]
                total = total + bt[1, first + dilation : last + dilation, :]
                total = total + bt[2, first + 2 * dilation : last + 2 * dilation, :]
                ig[first + base : last + base, :] = total.astype(BF16)
                if extra:
                    extra[0][first:last, :] = total.astype(BF16)
            gk[rows, :] = g[g_rows, :]
        if halves == (1,):
            for k in (1, 2):
                extra[1][k - 1] = bt[k, :padding, :]


def chain_call(stage, index, halves, padding, g, skip, a1, a2, w, carried, held):
    samples, channels = a1.shape
    chunk = samples // 2
    tile = pltpu.VMEM((samples, channels), BF16)
    outs = [pltpu.VMEM((samples, 2 * channels), BF16), tile, tile]
    if len(halves) == 1:
        outs.append(pltpu.VMEM((chunk, channels), BF16))
    if halves == (1,):
        outs.append(pltpu.VMEM((2, padding, channels), F32))
    inputs = in_vmem(g, skip, a1, a2, w, *carried, *held)
    return pl.pallas_call(
        functools.partial(chain_kernel, stage, index, halves, padding, len(carried), len(held)),
        out_shape=outs,
        in_specs=[VMEM] * len(inputs),
        out_specs=[VMEM] * len(outs),
        scratch_shapes=[pltpu.VMEM((3, len(halves) * chunk + padding, channels), F32)],
        input_output_aliases={len(inputs) - len(held) + i: i for i in range(len(held))},
        compiler_params=PARAMS,
        cost_estimate=cost(8 * len(halves) * chunk * channels * channels, 2**22),
    )(*inputs)


def term_kernel(replicas, offsets, micro, taps_t, skip, *refs):
    hids, refs = refs[:micro], refs[micro:]
    pgs, refs = refs[:micro], refs[micro:]
    gs, refs = refs[:micro], refs[micro:]
    outs = refs[-2 * len(offsets) :]
    samples, wide = pgs[0].shape
    channels = wide // 2
    part = channels // replicas
    places = [owner_row(replicas, part, offset) for offset in offsets]
    conv, mix_g, mix_s = None, None, None
    for m in range(micro):
        columns = slice(m * samples, (m + 1) * samples)
        lhs = jnp.concatenate([tap_rows(taps_t, row, part, columns) for row in places], axis=0)
        lhs_mix = jnp.concatenate([hids[m][pl.ds(row, part), :] for row in places], axis=0)
        new = [
            jnp.dot(lhs, pgs[m][...], preferred_element_type=F32),
            jnp.dot(lhs_mix, gs[m][...], preferred_element_type=F32),
            jnp.dot(lhs_mix, skip[m], preferred_element_type=F32),
        ]
        conv, mix_g, mix_s = new if m == 0 else (conv + new[0], mix_g + new[1], mix_s + new[2])
    for slot in range(len(offsets)):
        low, high = outs[2 * slot : 2 * slot + 2]
        at = slot * 3 * part
        for k, target in enumerate((low.at[0], low.at[1], high.at[0])):
            target[...] = conv[at + k * part : at + (k + 1) * part, :].astype(low.dtype)
        here = slice(slot * part, (slot + 1) * part)
        high[1, :, :channels] = mix_g[here, :].astype(low.dtype)
        high[1, :, channels:] = mix_s[here, :].astype(low.dtype)


def term_call(replicas, offsets, kind, taps_t, skip, hid_t, pre_grads, gs, tokens):
    micro, samples, channels = skip.shape
    part = channels // replicas
    inputs = in_vmem(taps_t, skip, *hid_t, *pre_grads, *gs, *tokens)
    outs = 2 * len(offsets)
    return pl.pallas_call(
        functools.partial(term_kernel, replicas, offsets, micro),
        out_shape=[pltpu.VMEM((2, part, 2 * channels), kind)] * outs,
        in_specs=[VMEM] * len(inputs),
        out_specs=[VMEM] * outs,
        compiler_params=PARAMS,
        cost_estimate=cost(2**29 * len(offsets), 2**20),
    )(*inputs)


def add_kernel(mine_r, mine_l, got_r, got_l, *refs):
    out_r, out_l = refs[-2:]
    out_r[...] = (mine_r[...].astype(F32) + got_r[...].astype(F32)).astype(BF16)
    out_l[...] = (mine_l[...].astype(F32) + got_l[...].astype(F32)).astype(BF16)


def add_call(mine, got, tokens):
    inputs = in_vmem(*mine, *got, *tokens)
    return pl.pallas_call(
        add_kernel,
        out_shape=[pltpu.VMEM(got[0].shape, BF16)] * 2,
        in_specs=[VMEM] * len(inputs),
        out_specs=[VMEM] * 2,
        compiler_params=PARAMS,
        cost_estimate=cost(2**18, 2**19),
    )(*inputs)


def final_kernel(low, high, low_r, low_l, high_r, high_l, conv, mix):
    conv[0:2] = low[...] + (low_r[...].astype(F32) + low_l[...].astype(F32))
    total = high[...] + (high_r[...].astype(F32) + high_l[...].astype(F32))
    conv[2] = total[0]
    mix[...] = total[1]


def final_call(*blocks):
    part, wide = blocks[0].shape[1:]
    return pl.pallas_call(
        final_kernel,
        out_shape=[jax.ShapeDtypeStruct((3, part, wide), F32), jax.ShapeDtypeStruct((part, wide), F32)],
        in_specs=[VMEM] * 6,
        out_specs=[VMEM] * 2,
        compiler_params=PARAMS,
        cost_estimate=cost(2**19, 2**20),
    )(*in_vmem(*blocks))


def local(x_ckpt, top_cot, skip_cot, w_conv, w_mix):
    sections = lax.axis_size("pipe")
    replicas = lax.axis_size("dp")
    micro, seqs, samples, channels = x_ckpt.shape[1:]
    block = seqs * samples
    half = replicas // 2
    right, left = ring_pairs(replicas)

    def send(to_right, to_left):
        return lax.ppermute(to_right, "dp", right), lax.ppermute(to_left, "dp", left)

    taps_t = prepare_call(x_ckpt[0].reshape(micro * seqs, samples, channels))
    low, high = split_call(w_conv[0].transpose(1, 0, 2), w_mix)
    streams = {0: (low, low), 2: (high, high)}
    held = partial_call(replicas, ((0, 0), (0, 2)), taps_t, [low, high], [])
    for step in range(1, half):
        for first, (to_right, to_left) in streams.items():
            got = send(to_right, to_left)
            items = ((-step, first), (step, first))
            *held, to_right, to_left = partial_call(replicas, items, taps_t, got, held)
            streams[first] = (to_right, to_left)
    acc, w_full = held
    low = lax.ppermute(streams[0][0], "dp", right)
    high = lax.ppermute(streams[2][1], "dp", left)

    skip = skip_cot.reshape(micro, block, channels)
    g = list(top_cot.reshape(micro, block, channels))
    padding = max(16, 2 * 2 ** (sections - 1))
    hid_t, held, ready = [], [()] * micro, []
    for m in range(micro):
        a1, a2, hid, *stored = forward_call(
            replicas, m, micro, m == 0, taps_t, low, high, acc, w_full
        )
        if stored:
            w_full = stored[0]
        hid_t.append(hid)
        ready.append((a1, a2))
    last = sections - 1
    g = [[piece, piece] for piece in g]
    for m in range(micro):
        held[m] = chain_call(last, m, (1, 0), padding, g[m][0], skip, *ready[m], w_full, (), ())
        g[m] = [lax.ppermute(held[m][1], "pipe", [(last, last - 1)])] * 2
    for stage in range(last - 1, -1, -1):
        piece = None
        for m in range(micro):
            carried = () if piece is None else (piece,)
            for half_at in (1, 0):
                out = chain_call(
                    stage, m, (half_at,), padding, g[m][half_at], skip, *ready[m], w_full, carried, held[m]
                )
                held[m], piece, carried = out[:3], out[3], out[4:]
                if stage:
                    g[m][half_at] = lax.ppermute(piece, "pipe", [(stage, stage - 1)])
    pre_grads, cots, gs = zip(*held)
    cot = jnp.stack(cots, axis=0)

    def terms(dist, tokens, kind=BF16):
        offsets = (dist,) if dist in (0, half) else (dist, -dist)
        return term_call(replicas, offsets, kind, taps_t, skip, hid_t, pre_grads, gs, tokens)

    low, high = terms(half, ())
    got_one = send(low, high)
    mine = terms(half - 1, (low,))
    got_two = send(mine[1], mine[2])
    token = ()
    for dist in range(half - 1, 0, -1):
        if dist < half - 1:
            out = add_call((mine[1], mine[2]), got_two, token)
            token = out[:1]
            got_two = send(*out)
        out = add_call((mine[0], mine[3]), got_one, token)
        token = out[:1]
        got_one = send(*out)
        if dist > 1:
            mine = terms(dist - 1, token)
    low, high = terms(0, token, F32)
    share_conv, share_mix = final_call(low, high, got_one[0], got_two[1], got_two[0], got_one[1])
    return (
        cot.reshape(1, micro, seqs, samples, channels),
        share_conv.transpose(1, 0, 2)[None],
        share_mix[None],
    )


def solution(mesh):
    placed = (
        P("pipe", None, "dp", None, None),
        P(None, "dp", None, None),
        P(None, "dp", None, None),
        P("pipe", "dp", None, None),
        P("pipe", "dp", None),
    )
    return jax.shard_map(
        local,
        mesh=mesh,
        in_specs=placed,
        out_specs=(
            P("pipe", None, "dp", None, None),
            P("pipe", "dp", None, None),
            P("pipe", "dp", None),
        ),
        check_vma=False,
    )
```

```python
import functools

import jax
import jax.numpy as jnp
from jax import lax
from jax.experimental import pallas as pl
from jax.experimental.pallas import tpu as pltpu
from jax.sharding import PartitionSpec as P

F32 = jnp.float32
BF16 = jnp.bfloat16
NT = (((1,), (1,)), ((), ()))
TN = (((0,), (0,)), ((), ()))
VMEM = pl.BlockSpec(memory_space=pltpu.VMEM)
PARAMS = pltpu.CompilerParams(vmem_limit_bytes=24 * 2**20)


def ring_pairs(count):
    order = list(range(0, count, 2)) + list(range(count - 1 - count % 2, 0, -2))
    right = [(order[i], order[(i + 1) % count]) for i in range(count)]
    return right, [(b, a) for a, b in right]


def in_vmem(*arrays):
    return [pltpu.with_memory_space_constraint(array, pltpu.VMEM) for array in arrays]


def cost(flops, moved):
    return pl.CostEstimate(flops=flops, bytes_accessed=moved, transcendentals=0)


def owner_row(replicas, part, offset):
    replica = lax.axis_index("dp")
    step = replica // 2
    place = jnp.where(lax.rem(replica, 2) == 0, step, replicas - 1 - step)
    at = lax.rem(place + (offset + replicas), replicas)
    owner = jnp.where(at < replicas // 2, 2 * at, 2 * (replicas - 1 - at) + 1)
    return pl.multiple_of(owner * part, part)


def split_kernel(conv, mix, low, high, sems):
    copies = [
        pltpu.make_async_copy(conv.at[0:2], low, sems.at[0]),
        pltpu.make_async_copy(conv.at[2], high.at[0], sems.at[1]),
        pltpu.make_async_copy(mix.at[0], high.at[1], sems.at[2]),
    ]
    for copy in copies:
        copy.start()
    for copy in copies:
        copy.wait()


def split_call(conv, mix):
    anywhere = pl.BlockSpec(memory_space=pl.ANY)
    return pl.pallas_call(
        split_kernel,
        out_shape=[pltpu.VMEM((2, *conv.shape[1:]), BF16)] * 2,
        in_specs=[anywhere] * 2,
        out_specs=[VMEM] * 2,
        scratch_shapes=[pltpu.SemaphoreType.DMA((3,))],
        compiler_params=PARAMS,
        cost_estimate=cost(0, 2**20),
    )(*[pltpu.with_memory_space_constraint(array, pltpu.HBM) for array in (conv, mix)])


def prepare_kernel(x, taps_t):
    seqs, samples, channels = x.shape
    dilation = jnp.left_shift(jnp.int32(1), lax.axis_index("pipe"))
    wide = 128
    for s in range(seqs):
        columns = slice(s * samples, (s + 1) * samples)
        for at in range(0, channels, wide):
            turned = x[s, :, at : at + wide].astype(F32).T
            position = lax.broadcasted_iota(jnp.int32, turned.shape, 1)
            taps_t[at : at + wide, columns] = turned.astype(BF16)
            for k in (1, 2):
                delayed = jnp.where(position >= k * dilation, pltpu.roll(turned, k * dilation, 1), 0.0)
                taps_t[k * channels + at : k * channels + at + wide, columns] = delayed.astype(BF16)


def prepare_call(x):
    seqs, samples, channels = x.shape
    return pl.pallas_call(
        prepare_kernel,
        out_shape=pltpu.VMEM((3 * channels, seqs * samples), BF16),
        in_specs=[VMEM],
        out_specs=VMEM,
        compiler_params=PARAMS,
        cost_estimate=cost(2**20, 2**22),
    )(x)


def tap_rows(taps_t, row, part, columns):
    channels = taps_t.shape[0] // 3
    return jnp.concatenate([taps_t[pl.ds(k * channels + row, part), columns] for k in range(3)], axis=0)


def place_rows(replicas, items, blocks):
    part = blocks[0].shape[1]
    return [(owner_row(replicas, part, offset), first, block) for (offset, first), block in zip(items, blocks)]


def shard_term(taps_t, columns, placed):
    channels = taps_t.shape[0] // 3
    part, wide = placed[0][2].shape[1:]
    rows, weights = [], []
    for row, first, block in placed:
        count = min(block.shape[0], 3 - first)
        if count == 0:
            continue
        rows += [taps_t[pl.ds((first + k) * channels + row, part), columns] for k in range(count)]
        weights.append(block[:count].reshape(count * part, wide))
    return lax.dot_general(
        jnp.concatenate(rows, axis=0), jnp.concatenate(weights, axis=0), TN, preferred_element_type=F32
    )


def store_shards(w, placed):
    channels = w.shape[0] // 4
    for row, first, block in placed:
        for k in range(block.shape[0]):
            w[pl.ds((first + k) * channels + row, block.shape[1]), :] = block[k]


def partial_kernel(replicas, items, first, quarters, tokens, taps_t, *refs):
    count = len(items)
    blocks = refs[:count]
    placed = place_rows(replicas, items, blocks)
    refs = refs[count:]
    acc, w, *passed = refs if first else refs[2 + tokens :]
    rows = taps_t.shape[1]
    chunk = min(256, rows)
    for at in range(0, rows, chunk):
        columns = slice(at, at + chunk)
        term = shard_term(taps_t, columns, placed)
        acc[columns, :] = term if first else refs[0][columns, :] + term
    store_shards(w, placed)
    if quarters:
        passed[0][...] = blocks[0][0:1]
        passed[1][...] = blocks[1][1:2]


def partial_call(replicas, items, taps_t, blocks, held, passing=None, tokens=()):
    part, wide = blocks[0].shape[1:]
    rows = taps_t.shape[1]
    count = len(items)
    inputs = in_vmem(taps_t, *blocks, *held, *tokens)
    aliases = {1 + count + i: i for i in range(len(held))}
    if passing == "whole":
        aliases |= {1 + i: 2 + i for i in range(count)}
    return pl.pallas_call(
        functools.partial(partial_kernel, replicas, items, not held, passing == "quarters", len(tokens)),
        out_shape=[pltpu.VMEM((rows, wide), F32), pltpu.VMEM((2 * wide, wide), BF16)]
        + [pltpu.VMEM((2 if passing == "whole" else 1, part, wide), BF16) for _ in blocks if passing],
        in_specs=[VMEM] * len(inputs),
        out_specs=[VMEM] * (2 + count if passing else 2),
        input_output_aliases=aliases,
        compiler_params=PARAMS,
        cost_estimate=cost(3 * rows * part * count * wide, 2**20),
    )(*inputs)


def forward_kernel(replicas, index, store, taps_t, acc, w_in, *refs):
    blocks, refs = refs[:2], refs[2:]
    a1, a2, hid_t = refs[:3]
    samples, channels = a1.shape
    placed = place_rows(replicas, [(replicas // 2, k) for k in (2, 3)], blocks)
    chunk = min(256, samples)
    for at in range(0, samples, chunk):
        columns = slice(index * samples + at, index * samples + at + chunk)
        pre = acc[columns, :] + shard_term(taps_t, columns, placed)
        filt = jnp.tanh(pre[:, :channels])
        gate = jax.nn.sigmoid(pre[:, channels:])
        a1[at : at + chunk, :] = (gate * (1.0 - filt * filt)).astype(BF16)
        a2[at : at + chunk, :] = (filt * gate * (1.0 - gate)).astype(BF16)
        hid_t[:, at : at + chunk] = (filt * gate).T.astype(BF16)
    if store:
        store_shards(refs[3], placed)


def forward_call(replicas, index, micro, store, taps_t, acc, w, blocks):
    rows, wide = acc.shape
    channels = wide // 2
    samples = rows // micro
    inputs = in_vmem(taps_t, acc, w, *blocks)
    return pl.pallas_call(
        functools.partial(forward_kernel, replicas, index, store),
        out_shape=[pltpu.VMEM((samples, channels), BF16)] * 2
        + [pltpu.VMEM((channels, samples), BF16)]
        + ([pltpu.VMEM(w.shape, BF16)] if store else []),
        in_specs=[VMEM] * len(inputs),
        out_specs=[VMEM] * (4 if store else 3),
        input_output_aliases={2: 3} if store else {},
        compiler_params=PARAMS,
        cost_estimate=cost(2**28, 2**22),
    )(*inputs)


def chain_kernel(stage, index, halves, padding, before, held, g, skip, a1, a2, w, *refs):
    bt = refs[-1]
    carried = refs[0] if halves == (0,) else None
    pg, ig, gk, *extra = refs[before + held : -1]
    samples, channels = gk.shape
    chunk = samples // 2
    base = min(halves) * chunk
    count = len(halves) * chunk
    dilation = 2**stage
    g_base = base if g.shape[0] == samples else 0

    @pl.when(lax.axis_index("pipe") == stage)
    def _():
        for k in (1, 2):
            bt[k, count:, :] = jnp.zeros((padding, channels), F32) if carried is None else carried[k - 1]
        for half in halves:
            at = half * chunk
            rows = slice(at, at + chunk)
            here = slice(at - base, at - base + chunk)
            g_rows = slice(at - base + g_base, at - base + g_base + chunk)
            hid = lax.dot_general(
                g[g_rows, :], w[3 * channels :, :channels], NT, preferred_element_type=F32
            ) + lax.dot_general(
                skip[index, rows, :], w[3 * channels :, channels:], NT, preferred_element_type=F32
            )
            pg[rows, :channels] = (hid * a1[rows, :].astype(F32)).astype(BF16)
            pg[rows, channels:] = (hid * a2[rows, :].astype(F32)).astype(BF16)
            for k in range(3):
                bt[k, here, :] = lax.dot_general(
                    pg[rows, :], w[k * channels : (k + 1) * channels, :], NT, preferred_element_type=F32
                )
            piece = 64
            for first in range(at - base + chunk - piece, at - base - 1, -piece):
                last = first + piece
                total = g[first + g_base : last + g_base, :].astype(F32) + bt[0, first:last, :]
                total = total + bt[1, first + dilation : last + dilation, :]
                total = total + bt[2, first + 2 * dilation : last + 2 * dilation, :]
                ig[first + base : last + base, :] = total.astype(BF16)
                if len(halves) == 1 and stage:
                    extra[0][first:last, :] = total.astype(BF16)
            gk[rows, :] = g[g_rows, :]
        if halves == (1,):
            for k in (1, 2):
                extra[-1][k - 1] = bt[k, :padding, :]


def chain_call(stage, index, halves, padding, g, skip, a1, a2, w, carried, held):
    samples, channels = a1.shape
    chunk = samples // 2
    tile = pltpu.VMEM((samples, channels), BF16)
    outs = [pltpu.VMEM((samples, 2 * channels), BF16), tile, tile]
    if len(halves) == 1 and stage:
        outs.append(pltpu.VMEM((chunk, channels), BF16))
    if halves == (1,):
        outs.append(pltpu.VMEM((2, padding, channels), F32))
    inputs = in_vmem(g, skip, a1, a2, w, *carried, *held)
    return pl.pallas_call(
        functools.partial(chain_kernel, stage, index, halves, padding, len(carried), len(held)),
        out_shape=outs,
        in_specs=[VMEM] * len(inputs),
        out_specs=[VMEM] * len(outs),
        scratch_shapes=[pltpu.VMEM((3, len(halves) * chunk + padding, channels), F32)],
        input_output_aliases={len(inputs) - len(held) + i: i for i in range(len(held))},
        compiler_params=PARAMS,
        cost_estimate=cost(8 * len(halves) * chunk * channels * channels, 2**22),
    )(*inputs)


def term_kernel(replicas, offsets, micro, taps_t, skip, *refs):
    hids, refs = refs[:micro], refs[micro:]
    pgs, refs = refs[:micro], refs[micro:]
    gs, refs = refs[:micro], refs[micro:]
    outs = refs[-2 * len(offsets) :]
    samples, wide = pgs[0].shape
    channels = wide // 2
    part = channels // replicas
    places = [owner_row(replicas, part, offset) for offset in offsets]
    conv, mix_g, mix_s = None, None, None
    for m in range(micro):
        columns = slice(m * samples, (m + 1) * samples)
        lhs = jnp.concatenate([tap_rows(taps_t, row, part, columns) for row in places], axis=0)
        lhs_mix = jnp.concatenate([hids[m][pl.ds(row, part), :] for row in places], axis=0)
        new = [
            jnp.dot(lhs, pgs[m][...], preferred_element_type=F32),
            jnp.dot(lhs_mix, gs[m][...], preferred_element_type=F32),
            jnp.dot(lhs_mix, skip[m], preferred_element_type=F32),
        ]
        conv, mix_g, mix_s = new if m == 0 else (conv + new[0], mix_g + new[1], mix_s + new[2])
    for slot in range(len(offsets)):
        low, high = outs[2 * slot : 2 * slot + 2]
        at = slot * 3 * part
        for k, target in enumerate((low.at[0], low.at[1], high.at[0])):
            target[...] = conv[at + k * part : at + (k + 1) * part, :].astype(low.dtype)
        here = slice(slot * part, (slot + 1) * part)
        high[1, :, :channels] = mix_g[here, :].astype(low.dtype)
        high[1, :, channels:] = mix_s[here, :].astype(low.dtype)


def term_call(replicas, offsets, kind, taps_t, skip, hid_t, pre_grads, gs, tokens):
    micro, samples, channels = skip.shape
    part = channels // replicas
    inputs = in_vmem(taps_t, skip, *hid_t, *pre_grads, *gs, *tokens)
    outs = 2 * len(offsets)
    return pl.pallas_call(
        functools.partial(term_kernel, replicas, offsets, micro),
        out_shape=[pltpu.VMEM((2, part, 2 * channels), kind)] * outs,
        in_specs=[VMEM] * len(inputs),
        out_specs=[VMEM] * outs,
        compiler_params=PARAMS,
        cost_estimate=cost(2**29 * len(offsets), 2**20),
    )(*inputs)


def add_kernel(mine_r, mine_l, got_r, got_l, *refs):
    out_r, out_l = refs[-2:]
    out_r[...] = (mine_r[...].astype(F32) + got_r[...].astype(F32)).astype(BF16)
    out_l[...] = (mine_l[...].astype(F32) + got_l[...].astype(F32)).astype(BF16)


def add_call(mine, got, tokens):
    inputs = in_vmem(*mine, *got, *tokens)
    return pl.pallas_call(
        add_kernel,
        out_shape=[pltpu.VMEM(got[0].shape, BF16)] * 2,
        in_specs=[VMEM] * len(inputs),
        out_specs=[VMEM] * 2,
        compiler_params=PARAMS,
        cost_estimate=cost(2**18, 2**19),
    )(*inputs)


def final_kernel(low, high, low_r, low_l, high_r, high_l, conv, mix):
    conv[0:2] = low[...] + (low_r[...].astype(F32) + low_l[...].astype(F32))
    total = high[...] + (high_r[...].astype(F32) + high_l[...].astype(F32))
    conv[2] = total[0]
    mix[...] = total[1]


def final_call(*blocks):
    part, wide = blocks[0].shape[1:]
    return pl.pallas_call(
        final_kernel,
        out_shape=[jax.ShapeDtypeStruct((3, part, wide), F32), jax.ShapeDtypeStruct((part, wide), F32)],
        in_specs=[VMEM] * 6,
        out_specs=[VMEM] * 2,
        compiler_params=PARAMS,
        cost_estimate=cost(2**19, 2**20),
    )(*in_vmem(*blocks))


def local(x_ckpt, top_cot, skip_cot, w_conv, w_mix):
    sections = lax.axis_size("pipe")
    replicas = lax.axis_size("dp")
    micro, seqs, samples, channels = x_ckpt.shape[1:]
    block = seqs * samples
    half = replicas // 2
    right, left = ring_pairs(replicas)

    def send(to_right, to_left):
        return lax.ppermute(to_right, "dp", right), lax.ppermute(to_left, "dp", left)

    taps_t = prepare_call(x_ckpt[0].reshape(micro * seqs, samples, channels))
    low, high = split_call(w_conv[0].transpose(1, 0, 2), w_mix)
    streams = {0: (low, low), 2: (high, high)}
    held = partial_call(replicas, ((0, 0), (0, 2)), taps_t, [low, high], [])
    skip = skip_cot.reshape(micro, block, channels)
    for step in range(1, half):
        last = step == half - 1
        for first, (to_right, to_left) in streams.items():
            got = send(to_right, to_left)
            items = ((-step, first), (step, first))
            if last and first:
                blocks = send(got[0][:1], got[1][1:])
                items += ((half, 0), (half, 1))
                held = partial_call(replicas, items, taps_t, [*got, *ahead], held, None, (skip,))
                continue
            passing = "quarters" if last else "whole"
            *held, to_right, to_left = partial_call(replicas, items, taps_t, got, held, passing)
            streams[first] = (to_right, to_left)
            if last:
                ahead = send(to_right, to_left)
    acc, w_full = held

    g = list(top_cot.reshape(micro, block, channels))
    padding = max(16, 2 * 2 ** (sections - 1))
    hid_t, held, ready = [], [()] * micro, []
    for m in range(micro):
        a1, a2, hid, *stored = forward_call(
            replicas, m, micro, m == 0, taps_t, acc, w_full, blocks
        )
        if stored:
            w_full = stored[0]
        hid_t.append(hid)
        ready.append((a1, a2))
    last = sections - 1
    g = [[piece, piece] for piece in g]
    for m in range(micro):
        held[m] = chain_call(last, m, (1, 0), padding, g[m][0], skip, *ready[m], w_full, (), ())
        g[m] = [lax.ppermute(held[m][1], "pipe", [(last, last - 1)])] * 2
    for stage in range(last - 1, -1, -1):
        piece = None
        for m in range(micro):
            carried = () if piece is None else (piece,)
            for half_at in (1, 0):
                out = chain_call(
                    stage, m, (half_at,), padding, g[m][half_at], skip, *ready[m], w_full, carried, held[m]
                )
                held[m], carried = out[:3], out[-1:]
                piece = out[3] if stage else out[1]
                if stage:
                    g[m][half_at] = lax.ppermute(piece, "pipe", [(stage, stage - 1)])
    pre_grads, cots, gs = zip(*held)
    cot = jnp.stack(cots, axis=0)

    def terms(dist, tokens, kind=BF16):
        offsets = (dist,) if dist in (0, half) else (dist, -dist)
        return term_call(replicas, offsets, kind, taps_t, skip, hid_t, pre_grads, gs, tokens)

    low, high = terms(half, ())
    got_one = send(low, high)
    mine = terms(half - 1, (low,))
    got_two = send(mine[1], mine[2])
    token = ()
    for dist in range(half - 1, 0, -1):
        if dist < half - 1:
            out = add_call((mine[1], mine[2]), got_two, token)
            token = out[:1]
            got_two = send(*out)
        out = add_call((mine[0], mine[3]), got_one, token)
        token = out[:1]
        got_one = send(*out)
        if dist > 1:
            mine = terms(dist - 1, token)
    low, high = terms(0, token, F32)
    share_conv, share_mix = final_call(low, high, got_one[0], got_two[1], got_two[0], got_one[1])
    return (
        cot.reshape(1, micro, seqs, samples, channels),
        share_conv.transpose(1, 0, 2)[None],
        share_mix[None],
    )


def solution(mesh):
    placed = (
        P("pipe", None, "dp", None, None),
        P(None, "dp", None, None),
        P(None, "dp", None, None),
        P("pipe", "dp", None, None),
        P("pipe", "dp", None),
    )
    return jax.shard_map(
        local,
        mesh=mesh,
        in_specs=placed,
        out_specs=(
            P("pipe", None, "dp", None, None),
            P("pipe", "dp", None, None),
            P("pipe", "dp", None),
        ),
        check_vma=False,
    )
```

```python
import functools

import jax
import jax.numpy as jnp
from jax import lax
from jax.experimental import pallas as pl
from jax.experimental.pallas import tpu as pltpu
from jax.sharding import PartitionSpec as P

F32 = jnp.float32
BF16 = jnp.bfloat16
NT = (((1,), (1,)), ((), ()))
TN = (((0,), (0,)), ((), ()))
VMEM = pl.BlockSpec(memory_space=pltpu.VMEM)
PARAMS = pltpu.CompilerParams(vmem_limit_bytes=24 * 2**20)


def ring_pairs(count):
    order = list(range(0, count, 2)) + list(range(count - 1 - count % 2, 0, -2))
    right = [(order[i], order[(i + 1) % count]) for i in range(count)]
    return right, [(b, a) for a, b in right]


def in_vmem(*arrays):
    return [pltpu.with_memory_space_constraint(array, pltpu.VMEM) for array in arrays]


def cost(flops, moved):
    return pl.CostEstimate(flops=flops, bytes_accessed=moved, transcendentals=0)


def owner_row(replicas, part, offset):
    replica = lax.axis_index("dp")
    step = replica // 2
    place = jnp.where(lax.rem(replica, 2) == 0, step, replicas - 1 - step)
    at = lax.rem(place + (offset + replicas), replicas)
    owner = jnp.where(at < replicas // 2, 2 * at, 2 * (replicas - 1 - at) + 1)
    return pl.multiple_of(owner * part, part)


def split_kernel(conv, mix, low, high, sems):
    copies = [
        pltpu.make_async_copy(conv.at[0:2], low, sems.at[0]),
        pltpu.make_async_copy(conv.at[2], high.at[0], sems.at[1]),
        pltpu.make_async_copy(mix.at[0], high.at[1], sems.at[2]),
    ]
    for copy in copies:
        copy.start()
    for copy in copies:
        copy.wait()


def split_call(conv, mix):
    anywhere = pl.BlockSpec(memory_space=pl.ANY)
    return pl.pallas_call(
        split_kernel,
        out_shape=[pltpu.VMEM((2, *conv.shape[1:]), BF16)] * 2,
        in_specs=[anywhere] * 2,
        out_specs=[VMEM] * 2,
        scratch_shapes=[pltpu.SemaphoreType.DMA((3,))],
        compiler_params=PARAMS,
        cost_estimate=cost(0, 2**20),
    )(*[pltpu.with_memory_space_constraint(array, pltpu.HBM) for array in (conv, mix)])


def prepare_kernel(x, taps_t):
    seqs, samples, channels = x.shape
    dilation = jnp.left_shift(jnp.int32(1), lax.axis_index("pipe"))
    wide = 128
    for s in range(seqs):
        columns = slice(s * samples, (s + 1) * samples)
        for at in range(0, channels, wide):
            turned = x[s, :, at : at + wide].astype(F32).T
            position = lax.broadcasted_iota(jnp.int32, turned.shape, 1)
            taps_t[at : at + wide, columns] = turned.astype(BF16)
            for k in (1, 2):
                delayed = jnp.where(position >= k * dilation, pltpu.roll(turned, k * dilation, 1), 0.0)
                taps_t[k * channels + at : k * channels + at + wide, columns] = delayed.astype(BF16)


def prepare_call(x):
    seqs, samples, channels = x.shape
    return pl.pallas_call(
        prepare_kernel,
        out_shape=pltpu.VMEM((3 * channels, seqs * samples), BF16),
        in_specs=[VMEM],
        out_specs=VMEM,
        compiler_params=PARAMS,
        cost_estimate=cost(2**20, 2**22),
    )(x)


def tap_rows(taps_t, row, part, columns):
    channels = taps_t.shape[0] // 3
    return jnp.concatenate([taps_t[pl.ds(k * channels + row, part), columns] for k in range(3)], axis=0)


def place_rows(replicas, items, blocks):
    part = blocks[0].shape[1]
    return [(owner_row(replicas, part, offset), first, block) for (offset, first), block in zip(items, blocks)]


def shard_term(taps_t, columns, placed):
    channels = taps_t.shape[0] // 3
    part, wide = placed[0][2].shape[1:]
    rows, weights = [], []
    for row, first, block in placed:
        count = min(block.shape[0], 3 - first)
        if count == 0:
            continue
        rows += [taps_t[pl.ds((first + k) * channels + row, part), columns] for k in range(count)]
        weights.append(block[:count].reshape(count * part, wide))
    return lax.dot_general(
        jnp.concatenate(rows, axis=0), jnp.concatenate(weights, axis=0), TN, preferred_element_type=F32
    )


def store_shards(w, placed):
    channels = w.shape[0] // 4
    for row, first, block in placed:
        for k in range(block.shape[0]):
            w[pl.ds((first + k) * channels + row, block.shape[1]), :] = block[k]


def partial_kernel(replicas, items, first, quarters, tokens, taps_t, *refs):
    count = len(items)
    blocks = refs[:count]
    placed = place_rows(replicas, items, blocks)
    refs = refs[count:]
    acc, w, *passed = refs if first else refs[2 + tokens :]
    rows = taps_t.shape[1]
    chunk = min(256, rows)
    for at in range(0, rows, chunk):
        columns = slice(at, at + chunk)
        term = shard_term(taps_t, columns, placed)
        acc[columns, :] = term if first else refs[0][columns, :] + term
    store_shards(w, placed)
    if quarters:
        passed[0][...] = blocks[0][0:1]
        passed[1][...] = blocks[1][1:2]


def partial_call(replicas, items, taps_t, blocks, held, passing=None, tokens=()):
    part, wide = blocks[0].shape[1:]
    rows = taps_t.shape[1]
    count = len(items)
    inputs = in_vmem(taps_t, *blocks, *held, *tokens)
    aliases = {1 + count + i: i for i in range(len(held))}
    if passing == "whole":
        aliases |= {1 + i: 2 + i for i in range(count)}
    return pl.pallas_call(
        functools.partial(partial_kernel, replicas, items, not held, passing == "quarters", len(tokens)),
        out_shape=[pltpu.VMEM((rows, wide), F32), pltpu.VMEM((2 * wide, wide), BF16)]
        + [pltpu.VMEM((2 if passing == "whole" else 1, part, wide), BF16) for _ in blocks if passing],
        in_specs=[VMEM] * len(inputs),
        out_specs=[VMEM] * (2 + count if passing else 2),
        input_output_aliases=aliases,
        compiler_params=PARAMS,
        cost_estimate=cost(3 * rows * part * count * wide, 2**20),
    )(*inputs)


def forward_kernel(replicas, index, store, taps_t, acc, w_in, *refs):
    blocks, refs = refs[:2], refs[2:]
    a1, a2, hid_t = refs[:3]
    samples, channels = a1.shape
    placed = place_rows(replicas, [(replicas // 2, k) for k in (2, 3)], blocks)
    chunk = min(256, samples)
    for at in range(0, samples, chunk):
        columns = slice(index * samples + at, index * samples + at + chunk)
        pre = acc[columns, :] + shard_term(taps_t, columns, placed)
        filt = jnp.tanh(pre[:, :channels])
        gate = jax.nn.sigmoid(pre[:, channels:])
        a1[at : at + chunk, :] = (gate * (1.0 - filt * filt)).astype(BF16)
        a2[at : at + chunk, :] = (filt * gate * (1.0 - gate)).astype(BF16)
        hid_t[:, at : at + chunk] = (filt * gate).T.astype(BF16)
    if store:
        store_shards(refs[3], placed)


def forward_call(replicas, index, micro, store, taps_t, acc, w, blocks):
    rows, wide = acc.shape
    channels = wide // 2
    samples = rows // micro
    inputs = in_vmem(taps_t, acc, w, *blocks)
    return pl.pallas_call(
        functools.partial(forward_kernel, replicas, index, store),
        out_shape=[pltpu.VMEM((samples, channels), BF16)] * 2
        + [pltpu.VMEM((channels, samples), BF16)]
        + ([pltpu.VMEM(w.shape, BF16)] if store else []),
        in_specs=[VMEM] * len(inputs),
        out_specs=[VMEM] * (4 if store else 3),
        input_output_aliases={2: 3} if store else {},
        compiler_params=PARAMS,
        cost_estimate=cost(2**28, 2**22),
    )(*inputs)


def chain_kernel(stage, index, halves, padding, before, held, g, skip, a1, a2, w, *refs):
    bt = refs[-1]
    carried = refs[0] if halves == (0,) else None
    pg, ig, gk, *extra = refs[before + held : -1]
    samples, channels = gk.shape
    chunk = samples // 2
    base = min(halves) * chunk
    count = len(halves) * chunk
    dilation = 2**stage
    g_base = base if g.shape[0] == samples else 0

    @pl.when(lax.axis_index("pipe") == stage)
    def _():
        for k in (1, 2):
            bt[k, count:, :] = jnp.zeros((padding, channels), F32) if carried is None else carried[k - 1]
        for half in halves:
            at = half * chunk
            rows = slice(at, at + chunk)
            here = slice(at - base, at - base + chunk)
            g_rows = slice(at - base + g_base, at - base + g_base + chunk)
            hid = lax.dot_general(
                g[g_rows, :], w[3 * channels :, :channels], NT, preferred_element_type=F32
            ) + lax.dot_general(
                skip[index, rows, :], w[3 * channels :, channels:], NT, preferred_element_type=F32
            )
            pg[rows, :channels] = (hid * a1[rows, :].astype(F32)).astype(BF16)
            pg[rows, channels:] = (hid * a2[rows, :].astype(F32)).astype(BF16)
            for k in range(3):
                bt[k, here, :] = lax.dot_general(
                    pg[rows, :], w[k * channels : (k + 1) * channels, :], NT, preferred_element_type=F32
                )
            piece = 64
            for first in range(at - base + chunk - piece, at - base - 1, -piece):
                last = first + piece
                total = g[first + g_base : last + g_base, :].astype(F32) + bt[0, first:last, :]
                total = total + bt[1, first + dilation : last + dilation, :]
                total = total + bt[2, first + 2 * dilation : last + 2 * dilation, :]
                ig[first + base : last + base, :] = total.astype(BF16)
                if len(halves) == 1 and stage:
                    extra[0][first:last, :] = total.astype(BF16)
            gk[rows, :] = g[g_rows, :]
        if halves == (1,):
            for k in (1, 2):
                extra[-1][k - 1] = bt[k, :padding, :]


def chain_call(stage, index, halves, padding, g, skip, a1, a2, w, carried, held):
    samples, channels = a1.shape
    chunk = samples // 2
    tile = pltpu.VMEM((samples, channels), BF16)
    outs = [pltpu.VMEM((samples, 2 * channels), BF16), tile, tile]
    if len(halves) == 1 and stage:
        outs.append(pltpu.VMEM((chunk, channels), BF16))
    if halves == (1,):
        outs.append(pltpu.VMEM((2, padding, channels), F32))
    inputs = in_vmem(g, skip, a1, a2, w, *carried, *held)
    return pl.pallas_call(
        functools.partial(chain_kernel, stage, index, halves, padding, len(carried), len(held)),
        out_shape=outs,
        in_specs=[VMEM] * len(inputs),
        out_specs=[VMEM] * len(outs),
        scratch_shapes=[pltpu.VMEM((3, len(halves) * chunk + padding, channels), F32)],
        input_output_aliases={len(inputs) - len(held) + i: i for i in range(len(held))},
        compiler_params=PARAMS,
        cost_estimate=cost(8 * len(halves) * chunk * channels * channels, 2**22),
    )(*inputs)


def term_kernel(replicas, offsets, micro, taps_t, skip, *refs):
    hids, refs = refs[:micro], refs[micro:]
    pgs, refs = refs[:micro], refs[micro:]
    gs, refs = refs[:micro], refs[micro:]
    outs = refs[-2 * len(offsets) :]
    samples, wide = pgs[0].shape
    channels = wide // 2
    part = channels // replicas
    places = [owner_row(replicas, part, offset) for offset in offsets]
    step = min(256, channels)

    def product(rows_of, right, columns):
        total = None
        for m in range(micro):
            new = jnp.dot(rows_of(m), right(m, columns), preferred_element_type=F32)
            total = new if total is None else total + new
        return total

    def conv_rows(m):
        here = slice(m * samples, (m + 1) * samples)
        return jnp.concatenate([tap_rows(taps_t, row, part, here) for row in places], axis=0)

    def mix_rows(m):
        return jnp.concatenate([hids[m][pl.ds(row, part), :] for row in places], axis=0)

    @pl.loop(0, wide // step)
    def _(j):
        columns = pl.ds(pl.multiple_of(j * step, step), step)
        conv = product(conv_rows, lambda m, at: pgs[m][:, at], columns)
        for slot in range(len(offsets)):
            low, high = outs[2 * slot : 2 * slot + 2]
            for k, (target, index) in enumerate(((low, 0), (low, 1), (high, 0))):
                at = (slot * 3 + k) * part
                target[index, :, columns] = conv[at : at + part, :].astype(low.dtype)

    @pl.loop(0, channels // step)
    def _(j):
        columns = pl.ds(pl.multiple_of(j * step, step), step)
        after = pl.ds(pl.multiple_of(channels + j * step, step), step)
        mix_g = product(mix_rows, lambda m, at: gs[m][:, at], columns)
        mix_s = product(mix_rows, lambda m, at: skip[m, :, at], columns)
        for slot in range(len(offsets)):
            high = outs[2 * slot + 1]
            here = slice(slot * part, (slot + 1) * part)
            high[1, :, columns] = mix_g[here, :].astype(high.dtype)
            high[1, :, after] = mix_s[here, :].astype(high.dtype)


def term_call(replicas, offsets, kind, taps_t, skip, hid_t, pre_grads, gs, tokens):
    micro, samples, channels = skip.shape
    part = channels // replicas
    inputs = in_vmem(taps_t, skip, *hid_t, *pre_grads, *gs, *tokens)
    outs = 2 * len(offsets)
    return pl.pallas_call(
        functools.partial(term_kernel, replicas, offsets, micro),
        out_shape=[pltpu.VMEM((2, part, 2 * channels), kind)] * outs,
        in_specs=[VMEM] * len(inputs),
        out_specs=[VMEM] * outs,
        compiler_params=PARAMS,
        cost_estimate=cost(2**29 * len(offsets), 2**20),
    )(*inputs)


def add_kernel(mine_r, mine_l, got_r, got_l, *refs):
    out_r, out_l = refs[-2:]
    out_r[...] = (mine_r[...].astype(F32) + got_r[...].astype(F32)).astype(BF16)
    out_l[...] = (mine_l[...].astype(F32) + got_l[...].astype(F32)).astype(BF16)


def add_call(mine, got, tokens):
    inputs = in_vmem(*mine, *got, *tokens)
    return pl.pallas_call(
        add_kernel,
        out_shape=[pltpu.VMEM(got[0].shape, BF16)] * 2,
        in_specs=[VMEM] * len(inputs),
        out_specs=[VMEM] * 2,
        compiler_params=PARAMS,
        cost_estimate=cost(2**18, 2**19),
    )(*inputs)


def final_kernel(low, high, low_r, low_l, high_r, high_l, conv, mix):
    conv[0:2] = low[...] + (low_r[...].astype(F32) + low_l[...].astype(F32))
    total = high[...] + (high_r[...].astype(F32) + high_l[...].astype(F32))
    conv[2] = total[0]
    mix[...] = total[1]


def final_call(*blocks):
    part, wide = blocks[0].shape[1:]
    return pl.pallas_call(
        final_kernel,
        out_shape=[jax.ShapeDtypeStruct((3, part, wide), F32), jax.ShapeDtypeStruct((part, wide), F32)],
        in_specs=[VMEM] * 6,
        out_specs=[VMEM] * 2,
        compiler_params=PARAMS,
        cost_estimate=cost(2**19, 2**20),
    )(*in_vmem(*blocks))


def local(x_ckpt, top_cot, skip_cot, w_conv, w_mix):
    sections = lax.axis_size("pipe")
    replicas = lax.axis_size("dp")
    micro, seqs, samples, channels = x_ckpt.shape[1:]
    block = seqs * samples
    half = replicas // 2
    right, left = ring_pairs(replicas)

    def send(to_right, to_left):
        return lax.ppermute(to_right, "dp", right), lax.ppermute(to_left, "dp", left)

    taps_t = prepare_call(x_ckpt[0].reshape(micro * seqs, samples, channels))
    low, high = split_call(w_conv[0].transpose(1, 0, 2), w_mix)
    streams = {0: (low, low), 2: (high, high)}
    held = partial_call(replicas, ((0, 0), (0, 2)), taps_t, [low, high], [])
    skip = skip_cot.reshape(micro, block, channels)
    for step in range(1, half):
        last = step == half - 1
        for first, (to_right, to_left) in streams.items():
            got = send(to_right, to_left)
            items = ((-step, first), (step, first))
            if last and first:
                blocks = send(got[0][:1], got[1][1:])
                items += ((half, 0), (half, 1))
                held = partial_call(replicas, items, taps_t, [*got, *ahead], held, None, (skip,))
                continue
            passing = "quarters" if last else "whole"
            *held, to_right, to_left = partial_call(replicas, items, taps_t, got, held, passing)
            streams[first] = (to_right, to_left)
            if last:
                ahead = send(to_right, to_left)
    acc, w_full = held

    g = list(top_cot.reshape(micro, block, channels))
    padding = max(16, 2 * 2 ** (sections - 1))
    hid_t, held, ready = [], [()] * micro, []
    for m in range(micro):
        a1, a2, hid, *stored = forward_call(
            replicas, m, micro, m == 0, taps_t, acc, w_full, blocks
        )
        if stored:
            w_full = stored[0]
        hid_t.append(hid)
        ready.append((a1, a2))
    last = sections - 1
    g = [[piece, piece] for piece in g]
    for m in range(micro):
        held[m] = chain_call(last, m, (1, 0), padding, g[m][0], skip, *ready[m], w_full, (), ())
        g[m] = [lax.ppermute(held[m][1], "pipe", [(last, last - 1)])] * 2
    for stage in range(last - 1, -1, -1):
        piece = None
        for m in range(micro):
            carried = () if piece is None else (piece,)
            for half_at in (1, 0):
                out = chain_call(
                    stage, m, (half_at,), padding, g[m][half_at], skip, *ready[m], w_full, carried, held[m]
                )
                held[m], carried = out[:3], out[-1:]
                piece = out[3] if stage else out[1]
                if stage:
                    g[m][half_at] = lax.ppermute(piece, "pipe", [(stage, stage - 1)])
    pre_grads, cots, gs = zip(*held)
    cot = jnp.stack(cots, axis=0)

    def terms(dist, tokens, kind=BF16):
        offsets = (dist,) if dist in (0, half) else (dist, -dist)
        return term_call(replicas, offsets, kind, taps_t, skip, hid_t, pre_grads, gs, tokens)

    low, high = terms(half, ())
    got_one = send(low, high)
    mine = terms(half - 1, (low,))
    got_two = send(mine[1], mine[2])
    token = ()
    for dist in range(half - 1, 0, -1):
        if dist < half - 1:
            out = add_call((mine[1], mine[2]), got_two, token)
            token = out[:1]
            got_two = send(*out)
        out = add_call((mine[0], mine[3]), got_one, token)
        token = out[:1]
        got_one = send(*out)
        if dist > 1:
            mine = terms(dist - 1, token)
    low, high = terms(0, token, F32)
    share_conv, share_mix = final_call(low, high, got_one[0], got_two[1], got_two[0], got_one[1])
    return (
        cot.reshape(1, micro, seqs, samples, channels),
        share_conv.transpose(1, 0, 2)[None],
        share_mix[None],
    )


def solution(mesh):
    placed = (
        P("pipe", None, "dp", None, None),
        P(None, "dp", None, None),
        P(None, "dp", None, None),
        P("pipe", "dp", None, None),
        P("pipe", "dp", None),
    )
    return jax.shard_map(
        local,
        mesh=mesh,
        in_specs=placed,
        out_specs=(
            P("pipe", None, "dp", None, None),
            P("pipe", "dp", None, None),
            P("pipe", "dp", None),
        ),
        check_vma=False,
    )
```

```python
import functools

import jax
import jax.numpy as jnp
from jax import lax
from jax.experimental import pallas as pl
from jax.experimental.pallas import tpu as pltpu
from jax.sharding import PartitionSpec as P

F32 = jnp.float32
BF16 = jnp.bfloat16
NT = (((1,), (1,)), ((), ()))
TN = (((0,), (0,)), ((), ()))
VMEM = pl.BlockSpec(memory_space=pltpu.VMEM)
PARAMS = pltpu.CompilerParams(vmem_limit_bytes=24 * 2**20)


def ring_pairs(count):
    order = list(range(0, count, 2)) + list(range(count - 1 - count % 2, 0, -2))
    right = [(order[i], order[(i + 1) % count]) for i in range(count)]
    return right, [(b, a) for a, b in right]


def in_vmem(*arrays):
    return [pltpu.with_memory_space_constraint(array, pltpu.VMEM) for array in arrays]


def cost(flops, moved):
    return pl.CostEstimate(flops=flops, bytes_accessed=moved, transcendentals=0)


def owner_row(replicas, part, offset):
    replica = lax.axis_index("dp")
    step = replica // 2
    place = jnp.where(lax.rem(replica, 2) == 0, step, replicas - 1 - step)
    at = lax.rem(place + (offset + replicas), replicas)
    owner = jnp.where(at < replicas // 2, 2 * at, 2 * (replicas - 1 - at) + 1)
    return pl.multiple_of(owner * part, part)


def prepare_kernel(x, taps_t):
    seqs, samples, channels = x.shape
    dilation = jnp.left_shift(jnp.int32(1), lax.axis_index("pipe"))
    wide = 128
    for s in range(seqs):
        columns = slice(s * samples, (s + 1) * samples)
        for at in range(0, channels, wide):
            turned = x[s, :, at : at + wide].astype(F32).T
            position = lax.broadcasted_iota(jnp.int32, turned.shape, 1)
            taps_t[at : at + wide, columns] = turned.astype(BF16)
            for k in (1, 2):
                delayed = jnp.where(position >= k * dilation, pltpu.roll(turned, k * dilation, 1), 0.0)
                taps_t[k * channels + at : k * channels + at + wide, columns] = delayed.astype(BF16)


def prepare_call(x):
    seqs, samples, channels = x.shape
    return pl.pallas_call(
        prepare_kernel,
        out_shape=pltpu.VMEM((3 * channels, seqs * samples), BF16),
        in_specs=[VMEM],
        out_specs=VMEM,
        compiler_params=PARAMS,
        cost_estimate=cost(2**20, 2**22),
    )(x)


def tap_rows(taps_t, row, part, columns):
    channels = taps_t.shape[0] // 3
    return jnp.concatenate([taps_t[pl.ds(k * channels + row, part), columns] for k in range(3)], axis=0)


def place_rows(replicas, items, blocks):
    part = blocks[0].shape[1]
    return [(owner_row(replicas, part, offset), first, block) for (offset, first), block in zip(items, blocks)]


def shard_term(taps_t, columns, placed):
    channels = taps_t.shape[0] // 3
    part, wide = placed[0][2].shape[1:]
    rows, weights = [], []
    for row, first, block in placed:
        count = min(block.shape[0], 3 - first)
        if count == 0:
            continue
        rows += [taps_t[pl.ds((first + k) * channels + row, part), columns] for k in range(count)]
        weights.append(block[:count].reshape(count * part, wide))
    if not rows:
        return None
    return lax.dot_general(
        jnp.concatenate(rows, axis=0), jnp.concatenate(weights, axis=0), TN, preferred_element_type=F32
    )


def store_shards(w, placed):
    channels = w.shape[0] // 4
    for row, first, block in placed:
        for k in range(block.shape[0]):
            w[pl.ds((first + k) * channels + row, block.shape[1]), :] = block[k]


def partial_kernel(replicas, items, first, passing, tokens, taps_t, *refs):
    count = len(items)
    blocks = refs[:count]
    placed = place_rows(replicas, items, blocks)
    refs = refs[count:]
    acc, w, *passed = refs if first else refs[2 + tokens :]
    rows = taps_t.shape[1]
    chunk = min(256, rows)
    for at in range(0, rows, chunk):
        columns = slice(at, at + chunk)
        term = shard_term(taps_t, columns, placed)
        if term is not None:
            acc[columns, :] = term if first else refs[0][columns, :] + term
    store_shards(w, placed)
    if passing == "quarters":
        passed[0][...] = blocks[0][0:1]
        passed[1][...] = blocks[1][1:2]
    if passing == "low":
        for out, block in zip(passed, blocks):
            out[...] = block[0:2]
    if passing == "high":
        for out, conv, block in zip(passed, refs[2 : 2 + tokens], blocks):
            out[0] = conv[2]
            out[1] = block[0]


def partial_call(replicas, items, taps_t, blocks, held, passing=None, tokens=()):
    part, wide = blocks[0].shape[1:]
    rows = taps_t.shape[1]
    count = len(items)
    inputs = in_vmem(taps_t, *blocks, *held, *tokens)
    aliases = {1 + count + i: i for i in range(len(held))}
    if passing == "whole":
        aliases |= {1 + i: 2 + i for i in range(count)}
    return pl.pallas_call(
        functools.partial(partial_kernel, replicas, items, not held, passing, len(tokens)),
        out_shape=[pltpu.VMEM((rows, wide), F32), pltpu.VMEM((2 * wide, wide), BF16)]
        + [pltpu.VMEM((1 if passing == "quarters" else 2, part, wide), BF16) for _ in blocks if passing],
        in_specs=[VMEM] * len(inputs),
        out_specs=[VMEM] * (2 + count if passing else 2),
        input_output_aliases=aliases,
        compiler_params=PARAMS,
        cost_estimate=cost(3 * rows * part * count * wide, 2**20),
    )(*inputs)


def forward_kernel(replicas, index, store, taps_t, acc, w_in, *refs):
    blocks, refs = refs[:2], refs[2:]
    a1, a2, hid_t = refs[:3]
    samples, channels = a1.shape
    placed = place_rows(replicas, [(replicas // 2, k) for k in (2, 3)], blocks)
    chunk = min(256, samples)
    for at in range(0, samples, chunk):
        columns = slice(index * samples + at, index * samples + at + chunk)
        pre = acc[columns, :] + shard_term(taps_t, columns, placed)
        filt = jnp.tanh(pre[:, :channels])
        gate = jax.nn.sigmoid(pre[:, channels:])
        a1[at : at + chunk, :] = (gate * (1.0 - filt * filt)).astype(BF16)
        a2[at : at + chunk, :] = (filt * gate * (1.0 - gate)).astype(BF16)
        hid_t[:, at : at + chunk] = (filt * gate).T.astype(BF16)
    if store:
        store_shards(refs[3], placed)


def forward_call(replicas, index, micro, store, taps_t, acc, w, blocks):
    rows, wide = acc.shape
    channels = wide // 2
    samples = rows // micro
    inputs = in_vmem(taps_t, acc, w, *blocks)
    return pl.pallas_call(
        functools.partial(forward_kernel, replicas, index, store),
        out_shape=[pltpu.VMEM((samples, channels), BF16)] * 2
        + [pltpu.VMEM((channels, samples), BF16)]
        + ([pltpu.VMEM(w.shape, BF16)] if store else []),
        in_specs=[VMEM] * len(inputs),
        out_specs=[VMEM] * (4 if store else 3),
        input_output_aliases={2: 3} if store else {},
        compiler_params=PARAMS,
        cost_estimate=cost(2**28, 2**22),
    )(*inputs)


def chain_kernel(stage, index, halves, padding, before, held, g, skip, a1, a2, w, *refs):
    bt = refs[-1]
    carried = refs[0] if halves == (0,) else None
    pg, ig, gk, *extra = refs[before + held : -1]
    samples, channels = gk.shape
    chunk = samples // 2
    base = min(halves) * chunk
    count = len(halves) * chunk
    dilation = 2**stage
    g_base = base if g.shape[0] == samples else 0

    @pl.when(lax.axis_index("pipe") == stage)
    def _():
        for k in (1, 2):
            bt[k, count:, :] = jnp.zeros((padding, channels), F32) if carried is None else carried[k - 1]
        for half in halves:
            at = half * chunk
            rows = slice(at, at + chunk)
            here = slice(at - base, at - base + chunk)
            g_rows = slice(at - base + g_base, at - base + g_base + chunk)
            hid = lax.dot_general(
                g[g_rows, :], w[3 * channels :, :channels], NT, preferred_element_type=F32
            ) + lax.dot_general(
                skip[index, rows, :], w[3 * channels :, channels:], NT, preferred_element_type=F32
            )
            pg[rows, :channels] = (hid * a1[rows, :].astype(F32)).astype(BF16)
            pg[rows, channels:] = (hid * a2[rows, :].astype(F32)).astype(BF16)
            for k in range(3):
                bt[k, here, :] = lax.dot_general(
                    pg[rows, :], w[k * channels : (k + 1) * channels, :], NT, preferred_element_type=F32
                )
            piece = 64
            for first in range(at - base + chunk - piece, at - base - 1, -piece):
                last = first + piece
                total = g[first + g_base : last + g_base, :].astype(F32) + bt[0, first:last, :]
                total = total + bt[1, first + dilation : last + dilation, :]
                total = total + bt[2, first + 2 * dilation : last + 2 * dilation, :]
                ig[first + base : last + base, :] = total.astype(BF16)
                if len(halves) == 1 and stage:
                    extra[0][first:last, :] = total.astype(BF16)
            gk[rows, :] = g[g_rows, :]
        if halves == (1,):
            for k in (1, 2):
                extra[-1][k - 1] = bt[k, :padding, :]


def chain_call(stage, index, halves, padding, g, skip, a1, a2, w, carried, held):
    samples, channels = a1.shape
    chunk = samples // 2
    tile = pltpu.VMEM((samples, channels), BF16)
    outs = [pltpu.VMEM((samples, 2 * channels), BF16), tile, tile]
    if len(halves) == 1 and stage:
        outs.append(pltpu.VMEM((chunk, channels), BF16))
    if halves == (1,):
        outs.append(pltpu.VMEM((2, padding, channels), F32))
    inputs = in_vmem(g, skip, a1, a2, w, *carried, *held)
    return pl.pallas_call(
        functools.partial(chain_kernel, stage, index, halves, padding, len(carried), len(held)),
        out_shape=outs,
        in_specs=[VMEM] * len(inputs),
        out_specs=[VMEM] * len(outs),
        scratch_shapes=[pltpu.VMEM((3, len(halves) * chunk + padding, channels), F32)],
        input_output_aliases={len(inputs) - len(held) + i: i for i in range(len(held))},
        compiler_params=PARAMS,
        cost_estimate=cost(8 * len(halves) * chunk * channels * channels, 2**22),
    )(*inputs)


def term_kernel(replicas, offsets, micro, taps_t, skip, *refs):
    hids, refs = refs[:micro], refs[micro:]
    pgs, refs = refs[:micro], refs[micro:]
    gs, refs = refs[:micro], refs[micro:]
    outs = refs[-2 * len(offsets) :]
    samples, wide = pgs[0].shape
    channels = wide // 2
    part = channels // replicas
    places = [owner_row(replicas, part, offset) for offset in offsets]
    step = min(256, channels)

    def product(rows_of, right, columns):
        total = None
        for m in range(micro):
            new = jnp.dot(rows_of(m), right(m, columns), preferred_element_type=F32)
            total = new if total is None else total + new
        return total

    def conv_rows(m):
        here = slice(m * samples, (m + 1) * samples)
        return jnp.concatenate([tap_rows(taps_t, row, part, here) for row in places], axis=0)

    def mix_rows(m):
        return jnp.concatenate([hids[m][pl.ds(row, part), :] for row in places], axis=0)

    unroll = offsets == (replicas // 2,)

    @pl.loop(0, wide // step, unroll=unroll)
    def _(j):
        columns = pl.ds(pl.multiple_of(j * step, step), step)
        conv = product(conv_rows, lambda m, at: pgs[m][:, at], columns)
        for slot in range(len(offsets)):
            low, high = outs[2 * slot : 2 * slot + 2]
            for k, (target, index) in enumerate(((low, 0), (low, 1), (high, 0))):
                at = (slot * 3 + k) * part
                target[index, :, columns] = conv[at : at + part, :].astype(low.dtype)

    @pl.loop(0, channels // step, unroll=unroll)
    def _(j):
        columns = pl.ds(pl.multiple_of(j * step, step), step)
        after = pl.ds(pl.multiple_of(channels + j * step, step), step)
        mix_g = product(mix_rows, lambda m, at: gs[m][:, at], columns)
        mix_s = product(mix_rows, lambda m, at: skip[m, :, at], columns)
        for slot in range(len(offsets)):
            high = outs[2 * slot + 1]
            here = slice(slot * part, (slot + 1) * part)
            high[1, :, columns] = mix_g[here, :].astype(high.dtype)
            high[1, :, after] = mix_s[here, :].astype(high.dtype)


def term_call(replicas, offsets, kind, taps_t, skip, hid_t, pre_grads, gs, tokens):
    micro, samples, channels = skip.shape
    part = channels // replicas
    inputs = in_vmem(taps_t, skip, *hid_t, *pre_grads, *gs, *tokens)
    outs = 2 * len(offsets)
    return pl.pallas_call(
        functools.partial(term_kernel, replicas, offsets, micro),
        out_shape=[pltpu.VMEM((2, part, 2 * channels), kind)] * outs,
        in_specs=[VMEM] * len(inputs),
        out_specs=[VMEM] * outs,
        compiler_params=PARAMS,
        cost_estimate=cost(2**29 * len(offsets), 2**20),
    )(*inputs)


def add_kernel(mine_r, mine_l, got_r, got_l, *refs):
    out_r, out_l = refs[-2:]
    out_r[...] = (mine_r[...].astype(F32) + got_r[...].astype(F32)).astype(BF16)
    out_l[...] = (mine_l[...].astype(F32) + got_l[...].astype(F32)).astype(BF16)


def add_call(mine, got, tokens):
    inputs = in_vmem(*mine, *got, *tokens)
    return pl.pallas_call(
        add_kernel,
        out_shape=[pltpu.VMEM(got[0].shape, BF16)] * 2,
        in_specs=[VMEM] * len(inputs),
        out_specs=[VMEM] * 2,
        compiler_params=PARAMS,
        cost_estimate=cost(2**18, 2**19),
    )(*inputs)


def final_kernel(low, high, low_r, low_l, high_r, high_l, conv, mix):
    conv[0:2] = low[...] + (low_r[...].astype(F32) + low_l[...].astype(F32))
    total = high[...] + (high_r[...].astype(F32) + high_l[...].astype(F32))
    conv[2] = total[0]
    mix[...] = total[1]


def final_call(*blocks):
    part, wide = blocks[0].shape[1:]
    return pl.pallas_call(
        final_kernel,
        out_shape=[jax.ShapeDtypeStruct((3, part, wide), F32), jax.ShapeDtypeStruct((part, wide), F32)],
        in_specs=[VMEM] * 6,
        out_specs=[VMEM] * 2,
        compiler_params=PARAMS,
        cost_estimate=cost(2**19, 2**20),
    )(*in_vmem(*blocks))


def local(x_ckpt, top_cot, skip_cot, w_conv, w_mix):
    sections = lax.axis_size("pipe")
    replicas = lax.axis_size("dp")
    micro, seqs, samples, channels = x_ckpt.shape[1:]
    block = seqs * samples
    half = replicas // 2
    right, left = ring_pairs(replicas)

    def send(to_right, to_left):
        return lax.ppermute(to_right, "dp", right), lax.ppermute(to_left, "dp", left)

    taps_t = prepare_call(x_ckpt[0].reshape(micro * seqs, samples, channels))
    conv = w_conv[0].transpose(1, 0, 2)
    held = partial_call(replicas, ((0, 0), (0, 3)), taps_t, [conv, w_mix], [])
    convs, mixes = send(conv, conv), send(w_mix, w_mix)
    *held, low_r, low_l = partial_call(replicas, ((-1, 0), (1, 0)), taps_t, convs, held, "low")
    *held, high_r, high_l = partial_call(replicas, ((-1, 3), (1, 3)), taps_t, mixes, held, "high", convs)
    streams = {0: (low_r, low_l), 2: (high_r, high_l)}
    skip = skip_cot.reshape(micro, block, channels)
    for step in range(2, half):
        last = step == half - 1
        for first, (to_right, to_left) in streams.items():
            got = send(to_right, to_left)
            items = ((-step, first), (step, first))
            if last and first:
                blocks = send(got[0][:1], got[1][1:])
                items += ((half, 0), (half, 1))
                held = partial_call(replicas, items, taps_t, [*got, *ahead], held, None, (skip,))
                continue
            passing = "quarters" if last else "whole"
            *held, to_right, to_left = partial_call(replicas, items, taps_t, got, held, passing)
            streams[first] = (to_right, to_left)
            if last:
                ahead = send(to_right, to_left)
    acc, w_full = held

    g = list(top_cot.reshape(micro, block, channels))
    padding = max(16, 2 * 2 ** (sections - 1))
    hid_t, held, ready = [], [()] * micro, []
    for m in range(micro):
        a1, a2, hid, *stored = forward_call(
            replicas, m, micro, m == 0, taps_t, acc, w_full, blocks
        )
        if stored:
            w_full = stored[0]
        hid_t.append(hid)
        ready.append((a1, a2))
    last = sections - 1
    g = [[piece, piece] for piece in g]
    for m in range(micro):
        held[m] = chain_call(last, m, (1, 0), padding, g[m][0], skip, *ready[m], w_full, (), ())
        g[m] = [lax.ppermute(held[m][1], "pipe", [(last, last - 1)])] * 2
    for stage in range(last - 1, -1, -1):
        piece = None
        for m in range(micro):
            carried = () if piece is None else (piece,)
            for half_at in (1, 0):
                out = chain_call(
                    stage, m, (half_at,), padding, g[m][half_at], skip, *ready[m], w_full, carried, held[m]
                )
                held[m], carried = out[:3], out[-1:]
                piece = out[3] if stage else out[1]
                if stage:
                    g[m][half_at] = lax.ppermute(piece, "pipe", [(stage, stage - 1)])
    pre_grads, cots, gs = zip(*held)
    cot = jnp.stack(cots, axis=0)

    def terms(dist, tokens, kind=BF16):
        offsets = (dist,) if dist in (0, half) else (dist, -dist)
        return term_call(replicas, offsets, kind, taps_t, skip, hid_t, pre_grads, gs, tokens)

    low, high = terms(half, ())
    got_one = send(low, high)
    mine = terms(half - 1, (low,))
    got_two = send(mine[1], mine[2])
    token = ()
    for dist in range(half - 1, 0, -1):
        if dist < half - 1:
            out = add_call((mine[1], mine[2]), got_two, token)
            token = out[:1]
            got_two = send(*out)
        out = add_call((mine[0], mine[3]), got_one, token)
        token = out[:1]
        got_one = send(*out)
        if dist > 1:
            mine = terms(dist - 1, token)
    low, high = terms(0, token, F32)
    share_conv, share_mix = final_call(low, high, got_one[0], got_two[1], got_two[0], got_one[1])
    return (
        cot.reshape(1, micro, seqs, samples, channels),
        share_conv.transpose(1, 0, 2)[None],
        share_mix[None],
    )


def solution(mesh):
    placed = (
        P("pipe", None, "dp", None, None),
        P(None, "dp", None, None),
        P(None, "dp", None, None),
        P("pipe", "dp", None, None),
        P("pipe", "dp", None),
    )
    return jax.shard_map(
        local,
        mesh=mesh,
        in_specs=placed,
        out_specs=(
            P("pipe", None, "dp", None, None),
            P("pipe", "dp", None, None),
            P("pipe", "dp", None),
        ),
        check_vma=False,
    )
```

```python
import functools

import jax
import jax.numpy as jnp
from jax import lax
from jax.experimental import pallas as pl
from jax.experimental.pallas import tpu as pltpu
from jax.sharding import PartitionSpec as P

F32 = jnp.float32
BF16 = jnp.bfloat16
NT = (((1,), (1,)), ((), ()))
TN = (((0,), (0,)), ((), ()))
VMEM = pl.BlockSpec(memory_space=pltpu.VMEM)
PARAMS = pltpu.CompilerParams(vmem_limit_bytes=24 * 2**20)


def ring_pairs(count):
    order = list(range(0, count, 2)) + list(range(count - 1 - count % 2, 0, -2))
    right = [(order[i], order[(i + 1) % count]) for i in range(count)]
    return right, [(b, a) for a, b in right]


def in_vmem(*arrays):
    return [pltpu.with_memory_space_constraint(array, pltpu.VMEM) for array in arrays]


def cost(flops, moved):
    return pl.CostEstimate(flops=flops, bytes_accessed=moved, transcendentals=0)


def owner_row(replicas, part, offset):
    replica = lax.axis_index("dp")
    step = replica // 2
    place = jnp.where(lax.rem(replica, 2) == 0, step, replicas - 1 - step)
    at = lax.rem(place + (offset + replicas), replicas)
    owner = jnp.where(at < replicas // 2, 2 * at, 2 * (replicas - 1 - at) + 1)
    return pl.multiple_of(owner * part, part)


def split_kernel(conv, mix, low, high, sems):
    copies = [
        pltpu.make_async_copy(conv.at[0:2], low, sems.at[0]),
        pltpu.make_async_copy(conv.at[2], high.at[0], sems.at[1]),
        pltpu.make_async_copy(mix.at[0], high.at[1], sems.at[2]),
    ]
    for copy in copies:
        copy.start()
    for copy in copies:
        copy.wait()


def split_call(conv, mix):
    anywhere = pl.BlockSpec(memory_space=pl.ANY)
    return pl.pallas_call(
        split_kernel,
        out_shape=[pltpu.VMEM((2, *conv.shape[1:]), BF16)] * 2,
        in_specs=[anywhere] * 2,
        out_specs=[VMEM] * 2,
        scratch_shapes=[pltpu.SemaphoreType.DMA((3,))],
        compiler_params=PARAMS,
        cost_estimate=cost(0, 2**20),
    )(*[pltpu.with_memory_space_constraint(array, pltpu.HBM) for array in (conv, mix)])


def prepare_kernel(x, taps_t):
    seqs, samples, channels = x.shape
    dilation = jnp.left_shift(jnp.int32(1), lax.axis_index("pipe"))
    wide = 128
    for s in range(seqs):
        columns = slice(s * samples, (s + 1) * samples)
        for at in range(0, channels, wide):
            turned = x[s, :, at : at + wide].astype(F32).T
            position = lax.broadcasted_iota(jnp.int32, turned.shape, 1)
            taps_t[at : at + wide, columns] = turned.astype(BF16)
            for k in (1, 2):
                delayed = jnp.where(position >= k * dilation, pltpu.roll(turned, k * dilation, 1), 0.0)
                taps_t[k * channels + at : k * channels + at + wide, columns] = delayed.astype(BF16)


def prepare_call(x):
    seqs, samples, channels = x.shape
    return pl.pallas_call(
        prepare_kernel,
        out_shape=pltpu.VMEM((3 * channels, seqs * samples), BF16),
        in_specs=[VMEM],
        out_specs=VMEM,
        compiler_params=PARAMS,
        cost_estimate=cost(2**20, 2**22),
    )(x)


def tap_rows(taps_t, row, part, columns):
    channels = taps_t.shape[0] // 3
    return jnp.concatenate([taps_t[pl.ds(k * channels + row, part), columns] for k in range(3)], axis=0)


def place_rows(replicas, items, blocks):
    part = blocks[0].shape[1]
    return [(owner_row(replicas, part, offset), first, block) for (offset, first), block in zip(items, blocks)]


def shard_term(taps_t, columns, placed):
    channels = taps_t.shape[0] // 3
    part, wide = placed[0][2].shape[1:]
    rows, weights = [], []
    for row, first, block in placed:
        count = min(block.shape[0], 3 - first)
        if count == 0:
            continue
        rows += [taps_t[pl.ds((first + k) * channels + row, part), columns] for k in range(count)]
        weights.append(block[:count].reshape(count * part, wide))
    return lax.dot_general(
        jnp.concatenate(rows, axis=0), jnp.concatenate(weights, axis=0), TN, preferred_element_type=F32
    )


def store_shards(w, placed):
    channels = w.shape[0] // 4
    for row, first, block in placed:
        for k in range(block.shape[0]):
            w[pl.ds((first + k) * channels + row, block.shape[1]), :] = block[k]


def partial_kernel(replicas, items, first, quarters, tokens, taps_t, *refs):
    count = len(items)
    blocks = refs[:count]
    placed = place_rows(replicas, items, blocks)
    refs = refs[count:]
    acc, w, *passed = refs if first else refs[2 + tokens :]
    rows = taps_t.shape[1]
    chunk = min(256, rows)
    for at in range(0, rows, chunk):
        columns = slice(at, at + chunk)
        term = shard_term(taps_t, columns, placed)
        acc[columns, :] = term if first else refs[0][columns, :] + term
    store_shards(w, placed)
    if quarters:
        passed[0][...] = blocks[0][0:1]
        passed[1][...] = blocks[1][1:2]


def partial_call(replicas, items, taps_t, blocks, held, passing=None, tokens=()):
    part, wide = blocks[0].shape[1:]
    rows = taps_t.shape[1]
    count = len(items)
    inputs = in_vmem(taps_t, *blocks, *held, *tokens)
    aliases = {1 + count + i: i for i in range(len(held))}
    if passing == "whole":
        aliases |= {1 + i: 2 + i for i in range(count)}
    return pl.pallas_call(
        functools.partial(partial_kernel, replicas, items, not held, passing == "quarters", len(tokens)),
        out_shape=[pltpu.VMEM((rows, wide), F32), pltpu.VMEM((2 * wide, wide), BF16)]
        + [pltpu.VMEM((2 if passing == "whole" else 1, part, wide), BF16) for _ in blocks if passing],
        in_specs=[VMEM] * len(inputs),
        out_specs=[VMEM] * (2 + count if passing else 2),
        input_output_aliases=aliases,
        compiler_params=PARAMS,
        cost_estimate=cost(3 * rows * part * count * wide, 2**20),
    )(*inputs)


def forward_kernel(replicas, index, store, taps_t, acc, w_in, *refs):
    blocks, refs = refs[:2], refs[2:]
    a1, a2, hid_t = refs[:3]
    samples, channels = a1.shape
    placed = place_rows(replicas, [(replicas // 2, k) for k in (2, 3)], blocks)
    chunk = min(256, samples)
    for at in range(0, samples, chunk):
        columns = slice(index * samples + at, index * samples + at + chunk)
        pre = acc[columns, :] + shard_term(taps_t, columns, placed)
        filt = jnp.tanh(pre[:, :channels])
        gate = jax.nn.sigmoid(pre[:, channels:])
        a1[at : at + chunk, :] = (gate * (1.0 - filt * filt)).astype(BF16)
        a2[at : at + chunk, :] = (filt * gate * (1.0 - gate)).astype(BF16)
        hid_t[:, at : at + chunk] = (filt * gate).T.astype(BF16)
    if store:
        store_shards(refs[3], placed)


def forward_call(replicas, index, micro, store, taps_t, acc, w, blocks):
    rows, wide = acc.shape
    channels = wide // 2
    samples = rows // micro
    inputs = in_vmem(taps_t, acc, w, *blocks)
    return pl.pallas_call(
        functools.partial(forward_kernel, replicas, index, store),
        out_shape=[pltpu.VMEM((samples, channels), BF16)] * 2
        + [pltpu.VMEM((channels, samples), BF16)]
        + ([pltpu.VMEM(w.shape, BF16)] if store else []),
        in_specs=[VMEM] * len(inputs),
        out_specs=[VMEM] * (4 if store else 3),
        input_output_aliases={2: 3} if store else {},
        compiler_params=PARAMS,
        cost_estimate=cost(2**28, 2**22),
    )(*inputs)


def chain_kernel(stage, index, halves, padding, before, held, g, skip, a1, a2, w, *refs):
    bt = refs[-1]
    carried = refs[0] if halves == (0,) else None
    pg, ig, gk, *extra = refs[before + held : -1]
    samples, channels = gk.shape
    chunk = samples // 2
    base = min(halves) * chunk
    count = len(halves) * chunk
    dilation = 2**stage
    g_base = base if g.shape[0] == samples else 0

    @pl.when(lax.axis_index("pipe") == stage)
    def _():
        for k in (1, 2):
            bt[k, count:, :] = jnp.zeros((padding, channels), F32) if carried is None else carried[k - 1]
        for half in halves:
            at = half * chunk
            rows = slice(at, at + chunk)
            here = slice(at - base, at - base + chunk)
            g_rows = slice(at - base + g_base, at - base + g_base + chunk)
            hid = lax.dot_general(
                g[g_rows, :], w[3 * channels :, :channels], NT, preferred_element_type=F32
            ) + lax.dot_general(
                skip[index, rows, :], w[3 * channels :, channels:], NT, preferred_element_type=F32
            )
            pg[rows, :channels] = (hid * a1[rows, :].astype(F32)).astype(BF16)
            pg[rows, channels:] = (hid * a2[rows, :].astype(F32)).astype(BF16)
            for k in range(3):
                bt[k, here, :] = lax.dot_general(
                    pg[rows, :], w[k * channels : (k + 1) * channels, :], NT, preferred_element_type=F32
                )
            piece = 64
            for first in range(at - base + chunk - piece, at - base - 1, -piece):
                last = first + piece
                total = g[first + g_base : last + g_base, :].astype(F32) + bt[0, first:last, :]
                total = total + bt[1, first + dilation : last + dilation, :]
                total = total + bt[2, first + 2 * dilation : last + 2 * dilation, :]
                ig[first + base : last + base, :] = total.astype(BF16)
                if len(halves) == 1 and stage:
                    extra[0][first:last, :] = total.astype(BF16)
            gk[rows, :] = g[g_rows, :]
        if halves == (1,):
            for k in (1, 2):
                extra[-1][k - 1] = bt[k, :padding, :]


def chain_call(stage, index, halves, padding, g, skip, a1, a2, w, carried, held):
    samples, channels = a1.shape
    chunk = samples // 2
    tile = pltpu.VMEM((samples, channels), BF16)
    outs = [pltpu.VMEM((samples, 2 * channels), BF16), tile, tile]
    if len(halves) == 1 and stage:
        outs.append(pltpu.VMEM((chunk, channels), BF16))
    if halves == (1,):
        outs.append(pltpu.VMEM((2, padding, channels), F32))
    inputs = in_vmem(g, skip, a1, a2, w, *carried, *held)
    return pl.pallas_call(
        functools.partial(chain_kernel, stage, index, halves, padding, len(carried), len(held)),
        out_shape=outs,
        in_specs=[VMEM] * len(inputs),
        out_specs=[VMEM] * len(outs),
        scratch_shapes=[pltpu.VMEM((3, len(halves) * chunk + padding, channels), F32)],
        input_output_aliases={len(inputs) - len(held) + i: i for i in range(len(held))},
        compiler_params=PARAMS,
        cost_estimate=cost(8 * len(halves) * chunk * channels * channels, 2**22),
    )(*inputs)


def term_kernel(replicas, offsets, micro, taps_t, skip, *refs):
    hids, refs = refs[:micro], refs[micro:]
    pgs, refs = refs[:micro], refs[micro:]
    gs, refs = refs[:micro], refs[micro:]
    outs = refs[-2 * len(offsets) :]
    samples, wide = pgs[0].shape
    channels = wide // 2
    part = channels // replicas
    places = [owner_row(replicas, part, offset) for offset in offsets]
    step = min(256, channels)

    def product(rows_of, right, columns):
        total = None
        for m in range(micro):
            new = jnp.dot(rows_of(m), right(m, columns), preferred_element_type=F32)
            total = new if total is None else total + new
        return total

    def conv_rows(m):
        here = slice(m * samples, (m + 1) * samples)
        return jnp.concatenate([tap_rows(taps_t, row, part, here) for row in places], axis=0)

    def mix_rows(m):
        return jnp.concatenate([hids[m][pl.ds(row, part), :] for row in places], axis=0)

    unroll = offsets == (replicas // 2,)

    @pl.loop(0, wide // step, unroll=unroll)
    def _(j):
        columns = pl.ds(pl.multiple_of(j * step, step), step)
        conv = product(conv_rows, lambda m, at: pgs[m][:, at], columns)
        for slot in range(len(offsets)):
            low, high = outs[2 * slot : 2 * slot + 2]
            for k, (target, index) in enumerate(((low, 0), (low, 1), (high, 0))):
                at = (slot * 3 + k) * part
                target[index, :, columns] = conv[at : at + part, :].astype(low.dtype)

    @pl.loop(0, channels // step, unroll=unroll)
    def _(j):
        columns = pl.ds(pl.multiple_of(j * step, step), step)
        after = pl.ds(pl.multiple_of(channels + j * step, step), step)
        mix_g = product(mix_rows, lambda m, at: gs[m][:, at], columns)
        mix_s = product(mix_rows, lambda m, at: skip[m, :, at], columns)
        for slot in range(len(offsets)):
            high = outs[2 * slot + 1]
            here = slice(slot * part, (slot + 1) * part)
            high[1, :, columns] = mix_g[here, :].astype(high.dtype)
            high[1, :, after] = mix_s[here, :].astype(high.dtype)


def term_call(replicas, offsets, kind, taps_t, skip, hid_t, pre_grads, gs, tokens):
    micro, samples, channels = skip.shape
    part = channels // replicas
    inputs = in_vmem(taps_t, skip, *hid_t, *pre_grads, *gs, *tokens)
    outs = 2 * len(offsets)
    return pl.pallas_call(
        functools.partial(term_kernel, replicas, offsets, micro),
        out_shape=[pltpu.VMEM((2, part, 2 * channels), kind)] * outs,
        in_specs=[VMEM] * len(inputs),
        out_specs=[VMEM] * outs,
        compiler_params=PARAMS,
        cost_estimate=cost(2**29 * len(offsets), 2**20),
    )(*inputs)


def add_kernel(mine_r, mine_l, got_r, got_l, *refs):
    out_r, out_l = refs[-2:]
    out_r[...] = (mine_r[...].astype(F32) + got_r[...].astype(F32)).astype(BF16)
    out_l[...] = (mine_l[...].astype(F32) + got_l[...].astype(F32)).astype(BF16)


def add_call(mine, got, tokens):
    inputs = in_vmem(*mine, *got, *tokens)
    return pl.pallas_call(
        add_kernel,
        out_shape=[pltpu.VMEM(got[0].shape, BF16)] * 2,
        in_specs=[VMEM] * len(inputs),
        out_specs=[VMEM] * 2,
        compiler_params=PARAMS,
        cost_estimate=cost(2**18, 2**19),
    )(*inputs)


def final_kernel(low, high, low_r, low_l, high_r, high_l, conv, mix):
    conv[0:2] = low[...] + (low_r[...].astype(F32) + low_l[...].astype(F32))
    total = high[...] + (high_r[...].astype(F32) + high_l[...].astype(F32))
    conv[2] = total[0]
    mix[...] = total[1]


def final_call(*blocks):
    part, wide = blocks[0].shape[1:]
    return pl.pallas_call(
        final_kernel,
        out_shape=[jax.ShapeDtypeStruct((3, part, wide), F32), jax.ShapeDtypeStruct((part, wide), F32)],
        in_specs=[VMEM] * 6,
        out_specs=[VMEM] * 2,
        compiler_params=PARAMS,
        cost_estimate=cost(2**19, 2**20),
    )(*in_vmem(*blocks))


def local(x_ckpt, top_cot, skip_cot, w_conv, w_mix):
    sections = lax.axis_size("pipe")
    replicas = lax.axis_size("dp")
    micro, seqs, samples, channels = x_ckpt.shape[1:]
    block = seqs * samples
    half = replicas // 2
    right, left = ring_pairs(replicas)

    def send(to_right, to_left):
        return lax.ppermute(to_right, "dp", right), lax.ppermute(to_left, "dp", left)

    taps_t = prepare_call(x_ckpt[0].reshape(micro * seqs, samples, channels))
    low, high = split_call(w_conv[0].transpose(1, 0, 2), w_mix)
    streams = {0: (low, low), 2: (high, high)}
    held = partial_call(replicas, ((0, 0), (0, 2)), taps_t, [low, high], [])
    skip = skip_cot.reshape(micro, block, channels)
    for step in range(1, half):
        last = step == half - 1
        for first, (to_right, to_left) in streams.items():
            got = send(to_right, to_left)
            items = ((-step, first), (step, first))
            if last and first:
                blocks = send(got[0][:1], got[1][1:])
                items += ((half, 0), (half, 1))
                held = partial_call(replicas, items, taps_t, [*got, *ahead], held, None, (skip,))
                continue
            passing = "quarters" if last else "whole"
            *held, to_right, to_left = partial_call(replicas, items, taps_t, got, held, passing)
            streams[first] = (to_right, to_left)
            if last:
                ahead = send(to_right, to_left)
    acc, w_full = held

    g = list(top_cot.reshape(micro, block, channels))
    padding = max(16, 2 * 2 ** (sections - 1))
    hid_t, held, ready = [], [()] * micro, []
    for m in range(micro):
        a1, a2, hid, *stored = forward_call(
            replicas, m, micro, m == 0, taps_t, acc, w_full, blocks
        )
        if stored:
            w_full = stored[0]
        hid_t.append(hid)
        ready.append((a1, a2))
    last = sections - 1
    g = [[piece, piece] for piece in g]
    for m in range(micro):
        held[m] = chain_call(last, m, (1, 0), padding, g[m][0], skip, *ready[m], w_full, (), ())
        g[m] = [lax.ppermute(held[m][1], "pipe", [(last, last - 1)])] * 2
    for stage in range(last - 1, -1, -1):
        piece = None
        for m in range(micro):
            carried = () if piece is None else (piece,)
            for half_at in (1, 0):
                out = chain_call(
                    stage, m, (half_at,), padding, g[m][half_at], skip, *ready[m], w_full, carried, held[m]
                )
                held[m], carried = out[:3], out[-1:]
                piece = out[3] if stage else out[1]
                if stage:
                    g[m][half_at] = lax.ppermute(piece, "pipe", [(stage, stage - 1)])
    pre_grads, cots, gs = zip(*held)
    cot = jnp.stack(cots, axis=0)

    def terms(dist, tokens, kind=BF16):
        offsets = (dist,) if dist in (0, half) else (dist, -dist)
        return term_call(replicas, offsets, kind, taps_t, skip, hid_t, pre_grads, gs, tokens)

    low, high = terms(half, ())
    got_one = send(low, high)
    mine = terms(half - 1, (low,))
    got_two = send(mine[1], mine[2])
    token = ()
    for dist in range(half - 1, 0, -1):
        if dist < half - 1:
            out = add_call((mine[1], mine[2]), got_two, token)
            token = out[:1]
            got_two = send(*out)
        out = add_call((mine[0], mine[3]), got_one, token)
        token = out[:1]
        got_one = send(*out)
        if dist > 1:
            mine = terms(dist - 1, token)
    low, high = terms(0, token, F32)
    share_conv, share_mix = final_call(low, high, got_one[0], got_two[1], got_two[0], got_one[1])
    return (
        cot.reshape(1, micro, seqs, samples, channels),
        share_conv.transpose(1, 0, 2)[None],
        share_mix[None],
    )


def solution(mesh):
    placed = (
        P("pipe", None, "dp", None, None),
        P(None, "dp", None, None),
        P(None, "dp", None, None),
        P("pipe", "dp", None, None),
        P("pipe", "dp", None),
    )
    return jax.shard_map(
        local,
        mesh=mesh,
        in_specs=placed,
        out_specs=(
            P("pipe", None, "dp", None, None),
            P("pipe", "dp", None, None),
            P("pipe", "dp", None),
        ),
        check_vma=False,
    )
```

```python
import functools

import jax
import jax.numpy as jnp
from jax import lax
from jax.experimental import pallas as pl
from jax.experimental.pallas import tpu as pltpu
from jax.sharding import PartitionSpec as P

F32 = jnp.float32
BF16 = jnp.bfloat16
NT = (((1,), (1,)), ((), ()))
TN = (((0,), (0,)), ((), ()))
VMEM = pl.BlockSpec(memory_space=pltpu.VMEM)
PARAMS = pltpu.CompilerParams(vmem_limit_bytes=24 * 2**20)


def ring_pairs(count):
    order = list(range(0, count, 2)) + list(range(count - 1 - count % 2, 0, -2))
    right = [(order[i], order[(i + 1) % count]) for i in range(count)]
    return right, [(b, a) for a, b in right]


def in_vmem(*arrays):
    return [pltpu.with_memory_space_constraint(array, pltpu.VMEM) for array in arrays]


def cost(flops, moved):
    return pl.CostEstimate(flops=flops, bytes_accessed=moved, transcendentals=0)


def owner_row(replicas, part, offset):
    replica = lax.axis_index("dp")
    step = replica // 2
    place = jnp.where(lax.rem(replica, 2) == 0, step, replicas - 1 - step)
    at = lax.rem(place + (offset + replicas), replicas)
    owner = jnp.where(at < replicas // 2, 2 * at, 2 * (replicas - 1 - at) + 1)
    return pl.multiple_of(owner * part, part)


def split_kernel(conv, mix, _taps, low, high, sems):
    copies = [
        pltpu.make_async_copy(conv.at[0:2], low, sems.at[0]),
        pltpu.make_async_copy(conv.at[2], high.at[0], sems.at[1]),
        pltpu.make_async_copy(mix.at[0], high.at[1], sems.at[2]),
    ]
    for copy in copies:
        copy.start()
    for copy in copies:
        copy.wait()


def split_call(conv, mix, taps_t):
    anywhere = pl.BlockSpec(memory_space=pl.ANY)
    return pl.pallas_call(
        split_kernel,
        out_shape=[pltpu.VMEM((2, *conv.shape[1:]), BF16)] * 2,
        in_specs=[anywhere] * 2 + [VMEM],
        out_specs=[VMEM] * 2,
        scratch_shapes=[pltpu.SemaphoreType.DMA((3,))],
        compiler_params=PARAMS,
        cost_estimate=cost(0, 2**20),
    )(*[pltpu.with_memory_space_constraint(array, pltpu.HBM) for array in (conv, mix)], *in_vmem(taps_t))


def prepare_kernel(parity, x_hbm, *refs):
    taps_t, x, sem = refs[-3:]
    seqs, samples, channels = x.shape
    section = lax.axis_index("pipe")
    wide = 128

    @pl.when(lax.rem(section, 2) == parity)
    def _():
        copy = pltpu.make_async_copy(x_hbm, x, sem)
        copy.start()
        copy.wait()
        dilation = jnp.left_shift(jnp.int32(1), section)
        for s in range(seqs):
            columns = slice(s * samples, (s + 1) * samples)

            @pl.loop(0, channels // wide)
            def _(j):
                at = pl.multiple_of(j * wide, wide)
                turned = x[s, :, pl.ds(at, wide)].astype(F32).T
                position = lax.broadcasted_iota(jnp.int32, turned.shape, 1)
                taps_t[pl.ds(at, wide), columns] = turned.astype(BF16)
                for k in (1, 2):
                    delayed = jnp.where(position >= k * dilation, pltpu.roll(turned, k * dilation, 1), 0.0)
                    taps_t[pl.ds(k * channels + at, wide), columns] = delayed.astype(BF16)


def prepare_call(parity, x, held):
    seqs, samples, channels = x.shape
    return pl.pallas_call(
        functools.partial(prepare_kernel, parity),
        out_shape=pltpu.VMEM((3 * channels, seqs * samples), BF16),
        in_specs=[pl.BlockSpec(memory_space=pl.ANY)] + [VMEM] * len(held),
        out_specs=VMEM,
        scratch_shapes=[pltpu.VMEM(x.shape, BF16), pltpu.SemaphoreType.DMA],
        input_output_aliases={1: 0} if held else {},
        compiler_params=PARAMS,
        cost_estimate=cost(2**20, 2**22),
    )(pltpu.with_memory_space_constraint(x, pltpu.HBM), *in_vmem(*held))


def tap_rows(taps_t, row, part, columns):
    channels = taps_t.shape[0] // 3
    return jnp.concatenate([taps_t[pl.ds(k * channels + row, part), columns] for k in range(3)], axis=0)


def place_rows(replicas, items, blocks):
    part = blocks[0].shape[1]
    return [(owner_row(replicas, part, offset), first, block) for (offset, first), block in zip(items, blocks)]


def shard_term(taps_t, columns, placed):
    channels = taps_t.shape[0] // 3
    part, wide = placed[0][2].shape[1:]
    rows, weights = [], []
    for row, first, block in placed:
        count = min(block.shape[0], 3 - first)
        if count == 0:
            continue
        rows += [taps_t[pl.ds((first + k) * channels + row, part), columns] for k in range(count)]
        weights.append(block[:count].reshape(count * part, wide))
    return lax.dot_general(
        jnp.concatenate(rows, axis=0), jnp.concatenate(weights, axis=0), TN, preferred_element_type=F32
    )


def store_shards(w, placed):
    channels = w.shape[0] // 4
    for row, first, block in placed:
        for k in range(block.shape[0]):
            w[pl.ds((first + k) * channels + row, block.shape[1]), :] = block[k]


def partial_kernel(replicas, items, first, quarters, tokens, taps_t, *refs):
    count = len(items)
    blocks = refs[:count]
    placed = place_rows(replicas, items, blocks)
    refs = refs[count:]
    acc, w, *passed = refs if first else refs[2 + tokens :]
    rows = taps_t.shape[1]
    chunk = min(256, rows)
    for at in range(0, rows, chunk):
        columns = slice(at, at + chunk)
        term = shard_term(taps_t, columns, placed)
        acc[columns, :] = term if first else refs[0][columns, :] + term
    store_shards(w, placed)
    if quarters:
        passed[0][...] = blocks[0][0:1]
        passed[1][...] = blocks[1][1:2]


def partial_call(replicas, items, taps_t, blocks, held, passing=None, tokens=()):
    part, wide = blocks[0].shape[1:]
    rows = taps_t.shape[1]
    count = len(items)
    inputs = in_vmem(taps_t, *blocks, *held, *tokens)
    aliases = {1 + count + i: i for i in range(len(held))}
    if passing == "whole":
        aliases |= {1 + i: 2 + i for i in range(count)}
    return pl.pallas_call(
        functools.partial(partial_kernel, replicas, items, not held, passing == "quarters", len(tokens)),
        out_shape=[pltpu.VMEM((rows, wide), F32), pltpu.VMEM((2 * wide, wide), BF16)]
        + [pltpu.VMEM((2 if passing == "whole" else 1, part, wide), BF16) for _ in blocks if passing],
        in_specs=[VMEM] * len(inputs),
        out_specs=[VMEM] * (2 + count if passing else 2),
        input_output_aliases=aliases,
        compiler_params=PARAMS,
        cost_estimate=cost(3 * rows * part * count * wide, 2**20),
    )(*inputs)


def forward_kernel(replicas, index, store, taps_t, acc, w_in, *refs):
    blocks, refs = refs[:2], refs[2:]
    a1, a2, hid_t = refs[:3]
    samples, channels = a1.shape
    placed = place_rows(replicas, [(replicas // 2, k) for k in (2, 3)], blocks)
    chunk = min(256, samples)
    for at in range(0, samples, chunk):
        columns = slice(index * samples + at, index * samples + at + chunk)
        pre = acc[columns, :] + shard_term(taps_t, columns, placed)
        filt = jnp.tanh(pre[:, :channels])
        gate = jax.nn.sigmoid(pre[:, channels:])
        a1[at : at + chunk, :] = (gate * (1.0 - filt * filt)).astype(BF16)
        a2[at : at + chunk, :] = (filt * gate * (1.0 - gate)).astype(BF16)
        hid_t[:, at : at + chunk] = (filt * gate).T.astype(BF16)
    if store:
        store_shards(refs[3], placed)


def forward_call(replicas, index, micro, store, taps_t, acc, w, blocks):
    rows, wide = acc.shape
    channels = wide // 2
    samples = rows // micro
    inputs = in_vmem(taps_t, acc, w, *blocks)
    return pl.pallas_call(
        functools.partial(forward_kernel, replicas, index, store),
        out_shape=[pltpu.VMEM((samples, channels), BF16)] * 2
        + [pltpu.VMEM((channels, samples), BF16)]
        + ([pltpu.VMEM(w.shape, BF16)] if store else []),
        in_specs=[VMEM] * len(inputs),
        out_specs=[VMEM] * (4 if store else 3),
        input_output_aliases={2: 3} if store else {},
        compiler_params=PARAMS,
        cost_estimate=cost(2**28, 2**22),
    )(*inputs)


def chain_kernel(stage, index, halves, padding, before, held, g, skip, a1, a2, w, *refs):
    bt = refs[-1]
    carried = refs[0] if halves == (0,) else None
    pg, ig, gk, *extra = refs[before + held : -1]
    samples, channels = gk.shape
    chunk = samples // 2
    base = min(halves) * chunk
    count = len(halves) * chunk
    dilation = 2**stage
    g_base = base if g.shape[0] == samples else 0

    @pl.when(lax.axis_index("pipe") == stage)
    def _():
        for k in (1, 2):
            bt[k, count:, :] = jnp.zeros((padding, channels), F32) if carried is None else carried[k - 1]
        for half in halves:
            at = half * chunk
            rows = slice(at, at + chunk)
            here = slice(at - base, at - base + chunk)
            g_rows = slice(at - base + g_base, at - base + g_base + chunk)
            hid = lax.dot_general(
                g[g_rows, :], w[3 * channels :, :channels], NT, preferred_element_type=F32
            ) + lax.dot_general(
                skip[index, rows, :], w[3 * channels :, channels:], NT, preferred_element_type=F32
            )
            pg[rows, :channels] = (hid * a1[rows, :].astype(F32)).astype(BF16)
            pg[rows, channels:] = (hid * a2[rows, :].astype(F32)).astype(BF16)
            for k in range(3):
                bt[k, here, :] = lax.dot_general(
                    pg[rows, :], w[k * channels : (k + 1) * channels, :], NT, preferred_element_type=F32
                )
            piece = 64
            for first in range(at - base + chunk - piece, at - base - 1, -piece):
                last = first + piece
                total = g[first + g_base : last + g_base, :].astype(F32) + bt[0, first:last, :]
                total = total + bt[1, first + dilation : last + dilation, :]
                total = total + bt[2, first + 2 * dilation : last + 2 * dilation, :]
                ig[first + base : last + base, :] = total.astype(BF16)
                if len(halves) == 1 and stage:
                    extra[0][first:last, :] = total.astype(BF16)
            gk[rows, :] = g[g_rows, :]
        if halves == (1,):
            for k in (1, 2):
                extra[-1][k - 1] = bt[k, :padding, :]


def chain_call(stage, index, halves, padding, g, skip, a1, a2, w, carried, held):
    samples, channels = a1.shape
    chunk = samples // 2
    tile = pltpu.VMEM((samples, channels), BF16)
    outs = [pltpu.VMEM((samples, 2 * channels), BF16), tile, tile]
    if len(halves) == 1 and stage:
        outs.append(pltpu.VMEM((chunk, channels), BF16))
    if halves == (1,):
        outs.append(pltpu.VMEM((2, padding, channels), F32))
    inputs = in_vmem(g, skip, a1, a2, w, *carried, *held)
    return pl.pallas_call(
        functools.partial(chain_kernel, stage, index, halves, padding, len(carried), len(held)),
        out_shape=outs,
        in_specs=[VMEM] * len(inputs),
        out_specs=[VMEM] * len(outs),
        scratch_shapes=[pltpu.VMEM((3, len(halves) * chunk + padding, channels), F32)],
        input_output_aliases={len(inputs) - len(held) + i: i for i in range(len(held))},
        compiler_params=PARAMS,
        cost_estimate=cost(8 * len(halves) * chunk * channels * channels, 2**22),
    )(*inputs)


def term_kernel(replicas, offsets, micro, taps_t, skip, *refs):
    hids, refs = refs[:micro], refs[micro:]
    pgs, refs = refs[:micro], refs[micro:]
    gs, refs = refs[:micro], refs[micro:]
    outs = refs[-2 * len(offsets) :]
    samples, wide = pgs[0].shape
    channels = wide // 2
    part = channels // replicas
    places = [owner_row(replicas, part, offset) for offset in offsets]
    step = min(256, channels)

    def product(rows_of, right, columns):
        total = None
        for m in range(micro):
            new = jnp.dot(rows_of(m), right(m, columns), preferred_element_type=F32)
            total = new if total is None else total + new
        return total

    def conv_rows(m):
        here = slice(m * samples, (m + 1) * samples)
        return jnp.concatenate([tap_rows(taps_t, row, part, here) for row in places], axis=0)

    def mix_rows(m):
        return jnp.concatenate([hids[m][pl.ds(row, part), :] for row in places], axis=0)

    unroll = offsets == (replicas // 2,)

    @pl.loop(0, wide // step, unroll=unroll)
    def _(j):
        columns = pl.ds(pl.multiple_of(j * step, step), step)
        conv = product(conv_rows, lambda m, at: pgs[m][:, at], columns)
        for slot in range(len(offsets)):
            low, high = outs[2 * slot : 2 * slot + 2]
            for k, (target, index) in enumerate(((low, 0), (low, 1), (high, 0))):
                at = (slot * 3 + k) * part
                target[index, :, columns] = conv[at : at + part, :].astype(low.dtype)

    @pl.loop(0, channels // step, unroll=unroll)
    def _(j):
        columns = pl.ds(pl.multiple_of(j * step, step), step)
        after = pl.ds(pl.multiple_of(channels + j * step, step), step)
        mix_g = product(mix_rows, lambda m, at: gs[m][:, at], columns)
        mix_s = product(mix_rows, lambda m, at: skip[m, :, at], columns)
        for slot in range(len(offsets)):
            high = outs[2 * slot + 1]
            here = slice(slot * part, (slot + 1) * part)
            high[1, :, columns] = mix_g[here, :].astype(high.dtype)
            high[1, :, after] = mix_s[here, :].astype(high.dtype)


def term_call(replicas, offsets, kind, taps_t, skip, hid_t, pre_grads, gs, tokens):
    micro, samples, channels = skip.shape
    part = channels // replicas
    inputs = in_vmem(taps_t, skip, *hid_t, *pre_grads, *gs, *tokens)
    outs = 2 * len(offsets)
    return pl.pallas_call(
        functools.partial(term_kernel, replicas, offsets, micro),
        out_shape=[pltpu.VMEM((2, part, 2 * channels), kind)] * outs,
        in_specs=[VMEM] * len(inputs),
        out_specs=[VMEM] * outs,
        compiler_params=PARAMS,
        cost_estimate=cost(2**29 * len(offsets), 2**20),
    )(*inputs)


def add_kernel(mine_r, mine_l, got_r, got_l, *refs):
    out_r, out_l = refs[-2:]
    out_r[...] = (mine_r[...].astype(F32) + got_r[...].astype(F32)).astype(BF16)
    out_l[...] = (mine_l[...].astype(F32) + got_l[...].astype(F32)).astype(BF16)


def add_call(mine, got, tokens):
    inputs = in_vmem(*mine, *got, *tokens)
    return pl.pallas_call(
        add_kernel,
        out_shape=[pltpu.VMEM(got[0].shape, BF16)] * 2,
        in_specs=[VMEM] * len(inputs),
        out_specs=[VMEM] * 2,
        compiler_params=PARAMS,
        cost_estimate=cost(2**18, 2**19),
    )(*inputs)


def final_kernel(low, high, low_r, low_l, high_r, high_l, conv, mix):
    conv[0:2] = low[...] + (low_r[...].astype(F32) + low_l[...].astype(F32))
    total = high[...] + (high_r[...].astype(F32) + high_l[...].astype(F32))
    conv[2] = total[0]
    mix[...] = total[1]


def final_call(*blocks):
    part, wide = blocks[0].shape[1:]
    return pl.pallas_call(
        final_kernel,
        out_shape=[jax.ShapeDtypeStruct((3, part, wide), F32), jax.ShapeDtypeStruct((part, wide), F32)],
        in_specs=[VMEM] * 6,
        out_specs=[VMEM] * 2,
        compiler_params=PARAMS,
        cost_estimate=cost(2**19, 2**20),
    )(*in_vmem(*blocks))


def local(x_ckpt, top_cot, skip_cot, w_conv, w_mix):
    sections = lax.axis_size("pipe")
    replicas = lax.axis_size("dp")
    micro, seqs, samples, channels = x_ckpt.shape[1:]
    block = seqs * samples
    half = replicas // 2
    right, left = ring_pairs(replicas)

    def send(to_right, to_left):
        return lax.ppermute(to_right, "dp", right), lax.ppermute(to_left, "dp", left)

    x_rows = x_ckpt[0].reshape(micro * seqs, samples, channels)
    taps_t = prepare_call(1, x_rows, [])
    low, high = split_call(w_conv[0].transpose(1, 0, 2), w_mix, taps_t)
    taps_t = prepare_call(0, x_rows, [taps_t])
    streams = {0: (low, low), 2: (high, high)}
    held = partial_call(replicas, ((0, 0), (0, 2)), taps_t, [low, high], [])
    skip = skip_cot.reshape(micro, block, channels)
    for step in range(1, half):
        last = step == half - 1
        for first, (to_right, to_left) in streams.items():
            got = send(to_right, to_left)
            items = ((-step, first), (step, first))
            if last and first:
                blocks = send(got[0][:1], got[1][1:])
                items += ((half, 0), (half, 1))
                held = partial_call(replicas, items, taps_t, [*got, *ahead], held, None, (skip,))
                continue
            passing = "quarters" if last else "whole"
            *held, to_right, to_left = partial_call(replicas, items, taps_t, got, held, passing)
            streams[first] = (to_right, to_left)
            if last:
                ahead = send(to_right, to_left)
    acc, w_full = held

    g = list(top_cot.reshape(micro, block, channels))
    padding = max(16, 2 * 2 ** (sections - 1))
    hid_t, held, ready = [], [()] * micro, []
    for m in range(micro):
        a1, a2, hid, *stored = forward_call(
            replicas, m, micro, m == 0, taps_t, acc, w_full, blocks
        )
        if stored:
            w_full = stored[0]
        hid_t.append(hid)
        ready.append((a1, a2))
    last = sections - 1
    g = [[piece, piece] for piece in g]
    for m in range(micro):
        held[m] = chain_call(last, m, (1, 0), padding, g[m][0], skip, *ready[m], w_full, (), ())
        g[m] = [lax.ppermute(held[m][1], "pipe", [(last, last - 1)])] * 2
    for stage in range(last - 1, -1, -1):
        piece = None
        for m in range(micro):
            carried = () if piece is None else (piece,)
            for half_at in (1, 0):
                out = chain_call(
                    stage, m, (half_at,), padding, g[m][half_at], skip, *ready[m], w_full, carried, held[m]
                )
                held[m], carried = out[:3], out[-1:]
                piece = out[3] if stage else out[1]
                if stage:
                    g[m][half_at] = lax.ppermute(piece, "pipe", [(stage, stage - 1)])
    pre_grads, cots, gs = zip(*held)
    cot = jnp.stack(cots, axis=0)

    def terms(dist, tokens, kind=BF16):
        offsets = (dist,) if dist in (0, half) else (dist, -dist)
        return term_call(replicas, offsets, kind, taps_t, skip, hid_t, pre_grads, gs, tokens)

    low, high = terms(half, ())
    got_one = send(low, high)
    mine = terms(half - 1, (low,))
    got_two = send(mine[1], mine[2])
    token = ()
    for dist in range(half - 1, 0, -1):
        if dist < half - 1:
            out = add_call((mine[1], mine[2]), got_two, token)
            token = out[:1]
            got_two = send(*out)
        out = add_call((mine[0], mine[3]), got_one, token)
        token = out[:1]
        got_one = send(*out)
        if dist > 1:
            mine = terms(dist - 1, token)
    low, high = terms(0, token, F32)
    share_conv, share_mix = final_call(low, high, got_one[0], got_two[1], got_two[0], got_one[1])
    return (
        cot.reshape(1, micro, seqs, samples, channels),
        share_conv.transpose(1, 0, 2)[None],
        share_mix[None],
    )


def solution(mesh):
    placed = (
        P("pipe", None, "dp", None, None),
        P(None, "dp", None, None),
        P(None, "dp", None, None),
        P("pipe", "dp", None, None),
        P("pipe", "dp", None),
    )
    return jax.shard_map(
        local,
        mesh=mesh,
        in_specs=placed,
        out_specs=(
            P("pipe", None, "dp", None, None),
            P("pipe", "dp", None, None),
            P("pipe", "dp", None),
        ),
        check_vma=False,
    )
```

```python
import functools

import jax
import jax.numpy as jnp
from jax import lax
from jax.experimental import pallas as pl
from jax.experimental.pallas import tpu as pltpu
from jax.sharding import PartitionSpec as P

F32 = jnp.float32
BF16 = jnp.bfloat16
NT = (((1,), (1,)), ((), ()))
TN = (((0,), (0,)), ((), ()))
VMEM = pl.BlockSpec(memory_space=pltpu.VMEM)
PARAMS = pltpu.CompilerParams(vmem_limit_bytes=24 * 2**20)


def ring_pairs(count):
    order = list(range(0, count, 2)) + list(range(count - 1 - count % 2, 0, -2))
    right = [(order[i], order[(i + 1) % count]) for i in range(count)]
    return right, [(b, a) for a, b in right]


def in_vmem(*arrays):
    return [pltpu.with_memory_space_constraint(array, pltpu.VMEM) for array in arrays]


def cost(flops, moved):
    return pl.CostEstimate(flops=flops, bytes_accessed=moved, transcendentals=0)


def owner_row(replicas, part, offset):
    replica = lax.axis_index("dp")
    step = replica // 2
    place = jnp.where(lax.rem(replica, 2) == 0, step, replicas - 1 - step)
    at = lax.rem(place + (offset + replicas), replicas)
    owner = jnp.where(at < replicas // 2, 2 * at, 2 * (replicas - 1 - at) + 1)
    return pl.multiple_of(owner * part, part)


def split_kernel(conv, mix, low, high, sems):
    copies = [
        pltpu.make_async_copy(conv.at[0:2], low, sems.at[0]),
        pltpu.make_async_copy(conv.at[2], high.at[0], sems.at[1]),
        pltpu.make_async_copy(mix.at[0], high.at[1], sems.at[2]),
    ]
    for copy in copies:
        copy.start()
    for copy in copies:
        copy.wait()


def split_call(conv, mix):
    anywhere = pl.BlockSpec(memory_space=pl.ANY)
    return pl.pallas_call(
        split_kernel,
        out_shape=[pltpu.VMEM((2, *conv.shape[1:]), BF16)] * 2,
        in_specs=[anywhere] * 2,
        out_specs=[VMEM] * 2,
        scratch_shapes=[pltpu.SemaphoreType.DMA((3,))],
        compiler_params=PARAMS,
        cost_estimate=cost(0, 2**20),
    )(*[pltpu.with_memory_space_constraint(array, pltpu.HBM) for array in (conv, mix)])


def prepare_kernel(x, taps_t):
    seqs, samples, channels = x.shape
    dilation = jnp.left_shift(jnp.int32(1), lax.axis_index("pipe"))
    wide = 128
    for s in range(seqs):
        columns = slice(s * samples, (s + 1) * samples)
        for at in range(0, channels, wide):
            turned = x[s, :, at : at + wide].astype(F32).T
            position = lax.broadcasted_iota(jnp.int32, turned.shape, 1)
            taps_t[at : at + wide, columns] = turned.astype(BF16)
            for k in (1, 2):
                delayed = jnp.where(position >= k * dilation, pltpu.roll(turned, k * dilation, 1), 0.0)
                taps_t[k * channels + at : k * channels + at + wide, columns] = delayed.astype(BF16)


def prepare_call(x):
    seqs, samples, channels = x.shape
    return pl.pallas_call(
        prepare_kernel,
        out_shape=pltpu.VMEM((3 * channels, seqs * samples), BF16),
        in_specs=[VMEM],
        out_specs=VMEM,
        compiler_params=PARAMS,
        cost_estimate=cost(2**20, 2**22),
    )(x)


def tap_rows(taps_t, row, part, columns):
    channels = taps_t.shape[0] // 3
    return jnp.concatenate([taps_t[pl.ds(k * channels + row, part), columns] for k in range(3)], axis=0)


def place_rows(replicas, items, blocks):
    part = blocks[0].shape[1]
    return [(owner_row(replicas, part, offset), first, block) for (offset, first), block in zip(items, blocks)]


def shard_term(taps_t, columns, placed):
    channels = taps_t.shape[0] // 3
    part, wide = placed[0][2].shape[1:]
    rows, weights = [], []
    for row, first, block in placed:
        count = min(block.shape[0], 3 - first)
        if count == 0:
            continue
        rows += [taps_t[pl.ds((first + k) * channels + row, part), columns] for k in range(count)]
        weights.append(block[:count].reshape(count * part, wide))
    return lax.dot_general(
        jnp.concatenate(rows, axis=0), jnp.concatenate(weights, axis=0), TN, preferred_element_type=F32
    )


def store_shards(w, placed):
    channels = w.shape[0] // 4
    for row, first, block in placed:
        for k in range(block.shape[0]):
            w[pl.ds((first + k) * channels + row, block.shape[1]), :] = block[k]


def partial_kernel(replicas, items, first, quarters, tokens, taps_t, *refs):
    count = len(items)
    blocks = refs[:count]
    placed = place_rows(replicas, items, blocks)
    refs = refs[count:]
    acc, w, *passed = refs if first else refs[2 + tokens :]
    rows = taps_t.shape[1]
    chunk = min(256, rows)
    for at in range(0, rows, chunk):
        columns = slice(at, at + chunk)
        term = shard_term(taps_t, columns, placed)
        acc[columns, :] = term if first else refs[0][columns, :] + term
    store_shards(w, placed)
    if quarters:
        passed[0][...] = blocks[0][0:1]
        passed[1][...] = blocks[1][1:2]


def partial_call(replicas, items, taps_t, blocks, held, passing=None, tokens=()):
    part, wide = blocks[0].shape[1:]
    rows = taps_t.shape[1]
    count = len(items)
    inputs = in_vmem(taps_t, *blocks, *held, *tokens)
    aliases = {1 + count + i: i for i in range(len(held))}
    if passing == "whole":
        aliases |= {1 + i: 2 + i for i in range(count)}
    return pl.pallas_call(
        functools.partial(partial_kernel, replicas, items, not held, passing == "quarters", len(tokens)),
        out_shape=[pltpu.VMEM((rows, wide), F32), pltpu.VMEM((2 * wide, wide), BF16)]
        + [pltpu.VMEM((2 if passing == "whole" else 1, part, wide), BF16) for _ in blocks if passing],
        in_specs=[VMEM] * len(inputs),
        out_specs=[VMEM] * (2 + count if passing else 2),
        input_output_aliases=aliases,
        compiler_params=PARAMS,
        cost_estimate=cost(3 * rows * part * count * wide, 2**20),
    )(*inputs)


def forward_kernel(replicas, index, store, taps_t, acc, w_in, *refs):
    blocks, refs = refs[:2], refs[2:]
    a1, a2, hid_t = refs[:3]
    samples, channels = a1.shape
    placed = place_rows(replicas, [(replicas // 2, k) for k in (2, 3)], blocks)
    chunk = min(256, samples)
    for at in range(0, samples, chunk):
        columns = slice(index * samples + at, index * samples + at + chunk)
        pre = acc[columns, :] + shard_term(taps_t, columns, placed)
        filt = jnp.tanh(pre[:, :channels])
        gate = jax.nn.sigmoid(pre[:, channels:])
        a1[at : at + chunk, :] = (gate * (1.0 - filt * filt)).astype(BF16)
        a2[at : at + chunk, :] = (filt * gate * (1.0 - gate)).astype(BF16)
        hid_t[:, at : at + chunk] = (filt * gate).T.astype(BF16)
    if store:
        store_shards(refs[3], placed)


def forward_call(replicas, index, micro, store, taps_t, acc, w, blocks):
    rows, wide = acc.shape
    channels = wide // 2
    samples = rows // micro
    inputs = in_vmem(taps_t, acc, w, *blocks)
    return pl.pallas_call(
        functools.partial(forward_kernel, replicas, index, store),
        out_shape=[pltpu.VMEM((samples, channels), BF16)] * 2
        + [pltpu.VMEM((channels, samples), BF16)]
        + ([pltpu.VMEM(w.shape, BF16)] if store else []),
        in_specs=[VMEM] * len(inputs),
        out_specs=[VMEM] * (4 if store else 3),
        input_output_aliases={2: 3} if store else {},
        compiler_params=PARAMS,
        cost_estimate=cost(2**28, 2**22),
    )(*inputs)


def chain_kernel(stage, index, halves, padding, before, held, g, skip, a1, a2, w, *refs):
    bt = refs[-1]
    carried = refs[0] if halves == (0,) else None
    pg, ig, gk, *extra = refs[before + held : -1]
    samples, channels = gk.shape
    chunk = samples // 2
    base = min(halves) * chunk
    count = len(halves) * chunk
    dilation = 2**stage
    g_base = base if g.shape[0] == samples else 0

    @pl.when(lax.axis_index("pipe") == stage)
    def _():
        for k in (1, 2):
            bt[k, count:, :] = jnp.zeros((padding, channels), F32) if carried is None else carried[k - 1]
        for half in halves:
            at = half * chunk
            rows = slice(at, at + chunk)
            here = slice(at - base, at - base + chunk)
            g_rows = slice(at - base + g_base, at - base + g_base + chunk)
            hid = lax.dot_general(
                g[g_rows, :], w[3 * channels :, :channels], NT, preferred_element_type=F32
            ) + lax.dot_general(
                skip[index, rows, :], w[3 * channels :, channels:], NT, preferred_element_type=F32
            )
            pg[rows, :channels] = (hid * a1[rows, :].astype(F32)).astype(BF16)
            pg[rows, channels:] = (hid * a2[rows, :].astype(F32)).astype(BF16)
            for k in range(3):
                bt[k, here, :] = lax.dot_general(
                    pg[rows, :], w[k * channels : (k + 1) * channels, :], NT, preferred_element_type=F32
                )
            piece = 64
            for first in range(at - base + chunk - piece, at - base - 1, -piece):
                last = first + piece
                total = g[first + g_base : last + g_base, :].astype(F32) + bt[0, first:last, :]
                total = total + bt[1, first + dilation : last + dilation, :]
                total = total + bt[2, first + 2 * dilation : last + 2 * dilation, :]
                ig[first + base : last + base, :] = total.astype(BF16)
                if len(halves) == 1 and stage:
                    extra[0][first:last, :] = total.astype(BF16)
            gk[rows, :] = g[g_rows, :]
        if halves == (1,):
            for k in (1, 2):
                extra[-1][k - 1] = bt[k, :padding, :]


def chain_call(stage, index, halves, padding, g, skip, a1, a2, w, carried, held):
    samples, channels = a1.shape
    chunk = samples // 2
    tile = pltpu.VMEM((samples, channels), BF16)
    outs = [pltpu.VMEM((samples, 2 * channels), BF16), tile, tile]
    if len(halves) == 1 and stage:
        outs.append(pltpu.VMEM((chunk, channels), BF16))
    if halves == (1,):
        outs.append(pltpu.VMEM((2, padding, channels), F32))
    inputs = in_vmem(g, skip, a1, a2, w, *carried, *held)
    return pl.pallas_call(
        functools.partial(chain_kernel, stage, index, halves, padding, len(carried), len(held)),
        out_shape=outs,
        in_specs=[VMEM] * len(inputs),
        out_specs=[VMEM] * len(outs),
        scratch_shapes=[pltpu.VMEM((3, len(halves) * chunk + padding, channels), F32)],
        input_output_aliases={len(inputs) - len(held) + i: i for i in range(len(held))},
        compiler_params=PARAMS,
        cost_estimate=cost(8 * len(halves) * chunk * channels * channels, 2**22),
    )(*inputs)


def term_kernel(replicas, offsets, micro, taps_t, skip, *refs):
    hids, refs = refs[:micro], refs[micro:]
    pgs, refs = refs[:micro], refs[micro:]
    gs, refs = refs[:micro], refs[micro:]
    outs = refs[-2 * len(offsets) :]
    samples, wide = pgs[0].shape
    channels = wide // 2
    part = channels // replicas
    places = [owner_row(replicas, part, offset) for offset in offsets]
    step = min(256, channels)

    def product(rows_of, right, columns):
        total = None
        for m in range(micro):
            new = jnp.dot(rows_of(m), right(m, columns), preferred_element_type=F32)
            total = new if total is None else total + new
        return total

    def conv_rows(m):
        here = slice(m * samples, (m + 1) * samples)
        return jnp.concatenate([tap_rows(taps_t, row, part, here) for row in places], axis=0)

    def mix_rows(m):
        return jnp.concatenate([hids[m][pl.ds(row, part), :] for row in places], axis=0)

    unroll = offsets == (replicas // 2,)

    @pl.loop(0, wide // step, unroll=unroll)
    def _(j):
        columns = pl.ds(pl.multiple_of(j * step, step), step)
        conv = product(conv_rows, lambda m, at: pgs[m][:, at], columns)
        for slot in range(len(offsets)):
            low, high = outs[2 * slot : 2 * slot + 2]
            for k, (target, index) in enumerate(((low, 0), (low, 1), (high, 0))):
                at = (slot * 3 + k) * part
                target[index, :, columns] = conv[at : at + part, :].astype(low.dtype)

    @pl.loop(0, channels // step, unroll=unroll)
    def _(j):
        columns = pl.ds(pl.multiple_of(j * step, step), step)
        after = pl.ds(pl.multiple_of(channels + j * step, step), step)
        mix_g = product(mix_rows, lambda m, at: gs[m][:, at], columns)
        mix_s = product(mix_rows, lambda m, at: skip[m, :, at], columns)
        for slot in range(len(offsets)):
            high = outs[2 * slot + 1]
            here = slice(slot * part, (slot + 1) * part)
            high[1, :, columns] = mix_g[here, :].astype(high.dtype)
            high[1, :, after] = mix_s[here, :].astype(high.dtype)


def term_call(replicas, offsets, kind, taps_t, skip, hid_t, pre_grads, gs, tokens):
    micro, samples, channels = skip.shape
    part = channels // replicas
    inputs = in_vmem(taps_t, skip, *hid_t, *pre_grads, *gs, *tokens)
    outs = 2 * len(offsets)
    return pl.pallas_call(
        functools.partial(term_kernel, replicas, offsets, micro),
        out_shape=[pltpu.VMEM((2, part, 2 * channels), kind)] * outs,
        in_specs=[VMEM] * len(inputs),
        out_specs=[VMEM] * outs,
        compiler_params=PARAMS,
        cost_estimate=cost(2**29 * len(offsets), 2**20),
    )(*inputs)


def add_kernel(mine_r, mine_l, got_r, got_l, *refs):
    out_r, out_l = refs[-2:]
    out_r[...] = (mine_r[...].astype(F32) + got_r[...].astype(F32)).astype(BF16)
    out_l[...] = (mine_l[...].astype(F32) + got_l[...].astype(F32)).astype(BF16)


def add_call(mine, got, tokens):
    inputs = in_vmem(*mine, *got, *tokens)
    return pl.pallas_call(
        add_kernel,
        out_shape=[pltpu.VMEM(got[0].shape, BF16)] * 2,
        in_specs=[VMEM] * len(inputs),
        out_specs=[VMEM] * 2,
        compiler_params=PARAMS,
        cost_estimate=cost(2**18, 2**19),
    )(*inputs)


def final_low_kernel(mine, right, left, conv, total, sem):
    total[...] = mine[...] + (right[...].astype(F32) + left[...].astype(F32))
    copy = pltpu.make_async_copy(total, conv.at[0:2], sem)
    copy.start()
    copy.wait()


def final_high_kernel(mine, right, left, _conv, conv, mix, total, sems):
    total[...] = mine[...] + (right[...].astype(F32) + left[...].astype(F32))
    copies = [
        pltpu.make_async_copy(total.at[0], conv.at[2], sems.at[0]),
        pltpu.make_async_copy(total.at[1], mix, sems.at[1]),
    ]
    for copy in copies:
        copy.start()
    for copy in copies:
        copy.wait()


def final_call(low, high, low_r, low_l, high_r, high_l):
    part, wide = low.shape[1:]
    anywhere = pl.BlockSpec(memory_space=pl.ANY)
    conv_shape = jax.ShapeDtypeStruct((3, part, wide), F32)
    estimate = cost(2**18, 2**19)
    conv = pl.pallas_call(
        final_low_kernel,
        out_shape=conv_shape,
        in_specs=[VMEM] * 3,
        out_specs=anywhere,
        scratch_shapes=[pltpu.VMEM(low.shape, F32), pltpu.SemaphoreType.DMA],
        compiler_params=PARAMS,
        cost_estimate=estimate,
    )(*in_vmem(low, low_r, low_l))
    return pl.pallas_call(
        final_high_kernel,
        out_shape=[conv_shape, jax.ShapeDtypeStruct((part, wide), F32)],
        in_specs=[VMEM] * 3 + [anywhere],
        out_specs=[anywhere] * 2,
        scratch_shapes=[pltpu.VMEM(high.shape, F32), pltpu.SemaphoreType.DMA((2,))],
        input_output_aliases={3: 0},
        compiler_params=PARAMS,
        cost_estimate=estimate,
    )(*in_vmem(high, high_r, high_l), conv)


def local(x_ckpt, top_cot, skip_cot, w_conv, w_mix):
    sections = lax.axis_size("pipe")
    replicas = lax.axis_size("dp")
    micro, seqs, samples, channels = x_ckpt.shape[1:]
    block = seqs * samples
    half = replicas // 2
    right, left = ring_pairs(replicas)

    def send(to_right, to_left):
        return lax.ppermute(to_right, "dp", right), lax.ppermute(to_left, "dp", left)

    taps_t = prepare_call(x_ckpt[0].reshape(micro * seqs, samples, channels))
    low, high = split_call(w_conv[0].transpose(1, 0, 2), w_mix)
    streams = {0: (low, low), 2: (high, high)}
    held = partial_call(replicas, ((0, 0), (0, 2)), taps_t, [low, high], [])
    skip = skip_cot.reshape(micro, block, channels)
    for step in range(1, half):
        last = step == half - 1
        for first, (to_right, to_left) in streams.items():
            got = send(to_right, to_left)
            items = ((-step, first), (step, first))
            if last and first:
                blocks = send(got[0][:1], got[1][1:])
                items += ((half, 0), (half, 1))
                held = partial_call(replicas, items, taps_t, [*got, *ahead], held, None, (skip,))
                continue
            passing = "quarters" if last else "whole"
            *held, to_right, to_left = partial_call(replicas, items, taps_t, got, held, passing)
            streams[first] = (to_right, to_left)
            if last:
                ahead = send(to_right, to_left)
    acc, w_full = held

    g = list(top_cot.reshape(micro, block, channels))
    padding = max(16, 2 * 2 ** (sections - 1))
    hid_t, held, ready = [], [()] * micro, []
    for m in range(micro):
        a1, a2, hid, *stored = forward_call(
            replicas, m, micro, m == 0, taps_t, acc, w_full, blocks
        )
        if stored:
            w_full = stored[0]
        hid_t.append(hid)
        ready.append((a1, a2))
    last = sections - 1
    g = [[piece, piece] for piece in g]
    for m in range(micro):
        held[m] = chain_call(last, m, (1, 0), padding, g[m][0], skip, *ready[m], w_full, (), ())
        g[m] = [lax.ppermute(held[m][1], "pipe", [(last, last - 1)])] * 2
    for stage in range(last - 1, -1, -1):
        piece = None
        for m in range(micro):
            carried = () if piece is None else (piece,)
            for half_at in (1, 0):
                out = chain_call(
                    stage, m, (half_at,), padding, g[m][half_at], skip, *ready[m], w_full, carried, held[m]
                )
                held[m], carried = out[:3], out[-1:]
                piece = out[3] if stage else out[1]
                if stage:
                    g[m][half_at] = lax.ppermute(piece, "pipe", [(stage, stage - 1)])
    pre_grads, cots, gs = zip(*held)
    cot = jnp.stack(cots, axis=0)

    def terms(dist, tokens, kind=BF16):
        offsets = (dist,) if dist in (0, half) else (dist, -dist)
        return term_call(replicas, offsets, kind, taps_t, skip, hid_t, pre_grads, gs, tokens)

    low, high = terms(half, ())
    got_one = send(low, high)
    mine = terms(half - 1, (low,))
    got_two = send(mine[1], mine[2])
    token = ()
    for dist in range(half - 1, 0, -1):
        if dist < half - 1:
            out = add_call((mine[1], mine[2]), got_two, token)
            token = out[:1]
            got_two = send(*out)
        out = add_call((mine[0], mine[3]), got_one, token)
        token = out[:1]
        got_one = send(*out)
        if dist > 1:
            mine = terms(dist - 1, token)
    low, high = terms(0, token, F32)
    share_conv, share_mix = final_call(low, high, got_one[0], got_two[1], got_two[0], got_one[1])
    return (
        cot.reshape(1, micro, seqs, samples, channels),
        share_conv.transpose(1, 0, 2)[None],
        share_mix[None],
    )


def solution(mesh):
    placed = (
        P("pipe", None, "dp", None, None),
        P(None, "dp", None, None),
        P(None, "dp", None, None),
        P("pipe", "dp", None, None),
        P("pipe", "dp", None),
    )
    return jax.shard_map(
        local,
        mesh=mesh,
        in_specs=placed,
        out_specs=(
            P("pipe", None, "dp", None, None),
            P("pipe", "dp", None, None),
            P("pipe", "dp", None),
        ),
        check_vma=False,
    )
```
